32 devices in a mesh: sec: 4 (over x, core), tile: 8 (over z, y).
Axes of the slice: x: 2, y: 2, z: 4, core: 2. Of those that a mesh axis runs over, the one named last changes fastest.
Arguments:
- atmos: float32 [64, 256, 256], P('sec', 'tile'), may hold values from -6 to 6
- cloudy: int32 [64, 256], P('sec', 'tile'), may hold values from 0 to 1, as said below
- weight_in: bfloat16 [256, 1024], replicated, may hold values from -0.375 to 0.375
- weight_out: bfloat16 [1024, 256], replicated, may hold values from -0.1875 to 0.1875
- cloud_in: bfloat16 [256, 1024], replicated, may hold values from -0.375 to 0.375
- cloud_out: bfloat16 [1024, 256], replicated, may hold values from -0.1875 to 0.1875
- ocean: float32 [32, 128, 128], P('sec', 'tile'), may hold values from -6 to 6
- tile_map: int32 [8], replicated, may hold values from 0 to 7, each once
Outputs:
- atmos_out: float32 [64, 256, 256], P('sec', 'tile')
- ocean_out: float32 [32, 128, 128], P('sec', 'tile')
- sst_back: float32 [64, 256], P('sec', 'tile')
The draws below stay inside these ranges and needn't reach their ends.
Inputs may be any that keep to these rules, and one draw needn't show every extreme that they name: Read each device's 16 x 32 block of columns row by row and cut it into 8 runs of 64 columns. In every row of devices along tile, 1 device, drawn, have all 64 columns of every run cloudy; every other device has exactly 8 cloudy columns in every run, at drawn places.
All inputs are finite; a program needn't handle non-finite values.
Results may differ from the reference program's by a relative error of at most 0.0026.
Values may be sent and summed in bfloat16 or wider, within the bound.
No kernel may reach another device: no remote copies, remote signals or barrier semaphores. Data moves between devices by JAX's collectives and lax.ppermute only.
A program may use at most 64 MiB of HBM per device.

```python
import jax
import jax.numpy as jnp
from jax import lax

LEV = 128
PHID = 1024
CW = 1024
OLEV = 64
AY = 16
AX = 32
ASTEPS = 2
OSTEPS = 4
SECS = 4
TILES = 8
NY = 64
NX = 256
OY = 32
OX = 128


def draw_cloudy(key, part):
    piece = AY * AX // TILES
    busy = TILES // 8
    sparse = max(1, piece // 8)
    rank_key, spot_key = jax.random.split(key)

    def one_row(subkey):
        return jax.random.permutation(subkey, TILES)
    ranking = jax.vmap(one_row)(jax.random.split(rank_key, SECS))
    counts = jnp.where(ranking < busy, piece, sparse)
    scores = jax.random.randint(spot_key, (SECS, TILES, TILES, piece), 0, 1 << 16) * piece + jnp.arange(piece, dtype=jnp.int32)
    places = jnp.argsort(jnp.argsort(scores, axis=-1), axis=-1)
    flags = (places < counts[:, :, None, None]).astype(jnp.int32)
    flags = flags.reshape(SECS, TILES, AY, AX).transpose(0, 2, 1, 3)
    return flags.reshape(SECS * AY, TILES * AX)


def steps_of(key, dims, cuts, least, high):
    gain, own = 1.0, jax.random.fold_in(key, 6)
    for dim, parts in cuts:
        draws = jnp.exp(jax.random.uniform(jax.random.fold_in(own, dim), (parts,), jnp.float32, least / len(cuts), high / len(cuts)))
        gain = gain * jnp.repeat(draws, dims[dim] // parts).reshape([-1 if axis == dim else 1 for axis in range(len(dims))])
    return gain


def normal_values(rng, shape, scale, bound, cuts=(), kind=jnp.bfloat16):
    array = jax.random.normal(rng, shape, jnp.float32) * scale
    if len(cuts) > 0:
        array = steps_of(rng, shape, cuts, -0.22, 0.18) * array
    return jnp.clip(array, min=-bound, max=bound).astype(kind)


def setup_inputs(seed: int = 0) -> dict:
    key_list = jax.random.split(jax.random.key(seed), 9)
    atmos = normal_values(key_list[0], (NY, NX, 2 * LEV), 1.0, 6.0, ((0, 4), (1, 8)), jnp.float32)
    cloudy = draw_cloudy(jax.random.fold_in(key_list[8], 71), 0)
    weight_in = normal_values(key_list[2], (2 * LEV, PHID), (2 * LEV) ** -0.5, 0.375)
    weight_out = normal_values(key_list[3], (PHID, 2 * LEV), PHID ** -0.5, 0.1875)
    cloud_in = normal_values(key_list[4], (2 * LEV, CW), (2 * LEV) ** -0.5, 0.375)
    cloud_out = normal_values(key_list[5], (CW, 2 * LEV), CW ** -0.5, 0.1875)
    ocean = normal_values(key_list[6], (OY, OX, 2 * OLEV), 1.0, 6.0, ((0, 4), (1, 8)), jnp.float32)
    tile_map = jax.random.permutation(key_list[7], TILES).astype(jnp.int32)
    return dict(atmos=atmos, cloudy=cloudy, weight_in=weight_in, weight_out=weight_out, cloud_in=cloud_in, cloud_out=cloud_out, ocean=ocean, tile_map=tile_map)


kappa_air = 0.2
kappa_sea = 0.2


def relax(padded, rate):
    inner = padded[1:-1, 1:-1]
    beside = padded[2:, 1:-1] + padded[:-2, 1:-1] + padded[1:-1, 2:] + padded[1:-1, :-2]
    return inner + rate * (beside - 4.0 * inner)


def spread(values):
    return jnp.repeat(jnp.repeat(values, 2, axis=0), 2, axis=1)


def coarsen(values):
    height, width = values.shape
    return values.reshape(height // 2, 2, width // 2, 2).mean(axis=(1, 3))


def reference(atmos, cloudy, weight_in, weight_out, cloud_in, cloud_out, ocean, tile_map):
    half_cols = AX // 2
    owner = jnp.zeros((TILES,), jnp.int32).at[tile_map].set(jnp.arange(TILES, dtype=jnp.int32))

    def to_air(top):
        blocks = jnp.take(top.reshape(OY, TILES, half_cols), owner, axis=1)
        return spread(blocks.reshape(OY, OX))

    def to_sea(values):
        blocks = jnp.take(values.reshape(OY, TILES, half_cols), tile_map, axis=1)
        return blocks.reshape(OY, OX)

    landing = to_air(ocean[:, :, 0])
    field = atmos
    for step in range(ASTEPS):
        field = relax(jnp.pad(field, ((1, 1), (1, 1), (0, 0))), kappa_air)

    def physics(pair):
        rows, flags = pair
        inputs = rows.astype(jnp.bfloat16)
        hidden = jax.nn.silu(jnp.dot(inputs, weight_in, preferred_element_type=jnp.float32)).astype(jnp.bfloat16)
        condensed = jax.nn.silu(jnp.dot(inputs, cloud_in, preferred_element_type=jnp.float32)).astype(jnp.bfloat16)
        tendency = jnp.dot(hidden, weight_out, preferred_element_type=jnp.float32) + flags.astype(jnp.float32)[:, None] * jnp.dot(condensed, cloud_out, preferred_element_type=jnp.float32)
        return rows + tendency.astype(jnp.bfloat16).astype(jnp.float32)

    field = lax.map(physics, (field, cloudy))
    heat = 0.8 * (landing - field[:, :, 0])
    moisture = 0.8 * (0.5 * landing - field[:, :, LEV])
    field = field.at[:, :, 0].add(0.5 * heat).at[:, :, LEV].add(0.5 * moisture)
    heat_sea = to_sea(coarsen(heat))
    moist_sea = to_sea(coarsen(moisture))
    sea = ocean.at[:, :, 0].add(0.5 * heat_sea).at[:, :, OLEV].add(0.5 * moist_sea)
    for step in range(OSTEPS):
        sea = relax(jnp.pad(sea, ((1, 1), (1, 1), (0, 0))), kappa_sea)
    returned = to_air(sea[:, :, 0])
    return (field, sea, returned)
```

```python
import functools

import jax
import jax.numpy as jnp
from jax import lax
from jax.experimental import pallas as pl
from jax.experimental.pallas import tpu as pltpu
from jax.sharding import PartitionSpec as P

ASTEPS = 2
OSTEPS = 4
LANES = 128

kappa_air = 0.2
kappa_sea = 0.2

f32 = jnp.float32
bf16 = jnp.bfloat16
HIGHEST = lax.Precision.HIGHEST
VMEM = pl.BlockSpec(memory_space=pltpu.VMEM)
SMEM = pl.BlockSpec(memory_space=pltpu.SMEM)
AXES = ("sec", "tile")


def exchanges(secs, tiles):
    def whole(partner):
        return [
            (s * tiles + t, partner(s, t)[0] * tiles + partner(s, t)[1])
            for s in range(secs)
            for t in range(tiles)
        ]

    def odd_sec(s, t):
        if s in (0, secs - 1):
            return secs - 1 - s, t
        return (s + 1 if s % 2 else s - 1), t

    def odd_tile(s, t):
        if t in (0, tiles - 1):
            return s ^ 1, t
        return s, (t + 1 if t % 2 else t - 1)

    return (
        whole(lambda s, t: (s ^ 1, t)),
        whole(odd_sec),
        whole(lambda s, t: (s, t ^ 1)),
        whole(odd_tile),
    )


def pack_sec(atmos, ocean, out_a, out_b):
    rows, cols, feat = atmos.shape
    sea_rows, sea_cols, _ = ocean.shape
    even = lax.axis_index("sec") % 2 == 0
    halves = feat // LANES
    for out, south in ((out_a, even), (out_b, jnp.logical_not(even))):
        first = jnp.where(south, rows - ASTEPS, 0)
        sea_first = jnp.where(south, sea_rows - OSTEPS, 0)
        for r in range(ASTEPS):
            line = atmos[first + r].astype(bf16)
            for h in range(halves):
                at = (r * halves + h) * cols
                out[at : at + cols, :] = line[:, h * LANES : (h + 1) * LANES]
        base = ASTEPS * halves * cols
        for r in range(OSTEPS):
            at = base + r * sea_cols
            out[at : at + sea_cols, :] = ocean[sea_first + r].astype(bf16)


def from_sec(recv_a, recv_b):
    even = lax.axis_index("sec") % 2 == 0
    a, b = recv_a[...].astype(f32), recv_b[...].astype(f32)
    return jnp.where(even, b, a), jnp.where(even, a, b)


def air_pad(rows):
    return -(-(rows + 2) * ASTEPS // 8) * 8


def pack_tile(atmos, ocean, sec_a, sec_b, out_a, out_b, stage):
    rows, cols, feat = atmos.shape
    sea_rows, sea_cols, _ = ocean.shape
    even = lax.axis_index("tile") % 2 == 0
    halves = feat // LANES
    north, south = from_sec(sec_a, sec_b)
    base = ASTEPS * halves * cols
    pad = air_pad(rows)
    for side in range(2):
        first = (cols - ASTEPS) if side else 0
        sea_first = (sea_cols - OSTEPS) if side else 0
        for h in range(halves):
            lanes = slice(h * LANES, (h + 1) * LANES)
            above = ((ASTEPS - 1) * halves + h) * cols + first
            below = h * cols + first
            stage[side, h * pad : h * pad + ASTEPS, :] = north[above : above + ASTEPS]
            for r in range(rows):
                at = h * pad + (r + 1) * ASTEPS
                stage[side, at : at + ASTEPS, :] = atmos[r, first : first + ASTEPS, lanes]
            at = h * pad + (rows + 1) * ASTEPS
            stage[side, at : at + ASTEPS, :] = south[below : below + ASTEPS]
        sea = halves * pad
        for r in range(sea_rows + 2 * OSTEPS):
            at = sea + r * OSTEPS
            if r < OSTEPS:
                row = base + r * sea_cols + sea_first
                line = north[row : row + OSTEPS]
            elif r < OSTEPS + sea_rows:
                line = ocean[r - OSTEPS, sea_first : sea_first + OSTEPS, :]
            else:
                row = base + (r - OSTEPS - sea_rows) * sea_cols + sea_first
                line = south[row : row + OSTEPS]
            stage[side, at : at + OSTEPS, :] = line
    west, east = stage[0].astype(bf16), stage[1].astype(bf16)
    out_a[...] = jnp.where(even, east, west)
    out_b[...] = jnp.where(even, west, east)


def silu(v):
    return v * (0.5 + 0.5 * jnp.tanh(0.5 * v))


def spots(tile):
    lane = lax.broadcasted_iota(jnp.int32, (8, LANES), 1)
    sub = lax.broadcasted_iota(jnp.int32, (8, LANES), 0)
    return lane, sub


def main(
    secs, tiles, atmos, cloudy, w_in, w_out, c_in, c_out, ocean, sec_a, sec_b, tile_a, tile_b,
    field, pay, sea, side_w, side_e, xs, hid, stage, sea_w, sea_e,
):
    rows, cols, feat = atmos.shape
    sea_rows, sea_cols, sea_feat = ocean.shape
    halves = feat // LANES
    s, t = lax.axis_index("sec"), lax.axis_index("tile")
    ok_n, ok_s, ok_w, ok_e = s > 0, s < secs - 1, t > 0, t < tiles - 1
    north, south = from_sec(sec_a, sec_b)
    north = jnp.where(ok_n, north, 0.0)
    south = jnp.where(ok_s, south, 0.0)
    even_t = t % 2 == 0
    ta, tb = tile_a[...].astype(f32), tile_b[...].astype(f32)
    stage[0] = jnp.where(ok_w, jnp.where(even_t, tb, ta), 0.0)
    stage[1] = jnp.where(ok_e, jnp.where(even_t, ta, tb), 0.0)
    pad = air_pad(rows)
    zero_w = jnp.zeros(side_w.shape, f32)
    side_w[...] = zero_w
    side_e[...] = zero_w
    for r in range(rows + 2):
        keep = ok_n if r == 0 else ok_s if r == rows + 1 else None
        for h in range(halves):
            lanes = slice(h * LANES, (h + 1) * LANES)
            at = h * pad + r * ASTEPS
            w, e = stage[0, at : at + ASTEPS, :], stage[1, at : at + ASTEPS, :]
            if keep is not None:
                w, e = jnp.where(keep, w, 0.0), jnp.where(keep, e, 0.0)
            side_w[r, 8 - ASTEPS : 8, lanes] = w
            side_e[r, 0:ASTEPS, lanes] = e

    def whole_row(r):
        if r < 0 or r >= rows:
            piece = north if r < 0 else south
            k = (r + ASTEPS) if r < 0 else (r - rows)
            core = jnp.concatenate(
                [piece[(k * halves + h) * cols : (k * halves + h + 1) * cols] for h in range(halves)],
                axis=1,
            )
        else:
            core = atmos[r]
        if -1 <= r <= rows:
            left, right = side_w[r + 1], side_e[r + 1]
        else:
            left = right = jnp.zeros((8, feat), f32)
        return jnp.concatenate([left, core, right], axis=0)

    wide = cols + 16
    sub = lax.broadcasted_iota(jnp.int32, (wide, feat), 0)
    inside = jnp.logical_and(
        jnp.logical_or(sub >= 8, ok_w), jnp.logical_or(sub < 8 + cols, ok_e)
    )

    def relax(up, mid, down, rate):
        n = mid.shape[-2]
        axis = mid.ndim - 2
        beside = up + down + pltpu.roll(mid, 1, axis) + pltpu.roll(mid, n - 1, axis)
        return mid + rate * (beside - 4.0 * mid)

    lines = [whole_row(-2), whole_row(-1), whole_row(0)]
    ones = []
    for r in range(-1, rows + 1):
        one = relax(lines[0], lines[1], lines[2], kappa_air)
        one = jnp.where(inside, one, 0.0)
        if r == -1:
            one = jnp.where(ok_n, one, 0.0)
        if r == rows:
            one = jnp.where(ok_s, one, 0.0)
        ones.append(one)
        if len(ones) == 3:
            two = relax(ones[0], ones[1], ones[2], kappa_air)[8 : 8 + cols]
            field[r - 1] = two
            xs[(r - 1) * cols : r * cols, :] = two.astype(bf16)
            ones = ones[1:]
        if r < rows:
            lines = lines[1:] + [whole_row(r + 2)]

    flags = cloudy[...].astype(f32)
    eye = lax.broadcasted_iota(jnp.int32, (cols, cols), 0) == lax.broadcasted_iota(
        jnp.int32, (cols, cols), 1
    )
    x = xs[...]
    width = w_in.shape[1]
    block = 256
    total = None
    for which, (first, second) in enumerate(((c_in, c_out), (w_in, w_out))):
        for j in range(width // block):
            piece = slice(j * block, (j + 1) * block)
            h = jnp.dot(x, first[:, piece], preferred_element_type=f32)
            hid[which, :, piece] = silu(h).astype(bf16)
    cloud = jnp.dot(hid[0], c_out[...], preferred_element_type=f32)
    clear = jnp.dot(hid[1], w_out[...], preferred_element_type=f32)
    lane8 = lax.broadcasted_iota(jnp.int32, (8, LANES), 1)
    sub8 = lax.broadcasted_iota(jnp.int32, (8, LANES), 0)
    half_cols = cols // 2
    means = [jnp.zeros((8, LANES), f32) for _ in range(halves)]
    for r in range(rows):
        flag = jnp.sum(
            jnp.where(eye, jnp.broadcast_to(flags[r : r + 1, :], (cols, cols)), 0.0),
            axis=1,
            keepdims=True,
        )
        span = slice(r * cols, (r + 1) * cols)
        tendency = (clear[span] + flag * cloud[span]).astype(bf16).astype(f32)
        new = field[r] + tendency
        field[r] = new
        for k in range(cols // 8):
            at = (r // 2) * half_cols + 4 * k
            hit = lane8 == at + sub8 // 2
            for h in range(halves):
                value = new[8 * k : 8 * k + 8, h * LANES : h * LANES + 1]
                means[h] = means[h] + jnp.where(hit, value, 0.0)
    tops = [jnp.zeros((8, LANES), f32) for _ in range(2)]
    for r in range(sea_rows):
        for k in range(sea_cols // 8):
            hit = lane8 == r * sea_cols + 8 * k + sub8
            for h in range(2):
                at = h * (sea_feat // 2)
                value = ocean[r, 8 * k : 8 * k + 8, at : at + 1]
                tops[h] = tops[h] + jnp.where(hit, value, 0.0)
    for q, part in enumerate((0.25 * means[0], 0.25 * means[1], tops[0], tops[1])):
        line = jnp.sum(part, axis=0, keepdims=True)
        pay[:, q, :] = jnp.broadcast_to(line, (pay.shape[0], LANES))

    base = ASTEPS * halves * cols
    tall = sea_rows + 2 * OSTEPS
    sea_w[...] = jnp.zeros(sea_w.shape, f32)
    sea_e[...] = jnp.zeros(sea_e.shape, f32)
    for r in range(tall):
        keep = ok_n if r < OSTEPS else ok_s if r >= OSTEPS + sea_rows else None
        at = halves * pad + r * OSTEPS
        w, e = stage[0, at : at + OSTEPS, :], stage[1, at : at + OSTEPS, :]
        if keep is not None:
            w, e = jnp.where(keep, w, 0.0), jnp.where(keep, e, 0.0)
        sea_w[r, 8 - OSTEPS : 8, :] = w
        sea_e[r, 0:OSTEPS, :] = e

    sea_wide = sea_cols + 16
    sea_sub = lax.broadcasted_iota(jnp.int32, (tall, sea_wide, sea_feat), 1)
    sea_row = lax.broadcasted_iota(jnp.int32, (tall, sea_wide, sea_feat), 0)
    sea_in = jnp.logical_and(
        jnp.logical_and(
            jnp.logical_or(sea_sub >= 8, ok_w), jnp.logical_or(sea_sub < 8 + sea_cols, ok_e)
        ),
        jnp.logical_and(
            jnp.logical_or(sea_row >= OSTEPS, ok_n),
            jnp.logical_or(sea_row < OSTEPS + sea_rows, ok_s),
        ),
    )
    core = jnp.concatenate(
        [
            north[base : base + OSTEPS * sea_cols].reshape(OSTEPS, sea_cols, sea_feat),
            ocean[...],
            south[base : base + OSTEPS * sea_cols].reshape(OSTEPS, sea_cols, sea_feat),
        ],
        axis=0,
    )
    state = jnp.concatenate([sea_w[...], core, sea_e[...]], axis=1)
    nothing = jnp.zeros((1, sea_wide, sea_feat), f32)
    for step in range(OSTEPS):
        up = jnp.concatenate([nothing, state[:-1]], axis=0)
        down = jnp.concatenate([state[1:], nothing], axis=0)
        state = jnp.where(sea_in, relax(up, state, down, kappa_sea), 0.0)
    sea[...] = state[OSTEPS : OSTEPS + sea_rows, 8 : 8 + sea_cols]


def final(secs, tiles, tile_map, gathered, field, sea, air_out, sea_out, back):
    rows, cols, feat = field.shape
    sea_rows, sea_cols, sea_feat = sea.shape
    count = secs * tiles
    s, t = lax.axis_index("sec"), lax.axis_index("tile")
    me = s * tiles + t
    halves = feat // LANES
    row1 = lax.broadcasted_iota(jnp.int32, (count, 1), 0)
    row_t = row1 % tiles
    under = jnp.zeros((count, 1), jnp.int32)
    for k in range(tiles):
        under = jnp.where(row_t == k, tile_map[k], under)
    under = row1 - row_t + under
    perm = (lax.broadcasted_iota(jnp.int32, (count, count), 1) == under).astype(f32)
    air0 = jnp.dot(perm, gathered[:, 0, :], precision=HIGHEST, preferred_element_type=f32)
    air1 = jnp.dot(perm, gathered[:, 1, :], precision=HIGHEST, preferred_element_type=f32)
    top0, top1 = gathered[:, 2, :], gathered[:, 3, :]
    state0 = top0 + 0.5 * (0.8 * (top0 - air0))
    state1 = top1 + 0.5 * (0.8 * (0.5 * top0 - air1))

    lane = lax.broadcasted_iota(jnp.int32, (count, LANES), 1)
    row = lax.broadcasted_iota(jnp.int32, (count, LANES), 0)
    lane_c = lane % sea_cols
    first_c, last_c = lane_c == 0, lane_c == sea_cols - 1
    first_r, last_r = lane < sea_cols, lane >= LANES - sea_cols
    first_t, last_t = row % tiles == 0, row % tiles == tiles - 1
    first_s, last_s = row < tiles, row >= count - tiles

    def roll(v, shift, axis):
        return pltpu.roll(v, shift % v.shape[axis], axis)

    def relax(v):
        east_t = jnp.where(last_t, 0.0, roll(v, -1, 0))
        west_t = jnp.where(first_t, 0.0, roll(v, 1, 0))
        east = jnp.where(last_c, roll(east_t, sea_cols - 1, 1), roll(v, -1, 1))
        west = jnp.where(first_c, roll(west_t, 1 - sea_cols, 1), roll(v, 1, 1))
        down, up = roll(v, -sea_cols, 1), roll(v, sea_cols, 1)
        down_s = jnp.where(last_s, 0.0, roll(down, -tiles, 0))
        up_s = jnp.where(first_s, 0.0, roll(up, tiles, 0))
        beside = jnp.where(last_r, down_s, down) + jnp.where(first_r, up_s, up) + east + west
        return v + kappa_sea * (beside - 4.0 * v)

    for step in range(OSTEPS):
        state0, state1 = relax(state0), relax(state1)

    from_me = row1 == me
    source = under == me

    def pick(mask, v):
        return jnp.sum(jnp.where(mask, v, 0.0), axis=0, keepdims=True)

    own0, own1 = pick(from_me, state0), pick(from_me, state1)
    landing, returned = pick(source, top0), pick(source, state0)

    lane8 = lax.broadcasted_iota(jnp.int32, (8, LANES), 1)
    sub8 = lax.broadcasted_iota(jnp.int32, (8, LANES), 0)
    own0, own1 = jnp.broadcast_to(own0, (8, LANES)), jnp.broadcast_to(own1, (8, LANES))
    landing = jnp.broadcast_to(landing, (8, LANES))
    for r in range(sea_rows):
        for k in range(sea_cols // 8):
            hit = lane8 == r * sea_cols + 8 * k + sub8
            v0 = jnp.sum(jnp.where(hit, own0, 0.0), axis=1, keepdims=True)
            v1 = jnp.sum(jnp.where(hit, own1, 0.0), axis=1, keepdims=True)
            old = sea[r, 8 * k : 8 * k + 8, :]
            new = jnp.where(lane8 == 0, v0, jnp.where(lane8 == sea_feat // 2, v1, old))
            sea_out[r, 8 * k : 8 * k + 8, :] = new
    half_cols = cols // 2
    for r2 in range(rows // 2):
        for k in range(cols // 8):
            hit = lane8 == r2 * half_cols + 4 * k + sub8 // 2
            value = jnp.sum(jnp.where(hit, landing, 0.0), axis=1, keepdims=True)
            for r in (2 * r2, 2 * r2 + 1):
                for h in range(halves):
                    lanes = slice(h * LANES, (h + 1) * LANES)
                    old = field[r, 8 * k : 8 * k + 8, lanes]
                    flux = 0.8 * ((1.0 if h == 0 else 0.5) * value - old)
                    air_out[r, 8 * k : 8 * k + 8, lanes] = old + jnp.where(
                        lane8 == 0, 0.5 * flux, 0.0
                    )
    lane_b = lax.broadcasted_iota(jnp.int32, (rows, LANES), 1)
    row_b = lax.broadcasted_iota(jnp.int32, (rows, LANES), 0)
    lines = jnp.where(
        lane_b // half_cols == row_b // 2, jnp.broadcast_to(returned, (rows, LANES)), 0.0
    )
    spread = (
        lax.broadcasted_iota(jnp.int32, (LANES, cols), 0) % half_cols
        == lax.broadcasted_iota(jnp.int32, (LANES, cols), 1) // 2
    ).astype(f32)
    back[...] = jnp.dot(lines, spread, precision=HIGHEST, preferred_element_type=f32)


def local(atmos, cloudy, weight_in, weight_out, cloud_in, cloud_out, ocean, tile_map):
    rows, cols, feat = atmos.shape
    sea_rows, sea_cols, sea_feat = ocean.shape
    secs, tiles = lax.axis_size("sec"), lax.axis_size("tile")
    count = secs * tiles
    halves = feat // LANES
    columns = rows * cols
    width = weight_in.shape[1]
    sec_even, sec_odd, tile_even, tile_odd = exchanges(secs, tiles)
    shape = jax.ShapeDtypeStruct
    params = pltpu.CompilerParams(vmem_limit_bytes=16 * 1024 * 1024)

    lines = ASTEPS * halves * cols + OSTEPS * sea_cols
    out = shape((lines, LANES), bf16)
    send_a, send_b = pl.pallas_call(
        pack_sec, out_shape=(out, out), in_specs=[VMEM] * 2, out_specs=(VMEM, VMEM),
        compiler_params=params, name="pack_sec",
    )(atmos, ocean)
    sec_a = lax.ppermute(send_a, AXES, sec_even)
    sec_b = lax.ppermute(send_b, AXES, sec_odd)

    lines = halves * air_pad(rows) + OSTEPS * (sea_rows + 2 * OSTEPS)
    out = shape((lines, LANES), bf16)
    send_a, send_b = pl.pallas_call(
        pack_tile, out_shape=(out, out), in_specs=[VMEM] * 4, out_specs=(VMEM, VMEM),
        scratch_shapes=[pltpu.VMEM((2, lines, LANES), f32)],
        compiler_params=params, name="pack_tile",
    )(atmos, ocean, sec_a, sec_b)
    tile_a = lax.ppermute(send_a, AXES, tile_even)
    tile_b = lax.ppermute(send_b, AXES, tile_odd)

    field, pay, sea = pl.pallas_call(
        functools.partial(main, secs, tiles),
        out_shape=(
            shape(atmos.shape, f32),
            shape((count, 4, LANES), f32),
            shape(ocean.shape, f32),
        ),
        in_specs=[VMEM] * 11,
        out_specs=(VMEM,) * 3,
        scratch_shapes=[
            pltpu.VMEM((rows + 2, 8, feat), f32),
            pltpu.VMEM((rows + 2, 8, feat), f32),
            pltpu.VMEM((columns, feat), bf16),
            pltpu.VMEM((2, columns, width), bf16),
            pltpu.VMEM((2, lines, LANES), f32),
            pltpu.VMEM((sea_rows + 2 * OSTEPS, 8, sea_feat), f32),
            pltpu.VMEM((sea_rows + 2 * OSTEPS, 8, sea_feat), f32),
        ],
        compiler_params=params,
        name="main",
    )(atmos, cloudy, weight_in, weight_out, cloud_in, cloud_out, ocean, sec_a, sec_b, tile_a, tile_b)

    gathered = lax.all_to_all(pay, AXES, 0, 0)

    return pl.pallas_call(
        functools.partial(final, secs, tiles),
        out_shape=(
            shape(atmos.shape, f32),
            shape(ocean.shape, f32),
            shape((rows, cols), f32),
        ),
        in_specs=[SMEM] + [VMEM] * 3,
        out_specs=(VMEM,) * 3,
        compiler_params=params,
        name="final",
    )(tile_map, gathered, field, sea)


def solution(mesh):
    placed = (
        P("sec", "tile", None),
        P("sec", "tile"),
        P(),
        P(),
        P(),
        P(),
        P("sec", "tile", None),
        P(),
    )
    return jax.shard_map(
        local,
        mesh=mesh,
        in_specs=placed,
        out_specs=(P("sec", "tile", None), P("sec", "tile", None), P("sec", "tile")),
        check_vma=False,
    )
```

```python
import functools

import jax
import jax.numpy as jnp
from jax import lax
from jax.experimental import pallas as pl
from jax.experimental.pallas import tpu as pltpu
from jax.sharding import PartitionSpec as P

ASTEPS = 2
OSTEPS = 4
LANES = 128

kappa_air = 0.2
kappa_sea = 0.2

f32 = jnp.float32
bf16 = jnp.bfloat16
HIGHEST = lax.Precision.HIGHEST
VMEM = pl.BlockSpec(memory_space=pltpu.VMEM)
SMEM = pl.BlockSpec(memory_space=pltpu.SMEM)
HBM = pl.BlockSpec(memory_space=pltpu.HBM)
AXES = ("sec", "tile")


def exchanges(secs, tiles):
    def whole(partner):
        return [
            (s * tiles + t, partner(s, t)[0] * tiles + partner(s, t)[1])
            for s in range(secs)
            for t in range(tiles)
        ]

    def odd_sec(s, t):
        if s in (0, secs - 1):
            return secs - 1 - s, t
        return (s + 1 if s % 2 else s - 1), t

    def odd_tile(s, t):
        if t in (0, tiles - 1):
            return s ^ 1, t
        return s, (t + 1 if t % 2 else t - 1)

    return (
        whole(lambda s, t: (s ^ 1, t)),
        whole(odd_sec),
        whole(lambda s, t: (s, t ^ 1)),
        whole(odd_tile),
    )


def sublane(shape):
    return lax.broadcasted_iota(jnp.int32, shape, len(shape) - 2)


def turn(v, shift):
    return v if shift % 8 == 0 else pltpu.roll(v, shift % 8, 0)


def halves_of(v):
    return [v[:, at : at + LANES] for at in range(0, v.shape[1], LANES)]


def pack_tile(atmos, ocean, out_a, out_b, west, east, sea, sems):
    rows, cols, feat = atmos.shape
    sea_rows, sea_cols, _ = ocean.shape
    copies = (
        pltpu.make_async_copy(atmos.at[:, 0:8, :], west, sems.at[0]),
        pltpu.make_async_copy(atmos.at[:, cols - 8 : cols, :], east, sems.at[1]),
        pltpu.make_async_copy(ocean, sea, sems.at[2]),
    )
    for copy in copies:
        copy.start()
    for copy in copies:
        copy.wait()
    to_west, to_east = [], []
    sub = sublane((8, feat))
    for g in range(rows // 4):
        tile_w, tile_e = west[4 * g], turn(east[4 * g], 2)
        for k in range(1, 4):
            tile_w = jnp.where(sub < 2 * k, tile_w, turn(west[4 * g + k], 2 * k))
            tile_e = jnp.where(sub < 2 * k, tile_e, turn(east[4 * g + k], 2 * k + 2))
        to_west += halves_of(tile_w)
        to_east += halves_of(tile_e)
    low = sublane((8, LANES)) < 4
    for r in range(0, sea_rows, 2):
        to_west.append(jnp.where(low, sea[r, 0:8], turn(sea[r + 1, 0:8], 4)))
        to_east.append(
            jnp.where(low, turn(sea[r, sea_cols - 8 :], 4), sea[r + 1, sea_cols - 8 :])
        )
    to_west = jnp.concatenate(to_west, axis=0).astype(bf16)
    to_east = jnp.concatenate(to_east, axis=0).astype(bf16)
    even = lax.axis_index("tile") % 2 == 0
    out_a[...] = jnp.where(even, to_east, to_west)
    out_b[...] = jnp.where(even, to_west, to_east)


class Sides:
    def __init__(self, tiles, rows, feat, tile_a, tile_b):
        t = lax.axis_index("tile")
        even = t % 2 == 0
        a, b = tile_a[...].astype(f32), tile_b[...].astype(f32)
        self.west = jnp.where(t > 0, jnp.where(even, b, a), 0.0)
        self.east = jnp.where(t < tiles - 1, jnp.where(even, a, b), 0.0)
        self.halves = feat // LANES
        self.sea_at = rows // 4 * self.halves
        self.low = sublane((8, LANES)) < 4

    def merge(self, tile, shift_w, shift_e):
        span = slice(8 * tile, 8 * tile + 8)
        return jnp.where(self.low, turn(self.east[span], shift_e), turn(self.west[span], shift_w))

    def air(self, r):
        g, k = r // 4, r % 4
        return jnp.concatenate(
            [self.merge(g * self.halves + h, -2 * k - 2, -2 * k) for h in range(self.halves)],
            axis=1,
        )

    def sea(self, r):
        return self.merge(self.sea_at + r // 2, 4 if r % 2 == 0 else 0, 4 * (r % 2))


def pack_sec(tiles, atmos, ocean, tile_a, tile_b, out_a, out_b):
    rows, cols, feat = atmos.shape
    sea_rows, sea_cols, _ = ocean.shape
    sides = Sides(tiles, rows, feat, tile_a, tile_b)

    def payload(first, corner, sea_first):
        parts = []
        for r in range(ASTEPS):
            parts += halves_of(atmos[first + r])
        parts += halves_of(sides.air(corner))
        parts += [ocean[sea_first + r] for r in range(OSTEPS)]
        parts += [sides.sea(sea_first + r) for r in range(OSTEPS)]
        return jnp.concatenate(parts, axis=0).astype(bf16)

    to_north = payload(0, 0, 0)
    to_south = payload(rows - ASTEPS, rows - 1, sea_rows - OSTEPS)
    even = lax.axis_index("sec") % 2 == 0
    out_a[...] = jnp.where(even, to_south, to_north)
    out_b[...] = jnp.where(even, to_north, to_south)


class Ends:
    def __init__(self, secs, cols, feat, sea_cols, sec_a, sec_b):
        s = lax.axis_index("sec")
        even = s % 2 == 0
        a, b = sec_a[...].astype(f32), sec_b[...].astype(f32)
        self.north = jnp.where(s > 0, jnp.where(even, b, a), 0.0)
        self.south = jnp.where(s < secs - 1, jnp.where(even, a, b), 0.0)
        self.halves, self.cols, self.sea_cols = feat // LANES, cols, sea_cols
        self.corner = ASTEPS * self.halves * cols
        self.sea_at = self.corner + 8 * self.halves
        self.side_at = self.sea_at + OSTEPS * sea_cols

    def air(self, piece, k):
        cut = [(k * self.halves + h) * self.cols for h in range(self.halves)]
        return jnp.concatenate([piece[at : at + self.cols] for at in cut], axis=1)

    def air_side(self, piece):
        cut = [self.corner + 8 * h for h in range(self.halves)]
        return jnp.concatenate([piece[at : at + 8] for at in cut], axis=1)

    def sea(self, piece, k):
        core = piece[self.sea_at + k * self.sea_cols : self.sea_at + (k + 1) * self.sea_cols]
        side = piece[self.side_at + 8 * k : self.side_at + 8 * k + 8]
        return core, side


def relax(up, mid, down, rate):
    axis = mid.ndim - 2
    beside = up + down + pltpu.roll(mid, 1, axis) + pltpu.roll(mid, mid.shape[axis] - 1, axis)
    return mid + rate * (beside - 4.0 * mid)


def columns_inside(tiles, shape):
    t = lax.axis_index("tile")
    sub = sublane(shape)
    return jnp.logical_and(
        jnp.logical_or(sub >= 8, t > 0), jnp.logical_or(sub < shape[-2] - 8, t < tiles - 1)
    )


def silu(v):
    return v * (0.5 + 0.5 * jnp.tanh(0.5 * v))


def physics(x, w_in, w_out, c_in, c_out, hid):
    width = w_in.shape[1]
    block = 256
    for which, first in enumerate((w_in, c_in)):
        for j in range(0, width, block):
            h = jnp.dot(x, first[:, j : j + block], preferred_element_type=f32)
            hid[which, :, j : j + block] = silu(h).astype(bf16)
    clear = jnp.dot(hid[0], w_out[...], preferred_element_type=f32)
    cloud = jnp.dot(hid[1], c_out[...], preferred_element_type=f32)
    return clear, cloud


def upright(line):
    n = line.shape[1]
    shape = (n, n)
    eye = sublane(shape) == lax.broadcasted_iota(jnp.int32, shape, 1)
    return jnp.sum(jnp.where(eye, jnp.broadcast_to(line, shape), 0.0), axis=1, keepdims=True)


def tile_iotas():
    return lax.broadcasted_iota(jnp.int32, (8, LANES), 1), sublane((8, LANES))


def add_row(means, new, r):
    lane, sub = tile_iotas()
    cols = new.shape[0]
    for k in range(cols // 8):
        hit = lane == (r // 2) * (cols // 2) + 4 * k + sub // 2
        for q in range(2):
            value = new[8 * k : 8 * k + 8, q * LANES : q * LANES + 1]
            means[q] = means[q] + jnp.where(hit, value, 0.0)


def inner(
    secs, tiles, tile_map, atmos, cloudy, w_in, w_out, c_in, c_out, ocean, tile_a, tile_b,
    field, sums, perm, source, xs, hid,
):
    rows, cols, feat = atmos.shape
    sea_rows, sea_cols, sea_feat = ocean.shape
    sides = Sides(tiles, rows, feat, tile_a, tile_b)
    inside = columns_inside(tiles, (cols + 16, feat))

    def line(r):
        side = sides.air(r)
        return jnp.concatenate([side, atmos[r], side], axis=0)

    lines, ones = [line(0), line(1)], []
    for r in range(1, rows - 1):
        lines.append(line(r + 1))
        ones.append(jnp.where(inside, relax(*lines[-3:], kappa_air), 0.0))
        if len(ones) >= 3:
            two = relax(*ones[-3:], kappa_air)[8 : 8 + cols]
            field[r - 3] = two
            xs[(r - 3) * cols : (r - 2) * cols, :] = two.astype(bf16)
    clear, cloud = physics(xs[...], w_in, w_out, c_in, c_out, hid)
    flags = cloudy[...].astype(f32)
    means = [jnp.zeros((8, LANES), f32) for _ in range(2)]
    for k in range(rows - 4):
        span = slice(k * cols, (k + 1) * cols)
        flag = upright(flags[k + 2 : k + 3, :])
        new = field[k] + (clear[span] + flag * cloud[span]).astype(bf16).astype(f32)
        field[k] = new
        add_row(means, new, k + 2)
    lane, sub = tile_iotas()
    tops = [jnp.zeros((8, LANES), f32) for _ in range(2)]
    for r in range(sea_rows):
        for k in range(sea_cols // 8):
            hit = lane == r * sea_cols + 8 * k + sub
            for q in range(2):
                at = q * (sea_feat // 2)
                value = ocean[r, 8 * k : 8 * k + 8, at : at + 1]
                tops[q] = tops[q] + jnp.where(hit, value, 0.0)
    for q, part in enumerate(means + tops):
        sums[q] = part
    count = secs * tiles
    me = lax.axis_index("sec") * tiles + lax.axis_index("tile")
    row = sublane((count, LANES))
    row_t = row % tiles
    under = jnp.zeros((count, LANES), jnp.int32)
    for k in range(tiles):
        under = jnp.where(row_t == k, tile_map[k], under)
    under = row - row_t + under
    source[...] = (under == me).astype(f32)
    perm[...] = (lax.broadcasted_iota(jnp.int32, (count, count), 1) == under[:, 0:1]).astype(f32)


def border(
    secs, tiles, atmos, cloudy, w_in, w_out, c_in, c_out, tile_a, tile_b, sec_a, sec_b, sums,
    field, pay, xs, hid,
):
    rows, cols, feat = atmos.shape
    s = lax.axis_index("sec")
    sides = Sides(tiles, rows, feat, tile_a, tile_b)
    ends = Ends(secs, cols, feat, sums.shape[2] // (rows // 2), sec_a, sec_b)
    inside = columns_inside(tiles, (cols + 16, feat))

    def line(r):
        if 0 <= r < rows:
            core, side = atmos[r], sides.air(r)
        else:
            piece = ends.north if r < 0 else ends.south
            core = ends.air(piece, r + ASTEPS if r < 0 else r - rows)
            side = ends.air_side(piece)
        return jnp.concatenate([side, core, side], axis=0)

    at = 0
    for first in (0, rows - 2):
        lines = [line(r) for r in range(first - 2, first + 4)]
        ones = [jnp.where(inside, relax(*lines[k : k + 3], kappa_air), 0.0) for k in range(4)]
        if first == 0:
            ones[0] = jnp.where(s > 0, ones[0], 0.0)
        else:
            ones[3] = jnp.where(s < secs - 1, ones[3], 0.0)
        for k in range(2):
            two = relax(*ones[k : k + 3], kappa_air)[8 : 8 + cols]
            field[at] = two
            xs[at * cols : (at + 1) * cols, :] = two.astype(bf16)
            at += 1
    clear, cloud = physics(xs[...], w_in, w_out, c_in, c_out, hid)
    flags = cloudy[...].astype(f32)
    means = [sums[0], sums[1]]
    for at, r in enumerate((0, 1, rows - 2, rows - 1)):
        span = slice(at * cols, (at + 1) * cols)
        flag = upright(flags[r : r + 1, :])
        new = field[at] + (clear[span] + flag * cloud[span]).astype(bf16).astype(f32)
        field[at] = new
        add_row(means, new, r)
    for q, part in enumerate((0.25 * means[0], 0.25 * means[1], sums[2], sums[3])):
        total = jnp.sum(part, axis=0, keepdims=True)
        pay[:, q, :] = jnp.broadcast_to(total, (pay.shape[0], LANES))


def sea_steps(secs, tiles, rows, cols, feat, ocean, tile_a, tile_b, sec_a, sec_b, out):
    sea_rows, sea_cols, sea_feat = ocean.shape
    s = lax.axis_index("sec")
    sides = Sides(tiles, rows, feat, tile_a, tile_b)
    ends = Ends(secs, cols, feat, sea_cols, sec_a, sec_b)
    inside = columns_inside(tiles, (sea_cols + 16, sea_feat))
    state = []
    for r in range(-OSTEPS, sea_rows + OSTEPS):
        if 0 <= r < sea_rows:
            core, side = ocean[r], sides.sea(r)
        elif r < 0:
            core, side = ends.sea(ends.north, r + OSTEPS)
        else:
            core, side = ends.sea(ends.south, r - sea_rows)
        state.append(jnp.concatenate([side, core, side], axis=0))
    for step in range(OSTEPS):
        state = [relax(*state[k : k + 3], kappa_sea) for k in range(len(state) - 2)]
        depth = OSTEPS - 1 - step
        for k, new in enumerate(state):
            new = jnp.where(inside, new, 0.0)
            if k < depth:
                new = jnp.where(s > 0, new, 0.0)
            elif k >= depth + sea_rows:
                new = jnp.where(s < secs - 1, new, 0.0)
            state[k] = new
    for r in range(sea_rows):
        out[r] = state[r][8 : 8 + sea_cols]


def final(
    secs, tiles, gathered, perm, source, inner_rows, border_rows, sea,
    air_out, sea_out, back, stage, sems,
):
    rows, cols, feat = air_out.shape
    sea_rows, sea_cols, sea_feat = sea.shape
    count = secs * tiles
    me = lax.axis_index("sec") * tiles + lax.axis_index("tile")
    halves = feat // LANES
    half_cols = cols // 2
    top0, top1 = gathered[:, 2, :], gathered[:, 3, :]
    lane8, sub8 = tile_iotas()

    def pick(mask, v):
        return jnp.broadcast_to(jnp.sum(mask * v, axis=0, keepdims=True), (8, LANES))

    landing = pick(source[...], top0)
    step_rows = 4
    copies = []
    for first in range(0, rows, step_rows):
        for r2 in range(first // 2, (first + step_rows) // 2):
            for k in range(cols // 8):
                cells = slice(8 * k, 8 * k + 8)
                hit = lane8 == r2 * half_cols + 4 * k + sub8 // 2
                value = jnp.sum(jnp.where(hit, landing, 0.0), axis=1, keepdims=True)
                for r in (2 * r2, 2 * r2 + 1):
                    for h in range(halves):
                        lanes = slice(h * LANES, (h + 1) * LANES)
                        if r < 2:
                            old = border_rows[r, cells, lanes]
                        elif r >= rows - 2:
                            old = border_rows[r - rows + 4, cells, lanes]
                        else:
                            old = inner_rows[r - 2, cells, lanes]
                        flux = 0.8 * ((1.0 if h == 0 else 0.5) * value - old)
                        stage[r, cells, lanes] = old + jnp.where(lane8 == 0, 0.5 * flux, 0.0)
        copy = pltpu.make_async_copy(
            stage.at[first : first + step_rows],
            air_out.at[first : first + step_rows],
            sems.at[first // step_rows],
        )
        copy.start()
        copies.append(copy)

    air0 = jnp.dot(
        perm[...], gathered[:, 0, :], precision=HIGHEST, preferred_element_type=f32
    )
    air1 = jnp.dot(
        perm[...], gathered[:, 1, :], precision=HIGHEST, preferred_element_type=f32
    )
    state0 = top0 + 0.5 * (0.8 * (top0 - air0))
    state1 = top1 + 0.5 * (0.8 * (0.5 * top0 - air1))

    lane = lax.broadcasted_iota(jnp.int32, (count, LANES), 1)
    row = sublane((count, LANES))
    lane_c = lane % sea_cols
    first_c, last_c = lane_c == 0, lane_c == sea_cols - 1
    first_r, last_r = lane < sea_cols, lane >= LANES - sea_cols
    first_t, last_t = row % tiles == 0, row % tiles == tiles - 1
    first_s, last_s = row < tiles, row >= count - tiles

    def roll(v, shift, axis):
        return pltpu.roll(v, shift % v.shape[axis], axis)

    def step(v):
        east_t = jnp.where(last_t, 0.0, roll(v, -1, 0))
        west_t = jnp.where(first_t, 0.0, roll(v, 1, 0))
        east = jnp.where(last_c, roll(east_t, sea_cols - 1, 1), roll(v, -1, 1))
        west = jnp.where(first_c, roll(west_t, 1 - sea_cols, 1), roll(v, 1, 1))
        down, up = roll(v, -sea_cols, 1), roll(v, sea_cols, 1)
        down_s = jnp.where(last_s, 0.0, roll(down, -tiles, 0))
        up_s = jnp.where(first_s, 0.0, roll(up, tiles, 0))
        beside = jnp.where(last_r, down_s, down) + jnp.where(first_r, up_s, up) + east + west
        return v + kappa_sea * (beside - 4.0 * v)

    for _ in range(OSTEPS):
        state0, state1 = step(state0), step(state1)
    from_me = (row == me).astype(f32)
    own0, own1 = pick(from_me, state0), pick(from_me, state1)
    returned = pick(source[...], state0)
    for r in range(sea_rows):
        for k in range(sea_cols // 8):
            hit = lane8 == r * sea_cols + 8 * k + sub8
            v0 = jnp.sum(jnp.where(hit, own0, 0.0), axis=1, keepdims=True)
            v1 = jnp.sum(jnp.where(hit, own1, 0.0), axis=1, keepdims=True)
            old = sea[r, 8 * k : 8 * k + 8, :]
            new = jnp.where(lane8 == 0, v0, jnp.where(lane8 == sea_feat // 2, v1, old))
            sea_out[r, 8 * k : 8 * k + 8, :] = new
    lane_b = lax.broadcasted_iota(jnp.int32, (rows, LANES), 1)
    lines = jnp.where(
        lane_b // half_cols == sublane((rows, LANES)) // 2, jnp.tile(returned, (rows // 8, 1)), 0.0
    )
    spread = (
        sublane((LANES, cols)) % half_cols
        == lax.broadcasted_iota(jnp.int32, (LANES, cols), 1) // 2
    ).astype(f32)
    back[...] = jnp.dot(lines, spread, precision=HIGHEST, preferred_element_type=f32)
    for copy in copies:
        copy.wait()


def local(atmos, cloudy, weight_in, weight_out, cloud_in, cloud_out, ocean, tile_map):
    rows, cols, feat = atmos.shape
    sea_rows, sea_cols, sea_feat = ocean.shape
    secs, tiles = lax.axis_size("sec"), lax.axis_size("tile")
    count = secs * tiles
    halves = feat // LANES
    width = weight_in.shape[1]
    sec_even, sec_odd, tile_even, tile_odd = exchanges(secs, tiles)
    shape = jax.ShapeDtypeStruct

    def call(body, name, out_shape, in_specs, out_specs, scratch=(), flops=0, args=()):
        return pl.pallas_call(
            body,
            out_shape=out_shape,
            in_specs=in_specs,
            out_specs=out_specs,
            scratch_shapes=scratch,
            compiler_params=pltpu.CompilerParams(vmem_limit_bytes=8 * 1024 * 1024),
            cost_estimate=pl.CostEstimate(flops=flops, bytes_accessed=0, transcendentals=0),
            name=name,
        )(*args)

    out = shape((8 * (rows // 4 * halves + sea_rows // 2), LANES), bf16)
    send_a, send_b = call(
        pack_tile, "pack_tile", (out, out), [HBM] * 2, (VMEM, VMEM),
        [
            pltpu.VMEM((rows, 8, feat), f32),
            pltpu.VMEM((rows, 8, feat), f32),
            pltpu.VMEM(ocean.shape, f32),
            pltpu.SemaphoreType.DMA((3,)),
        ],
        args=(atmos, ocean),
    )
    tile_a = lax.ppermute(send_a, AXES, tile_even)
    tile_b = lax.ppermute(send_b, AXES, tile_odd)

    lines = halves * (ASTEPS * cols + 8) + OSTEPS * (sea_cols + 8)
    out = shape((lines, LANES), bf16)
    send_a, send_b = call(
        functools.partial(pack_sec, tiles), "pack_sec", (out, out), [VMEM] * 4, (VMEM, VMEM),
        args=(atmos, ocean, tile_a, tile_b),
    )
    sec_a = lax.ppermute(send_a, AXES, sec_even)
    sec_b = lax.ppermute(send_b, AXES, sec_odd)

    weights = (weight_in, weight_out, cloud_in, cloud_out)
    within = (rows - 4) * cols
    inner_rows, sums, perm, source = call(
        functools.partial(inner, secs, tiles), "inner",
        (
            shape((rows - 4, cols, feat), f32),
            shape((4, 8, LANES), f32),
            shape((count, count), f32),
            shape((count, LANES), f32),
        ),
        [SMEM] + [VMEM] * 9,
        (VMEM,) * 4,
        [pltpu.VMEM((within, feat), bf16), pltpu.VMEM((2, within, width), bf16)],
        flops=within * feat * width * 8,
        args=(tile_map, atmos, cloudy, *weights, ocean, tile_a, tile_b),
    )
    border_rows, pay = call(
        functools.partial(border, secs, tiles), "border",
        (shape((4, cols, feat), f32), shape((count, 4, LANES), f32)),
        [VMEM] * 11,
        (VMEM,) * 2,
        [pltpu.VMEM((4 * cols, feat), bf16), pltpu.VMEM((2, 4 * cols, width), bf16)],
        flops=4 * cols * feat * width * 8,
        args=(atmos, cloudy, *weights, tile_a, tile_b, sec_a, sec_b, sums),
    )
    gathered = lax.all_to_all(pay, AXES, 0, 0)
    sea = call(
        functools.partial(sea_steps, secs, tiles, rows, cols, feat), "sea_steps",
        shape(ocean.shape, f32), [VMEM] * 5, VMEM,
        flops=100 * ocean.size,
        args=(ocean, tile_a, tile_b, sec_a, sec_b),
    )
    return call(
        functools.partial(final, secs, tiles), "final",
        (shape(atmos.shape, f32), shape(ocean.shape, f32), shape((rows, cols), f32)),
        [VMEM] * 6,
        (HBM, VMEM, VMEM),
        [pltpu.VMEM(atmos.shape, f32), pltpu.SemaphoreType.DMA((rows // 4,))],
        args=(gathered, perm, source, inner_rows, border_rows, sea),
    )


def solution(mesh):
    placed = (
        P("sec", "tile", None),
        P("sec", "tile"),
        P(),
        P(),
        P(),
        P(),
        P("sec", "tile", None),
        P(),
    )
    return jax.shard_map(
        local,
        mesh=mesh,
        in_specs=placed,
        out_specs=(P("sec", "tile", None), P("sec", "tile", None), P("sec", "tile")),
        check_vma=False,
    )
```

```python
import functools

import jax
import jax.numpy as jnp
from jax import lax
from jax.experimental import pallas as pl
from jax.experimental.pallas import tpu as pltpu
from jax.sharding import PartitionSpec as P

ASTEPS = 2
OSTEPS = 4
LANES = 128

kappa_air = 0.2
kappa_sea = 0.2

f32 = jnp.float32
bf16 = jnp.bfloat16
VMEM = pl.BlockSpec(memory_space=pltpu.VMEM)
HBM = pl.BlockSpec(memory_space=pltpu.HBM)
AXES = ("sec", "tile")


def exchanges(secs, tiles):
    def whole(partner):
        return [
            (s * tiles + t, partner(s, t)[0] * tiles + partner(s, t)[1])
            for s in range(secs)
            for t in range(tiles)
        ]

    def odd_sec(s, t):
        if s in (0, secs - 1):
            return secs - 1 - s, t
        return (s + 1 if s % 2 else s - 1), t

    def odd_tile(s, t):
        if t in (0, tiles - 1):
            return s ^ 1, t
        return s, (t + 1 if t % 2 else t - 1)

    return (
        whole(lambda s, t: (s ^ 1, t)),
        whole(odd_sec),
        whole(lambda s, t: (s, t ^ 1)),
        whole(odd_tile),
    )


def sublane(shape):
    return lax.broadcasted_iota(jnp.int32, shape, len(shape) - 2)


def turn(v, shift):
    return v if shift % 8 == 0 else pltpu.roll(v, shift % 8, 0)


def halves_of(v):
    return [v[:, at : at + LANES] for at in range(0, v.shape[1], LANES)]


def pack_tile(atmos, ocean, out_a, out_b, west, east, sea, sems):
    rows, cols, feat = atmos.shape
    sea_rows, sea_cols, _ = ocean.shape
    copies = (
        pltpu.make_async_copy(atmos.at[:, 0:8, :], west, sems.at[0]),
        pltpu.make_async_copy(atmos.at[:, cols - 8 : cols, :], east, sems.at[1]),
        pltpu.make_async_copy(ocean, sea, sems.at[2]),
    )
    for copy in copies:
        copy.start()
    for copy in copies:
        copy.wait()
    to_west, to_east = [], []
    sub = sublane((8, feat))
    for g in range(rows // 4):
        tile_w, tile_e = west[4 * g], turn(east[4 * g], 2)
        for k in range(1, 4):
            tile_w = jnp.where(sub < 2 * k, tile_w, turn(west[4 * g + k], 2 * k))
            tile_e = jnp.where(sub < 2 * k, tile_e, turn(east[4 * g + k], 2 * k + 2))
        to_west += halves_of(tile_w)
        to_east += halves_of(tile_e)
    low = sublane((8, LANES)) < 4
    for r in range(0, sea_rows, 2):
        to_west.append(jnp.where(low, sea[r, 0:8], turn(sea[r + 1, 0:8], 4)))
        to_east.append(
            jnp.where(low, turn(sea[r, sea_cols - 8 :], 4), sea[r + 1, sea_cols - 8 :])
        )
    to_west = jnp.concatenate(to_west, axis=0).astype(bf16)
    to_east = jnp.concatenate(to_east, axis=0).astype(bf16)
    even = lax.axis_index("tile") % 2 == 0
    out_a[...] = jnp.where(even, to_east, to_west)
    out_b[...] = jnp.where(even, to_west, to_east)


class Sides:
    def __init__(self, tiles, rows, feat, tile_a, tile_b):
        t = lax.axis_index("tile")
        even = t % 2 == 0
        a, b = tile_a[...].astype(f32), tile_b[...].astype(f32)
        self.west = jnp.where(t > 0, jnp.where(even, b, a), 0.0)
        self.east = jnp.where(t < tiles - 1, jnp.where(even, a, b), 0.0)
        self.halves = feat // LANES
        self.sea_at = rows // 4 * self.halves
        self.low = sublane((8, LANES)) < 4

    def merge(self, tile, shift_w, shift_e):
        span = slice(8 * tile, 8 * tile + 8)
        return jnp.where(self.low, turn(self.east[span], shift_e), turn(self.west[span], shift_w))

    def air(self, r):
        g, k = r // 4, r % 4
        return jnp.concatenate(
            [self.merge(g * self.halves + h, -2 * k - 2, -2 * k) for h in range(self.halves)],
            axis=1,
        )

    def sea(self, r):
        return self.merge(self.sea_at + r // 2, 4 if r % 2 == 0 else 0, 4 * (r % 2))


def pack_sec(tiles, atmos, ocean, tile_a, tile_b, out_a, out_b):
    rows, cols, feat = atmos.shape
    sea_rows, sea_cols, _ = ocean.shape
    sides = Sides(tiles, rows, feat, tile_a, tile_b)

    def payload(first, corner, sea_first):
        parts = []
        for r in range(ASTEPS):
            parts += halves_of(atmos[first + r])
        parts += halves_of(sides.air(corner))
        parts += [ocean[sea_first + r] for r in range(OSTEPS)]
        parts += [sides.sea(sea_first + r) for r in range(OSTEPS)]
        return jnp.concatenate(parts, axis=0).astype(bf16)

    to_north = payload(0, 0, 0)
    to_south = payload(rows - ASTEPS, rows - 1, sea_rows - OSTEPS)
    even = lax.axis_index("sec") % 2 == 0
    out_a[...] = jnp.where(even, to_south, to_north)
    out_b[...] = jnp.where(even, to_north, to_south)


class Ends:
    def __init__(self, secs, cols, feat, sea_cols, sec_a, sec_b):
        s = lax.axis_index("sec")
        even = s % 2 == 0
        a, b = sec_a[...].astype(f32), sec_b[...].astype(f32)
        self.north = jnp.where(s > 0, jnp.where(even, b, a), 0.0)
        self.south = jnp.where(s < secs - 1, jnp.where(even, a, b), 0.0)
        self.halves, self.cols, self.sea_cols = feat // LANES, cols, sea_cols
        self.corner = ASTEPS * self.halves * cols
        self.sea_at = self.corner + 8 * self.halves
        self.side_at = self.sea_at + OSTEPS * sea_cols

    def air(self, piece, k):
        cut = [(k * self.halves + h) * self.cols for h in range(self.halves)]
        return jnp.concatenate([piece[at : at + self.cols] for at in cut], axis=1)

    def air_side(self, piece):
        cut = [self.corner + 8 * h for h in range(self.halves)]
        return jnp.concatenate([piece[at : at + 8] for at in cut], axis=1)

    def sea(self, piece, k):
        core = piece[self.sea_at + k * self.sea_cols : self.sea_at + (k + 1) * self.sea_cols]
        side = piece[self.side_at + 8 * k : self.side_at + 8 * k + 8]
        return core, side


def relax(up, mid, down, rate):
    axis = mid.ndim - 2
    beside = up + down + pltpu.roll(mid, 1, axis) + pltpu.roll(mid, mid.shape[axis] - 1, axis)
    return mid + rate * (beside - 4.0 * mid)


def columns_inside(tiles, shape):
    t = lax.axis_index("tile")
    sub = sublane(shape)
    return jnp.logical_and(
        jnp.logical_or(sub >= 8, t > 0), jnp.logical_or(sub < shape[-2] - 8, t < tiles - 1)
    )


def silu(v):
    return v * (0.5 + 0.5 * jnp.tanh(0.5 * v))


def physics(x, w_in, w_out, c_in, c_out, hid):
    width = w_in.shape[1]
    block = 256
    for which, first in enumerate((w_in, c_in)):
        for j in range(0, width, block):
            h = jnp.dot(x, first[:, j : j + block], preferred_element_type=f32)
            hid[which, :, j : j + block] = silu(h).astype(bf16)
    clear = jnp.dot(hid[0], w_out[...], preferred_element_type=f32)
    cloud = jnp.dot(hid[1], c_out[...], preferred_element_type=f32)
    return clear, cloud


def upright(line):
    n = line.shape[1]
    shape = (n, n)
    eye = sublane(shape) == lax.broadcasted_iota(jnp.int32, shape, 1)
    return jnp.sum(jnp.where(eye, jnp.broadcast_to(line, shape), 0.0), axis=1, keepdims=True)


def tile_iotas():
    return lax.broadcasted_iota(jnp.int32, (8, LANES), 1), sublane((8, LANES))


def add_row(means, new, r):
    lane, sub = tile_iotas()
    cols = new.shape[0]
    for k in range(cols // 8):
        hit = lane == (r // 2) * (cols // 2) + 4 * k + sub // 2
        for q in range(2):
            value = new[8 * k : 8 * k + 8, q * LANES : q * LANES + 1]
            means[q] = means[q] + jnp.where(hit, value, 0.0)


def inner(
    secs, tiles, tile_map, atmos, cloudy, w_in, w_out, c_in, c_out, ocean, tile_a, tile_b,
    field, sums, perm, source, spots, cells, spread, xs, hid, place, place_sem,
):
    map_copy = pltpu.make_async_copy(tile_map, place, place_sem)
    map_copy.start()
    rows, cols, feat = atmos.shape
    sea_rows, sea_cols, sea_feat = ocean.shape
    sides = Sides(tiles, rows, feat, tile_a, tile_b)
    inside = columns_inside(tiles, (cols + 16, feat))

    def line(r):
        side = sides.air(r)
        return jnp.concatenate([side, atmos[r], side], axis=0)

    lines, ones = [line(0), line(1)], []
    for r in range(1, rows - 1):
        lines.append(line(r + 1))
        ones.append(jnp.where(inside, relax(*lines[-3:], kappa_air), 0.0))
        if len(ones) >= 3:
            two = relax(*ones[-3:], kappa_air)[8 : 8 + cols]
            field[r - 3] = two
            xs[(r - 3) * cols : (r - 2) * cols, :] = two.astype(bf16)
    clear, cloud = physics(xs[...], w_in, w_out, c_in, c_out, hid)
    flags = cloudy[...].astype(f32)
    means = [jnp.zeros((8, LANES), f32) for _ in range(2)]
    for k in range(rows - 4):
        span = slice(k * cols, (k + 1) * cols)
        flag = upright(flags[k + 2 : k + 3, :])
        new = field[k] + (clear[span] + flag * cloud[span]).astype(bf16).astype(f32)
        field[k] = new
        add_row(means, new, k + 2)
    lane, sub = tile_iotas()
    tops = [jnp.zeros((8, LANES), f32) for _ in range(2)]
    for r in range(sea_rows):
        for k in range(sea_cols // 8):
            hit = lane == r * sea_cols + 8 * k + sub
            for q in range(2):
                at = q * (sea_feat // 2)
                value = ocean[r, 8 * k : 8 * k + 8, at : at + 1]
                tops[q] = tops[q] + jnp.where(hit, value, 0.0)
    for q, part in enumerate(means + tops):
        sums[q] = part
    half_cols = cols // 2
    cell = sublane(spots.shape)
    at = lax.broadcasted_iota(jnp.int32, spots.shape, 1) % LANES
    spots[...] = (at == cell // cols * half_cols + cell % cols // 2).astype(f32).astype(bf16)
    at = lax.broadcasted_iota(jnp.int32, cells.shape, 1) % LANES
    cells[...] = (at == sublane(cells.shape)).astype(f32).astype(bf16)
    at = lax.broadcasted_iota(jnp.int32, spread.shape, 1) // 2
    spread[...] = (at == sublane(spread.shape) % half_cols).astype(f32).astype(bf16)
    count = secs * tiles
    me = lax.axis_index("sec") * tiles + lax.axis_index("tile")
    row = sublane((count, LANES))
    row_t = row % tiles
    under = jnp.zeros((count, LANES), jnp.int32)
    map_copy.wait()
    for k in range(tiles):
        under = jnp.where(row_t == k, place[k], under)
    under = row - row_t + under
    source[...] = (under == me).astype(f32)
    at = lax.broadcasted_iota(jnp.int32, perm.shape, 1) % count
    perm[...] = (at == under[:, 0:1]).astype(f32).astype(bf16)


def border(
    secs, tiles, atmos, cloudy, w_in, w_out, c_in, c_out, tile_a, tile_b, sec_b, sec_a, sums,
    field, pay, xs, hid,
):
    rows, cols, feat = atmos.shape
    s = lax.axis_index("sec")
    sides = Sides(tiles, rows, feat, tile_a, tile_b)
    ends = Ends(secs, cols, feat, sums.shape[2] // (rows // 2), sec_a, sec_b)
    inside = columns_inside(tiles, (cols + 16, feat))

    def line(r):
        if 0 <= r < rows:
            core, side = atmos[r], sides.air(r)
        else:
            piece = ends.north if r < 0 else ends.south
            core = ends.air(piece, r + ASTEPS if r < 0 else r - rows)
            side = ends.air_side(piece)
        return jnp.concatenate([side, core, side], axis=0)

    at = 0
    for first in (0, rows - 2):
        lines = [line(r) for r in range(first - 2, first + 4)]
        ones = [jnp.where(inside, relax(*lines[k : k + 3], kappa_air), 0.0) for k in range(4)]
        if first == 0:
            ones[0] = jnp.where(s > 0, ones[0], 0.0)
        else:
            ones[3] = jnp.where(s < secs - 1, ones[3], 0.0)
        for k in range(2):
            two = relax(*ones[k : k + 3], kappa_air)[8 : 8 + cols]
            field[at] = two
            xs[at * cols : (at + 1) * cols, :] = two.astype(bf16)
            at += 1
    clear, cloud = physics(xs[...], w_in, w_out, c_in, c_out, hid)
    flags = cloudy[...].astype(f32)
    means = [sums[0], sums[1]]
    for at, r in enumerate((0, 1, rows - 2, rows - 1)):
        span = slice(at * cols, (at + 1) * cols)
        flag = upright(flags[r : r + 1, :])
        new = field[at] + (clear[span] + flag * cloud[span]).astype(bf16).astype(f32)
        field[at] = new
        add_row(means, new, r)
    for q, part in enumerate((0.25 * means[0], 0.25 * means[1], sums[2], sums[3])):
        total = jnp.sum(part, axis=0, keepdims=True)
        pay[:, q, :] = jnp.broadcast_to(total, (pay.shape[0], LANES))


def sea_steps(secs, tiles, rows, cols, feat, ocean, tile_a, tile_b, sec_b, sec_a, out):
    sea_rows, sea_cols, sea_feat = ocean.shape
    s = lax.axis_index("sec")
    sides = Sides(tiles, rows, feat, tile_a, tile_b)
    ends = Ends(secs, cols, feat, sea_cols, sec_a, sec_b)
    inside = columns_inside(tiles, (sea_cols + 16, sea_feat))
    state = []
    for r in range(-OSTEPS, sea_rows + OSTEPS):
        if 0 <= r < sea_rows:
            core, side = ocean[r], sides.sea(r)
        elif r < 0:
            core, side = ends.sea(ends.north, r + OSTEPS)
        else:
            core, side = ends.sea(ends.south, r - sea_rows)
        state.append(jnp.concatenate([side, core, side], axis=0))
    for step in range(OSTEPS):
        state = [relax(*state[k : k + 3], kappa_sea) for k in range(len(state) - 2)]
        depth = OSTEPS - 1 - step
        for k, new in enumerate(state):
            new = jnp.where(inside, new, 0.0)
            if k < depth:
                new = jnp.where(s > 0, new, 0.0)
            elif k >= depth + sea_rows:
                new = jnp.where(s < secs - 1, new, 0.0)
            state[k] = new
    for r in range(sea_rows):
        out[r] = state[r][8 : 8 + sea_cols]


def fetch(*refs):
    count = (len(refs) - 2) // 2
    sems = refs[-1]
    copies = [
        pltpu.make_async_copy(refs[1 + k], refs[1 + count + k], sems.at[k]) for k in range(count)
    ]
    for copy in copies:
        copy.start()
    for copy in copies:
        copy.wait()


def thirds(v, axis):
    high = v.astype(bf16)
    rest = v - high.astype(f32)
    middle = rest.astype(bf16)
    low = (rest - middle.astype(f32)).astype(bf16)
    return jnp.concatenate([high, middle, low], axis=axis)


def final(
    secs, tiles, gathered, perm, source, spots, cells, spread, inner_rows, border_rows,
    ocean, tile_a, tile_b, sec_b, sec_a,
    air_out, sea_out, back, stage, sea, sea_stage, back_stage, sems,
):
    rows, cols, feat = air_out.shape
    sea_rows, sea_cols, sea_feat = sea.shape
    count = secs * tiles
    me = lax.axis_index("sec") * tiles + lax.axis_index("tile")
    halves = feat // LANES
    half_cols = cols // 2
    top0, top1 = gathered[:, 2, :], gathered[:, 3, :]
    mine = source[...]

    def pick(mask, v):
        return jnp.sum(mask * v, axis=0, keepdims=True)

    def upright_at(line, *lanes):
        sub = sublane((LANES, 3 * LANES))
        out = jnp.zeros((LANES, 3 * LANES), f32)
        for v, at in zip(line, lanes):
            out = jnp.where(sub == at, jnp.broadcast_to(thirds(v, 1).astype(f32), out.shape), out)
        return out.astype(bf16)

    def against(one_hot, values):
        return lax.dot_general(
            one_hot, values, (((1,), (1,)), ((), ())), preferred_element_type=f32
        )

    landing = pick(mine, top0)
    patch = against(spots[...], upright_at([landing], 0))

    air = thirds(jnp.concatenate([gathered[:, 0, :], gathered[:, 1, :]], axis=1), 0)
    air = jnp.dot(perm[...], air, preferred_element_type=f32)
    state0 = top0 + 0.5 * (0.8 * (top0 - air[:, :LANES]))
    state1 = top1 + 0.5 * (0.8 * (0.5 * top0 - air[:, LANES:]))

    first_lane = lax.broadcasted_iota(jnp.int32, (cols, LANES), 1) == 0
    step_rows = 4
    copies = []
    for first in range(0, rows, step_rows):
        for r in range(first, first + step_rows):
            value = patch[(r // 2) * cols : (r // 2 + 1) * cols]
            for h in range(halves):
                lanes = slice(h * LANES, (h + 1) * LANES)
                if r < 2:
                    old = border_rows[r, :, lanes]
                elif r >= rows - 2:
                    old = border_rows[r - rows + 4, :, lanes]
                else:
                    old = inner_rows[r - 2, :, lanes]
                flux = 0.8 * ((1.0 if h == 0 else 0.5) * value - old)
                stage[r, :, lanes] = old + jnp.where(first_lane, 0.5 * flux, 0.0)
        copies.append(
            pltpu.make_async_copy(
                stage.at[first : first + step_rows],
                air_out.at[first : first + step_rows],
                sems.at[first // step_rows],
            )
        )
        copies[-1].start()

    sea_steps(secs, tiles, rows, cols, feat, ocean, tile_a, tile_b, sec_b, sec_a, sea)
    lane = lax.broadcasted_iota(jnp.int32, (count, LANES), 1)
    row = sublane((count, LANES))
    lane_c = lane % sea_cols
    first_c, last_c = lane_c == 0, lane_c == sea_cols - 1
    first_r, last_r = lane < sea_cols, lane >= LANES - sea_cols
    first_t, last_t = row % tiles == 0, row % tiles == tiles - 1
    first_s, last_s = row < tiles, row >= count - tiles

    def roll(v, shift, axis):
        return pltpu.roll(v, shift % v.shape[axis], axis)

    def step(v):
        east_t = jnp.where(last_t, 0.0, roll(v, -1, 0))
        west_t = jnp.where(first_t, 0.0, roll(v, 1, 0))
        east = jnp.where(last_c, roll(east_t, sea_cols - 1, 1), roll(v, -1, 1))
        west = jnp.where(first_c, roll(west_t, 1 - sea_cols, 1), roll(v, 1, 1))
        down, up = roll(v, -sea_cols, 1), roll(v, sea_cols, 1)
        down_s = jnp.where(last_s, 0.0, roll(down, -tiles, 0))
        up_s = jnp.where(first_s, 0.0, roll(up, tiles, 0))
        beside = jnp.where(last_r, down_s, down) + jnp.where(first_r, up_s, up) + east + west
        return v + kappa_sea * (beside - 4.0 * v)

    for _ in range(OSTEPS):
        state0, state1 = step(state0), step(state1)
    from_me = (row == me).astype(f32)
    own = upright_at([pick(from_me, state0), pick(from_me, state1)], 0, sea_feat // 2)
    own = against(cells[...], own)
    lane_s = lax.broadcasted_iota(jnp.int32, (sea_cols, sea_feat), 1)
    surface = jnp.logical_or(lane_s == 0, lane_s == sea_feat // 2)
    for r in range(sea_rows):
        new = own[r * sea_cols : (r + 1) * sea_cols]
        sea_stage[r] = jnp.where(surface, new, sea[r])
    copies.append(pltpu.make_async_copy(sea_stage, sea_out, sems.at[rows // step_rows]))
    copies[-1].start()

    returned = jnp.broadcast_to(pick(mine, state0), (rows, LANES))
    lane_b = lax.broadcasted_iota(jnp.int32, (rows, LANES), 1)
    lines = jnp.where(lane_b // half_cols == sublane((rows, LANES)) // 2, returned, 0.0)
    back_stage[...] = jnp.dot(thirds(lines, 1), spread[...], preferred_element_type=f32)
    copies.append(pltpu.make_async_copy(back_stage, back, sems.at[rows // step_rows + 1]))
    copies[-1].start()
    for copy in copies:
        copy.wait()


def local(atmos, cloudy, weight_in, weight_out, cloud_in, cloud_out, ocean, tile_map):
    rows, cols, feat = atmos.shape
    sea_rows, sea_cols, sea_feat = ocean.shape
    secs, tiles = lax.axis_size("sec"), lax.axis_size("tile")
    count = secs * tiles
    halves = feat // LANES
    width = weight_in.shape[1]
    sec_even, sec_odd, tile_even, tile_odd = exchanges(secs, tiles)
    shape = jax.ShapeDtypeStruct

    def call(body, name, out_shape, in_specs, out_specs, scratch=(), flops=0, args=()):
        return pl.pallas_call(
            body,
            out_shape=out_shape,
            in_specs=in_specs,
            out_specs=out_specs,
            scratch_shapes=scratch,
            compiler_params=pltpu.CompilerParams(vmem_limit_bytes=8 * 1024 * 1024),
            cost_estimate=pl.CostEstimate(flops=flops, bytes_accessed=0, transcendentals=0),
            name=name,
        )(*args)

    def hbm(a):
        return pltpu.with_memory_space_constraint(a, pltpu.HBM)

    out = shape((8 * (rows // 4 * halves + sea_rows // 2), LANES), bf16)
    send_a, send_b = call(
        pack_tile, "pack_tile", (out, out), [HBM] * 2, (VMEM, VMEM),
        [
            pltpu.VMEM((rows, 8, feat), f32),
            pltpu.VMEM((rows, 8, feat), f32),
            pltpu.VMEM(ocean.shape, f32),
            pltpu.SemaphoreType.DMA((3,)),
        ],
        args=(hbm(atmos), hbm(ocean)),
    )
    tile_a = lax.ppermute(send_a, AXES, tile_even)
    tile_b = lax.ppermute(send_b, AXES, tile_odd)
    wanted = (weight_in, cloud_in, weight_out, cloud_out, atmos, ocean, cloudy)
    weight_in, cloud_in, weight_out, cloud_out, atmos, ocean, cloudy = call(
        fetch, "fetch",
        tuple(pltpu.VMEM(a.shape, a.dtype) for a in wanted),
        [pl.BlockSpec(memory_space=pl.ANY)] + [HBM] * len(wanted),
        (VMEM,) * len(wanted),
        [pltpu.SemaphoreType.DMA((len(wanted),))],
        flops=1 << 30,
        args=(send_a, *(hbm(a) for a in wanted)),
    )

    lines = halves * (ASTEPS * cols + 8) + OSTEPS * (sea_cols + 8)
    out = shape((lines, LANES), bf16)
    send_a, send_b = call(
        functools.partial(pack_sec, tiles), "pack_sec", (out, out), [VMEM] * 4, (VMEM, VMEM),
        args=(atmos, ocean, tile_a, tile_b),
    )
    sec_a = lax.ppermute(send_a, AXES, sec_even)
    sec_b = lax.ppermute(send_b, AXES, sec_odd)

    weights = (weight_in, weight_out, cloud_in, cloud_out)
    within = (rows - 4) * cols
    inner_rows, sums, *plan = call(
        functools.partial(inner, secs, tiles), "inner",
        (
            shape((rows - 4, cols, feat), f32),
            shape((4, 8, LANES), f32),
            shape((count, 3 * count), bf16),
            shape((count, LANES), f32),
            shape((rows // 2 * cols, 3 * LANES), bf16),
            shape((LANES, 3 * LANES), bf16),
            shape((3 * LANES, cols), bf16),
        ),
        [HBM] + [VMEM] * 9,
        (VMEM,) * 7,
        [
            pltpu.VMEM((within, feat), bf16),
            pltpu.VMEM((2, within, width), bf16),
            pltpu.SMEM(tile_map.shape, jnp.int32),
            pltpu.SemaphoreType.DMA,
        ],
        flops=within * feat * width * 8,
        args=(hbm(tile_map), atmos, cloudy, *weights, ocean, tile_a, tile_b),
    )
    border_rows, pay = call(
        functools.partial(border, secs, tiles), "border",
        (shape((4, cols, feat), f32), shape((count, 4, LANES), f32)),
        [VMEM] * 11,
        (VMEM,) * 2,
        [pltpu.VMEM((4 * cols, feat), bf16), pltpu.VMEM((2, 4 * cols, width), bf16)],
        flops=4 * cols * feat * width * 8,
        args=(atmos, cloudy, *weights, tile_a, tile_b, sec_b, sec_a, sums),
    )
    gathered = lax.all_to_all(pay, AXES, 0, 0)
    return call(
        functools.partial(final, secs, tiles), "final",
        (shape(atmos.shape, f32), shape(ocean.shape, f32), shape((rows, cols), f32)),
        [VMEM] * 13,
        (HBM,) * 3,
        [
            pltpu.VMEM(atmos.shape, f32),
            pltpu.VMEM(ocean.shape, f32),
            pltpu.VMEM(ocean.shape, f32),
            pltpu.VMEM((rows, cols), f32),
            pltpu.SemaphoreType.DMA((rows // 4 + 2,)),
        ],
        args=(gathered, *plan, inner_rows, border_rows, ocean, tile_a, tile_b, sec_b, sec_a),
    )


def solution(mesh):
    placed = (
        P("sec", "tile", None),
        P("sec", "tile"),
        P(),
        P(),
        P(),
        P(),
        P("sec", "tile", None),
        P(),
    )
    return jax.shard_map(
        local,
        mesh=mesh,
        in_specs=placed,
        out_specs=(P("sec", "tile", None), P("sec", "tile", None), P("sec", "tile")),
        check_vma=False,
    )
```

```python
import functools

import jax
import jax.numpy as jnp
from jax import lax
from jax.experimental import pallas as pl
from jax.experimental.pallas import tpu as pltpu
from jax.sharding import PartitionSpec as P

ASTEPS = 2
OSTEPS = 4
LANES = 128

kappa_air = 0.2
kappa_sea = 0.2

f32 = jnp.float32
bf16 = jnp.bfloat16
VMEM = pl.BlockSpec(memory_space=pltpu.VMEM)
HBM = pl.BlockSpec(memory_space=pltpu.HBM)
AXES = ("sec", "tile")


def exchanges(secs, tiles):
    def whole(partner):
        return [
            (s * tiles + t, partner(s, t)[0] * tiles + partner(s, t)[1])
            for s in range(secs)
            for t in range(tiles)
        ]

    def odd_sec(s, t):
        if s in (0, secs - 1):
            return secs - 1 - s, t
        return (s + 1 if s % 2 else s - 1), t

    def odd_tile(s, t):
        if t in (0, tiles - 1):
            return s ^ 1, t
        return s, (t + 1 if t % 2 else t - 1)

    return (
        whole(lambda s, t: (s ^ 1, t)),
        whole(odd_sec),
        whole(lambda s, t: (s, t ^ 1)),
        whole(odd_tile),
    )


def sublane(shape):
    return lax.broadcasted_iota(jnp.int32, shape, len(shape) - 2)


def turn(v, shift):
    return v if shift % 8 == 0 else pltpu.roll(v, shift % 8, 0)


def halves_of(v):
    return [v[:, at : at + LANES] for at in range(0, v.shape[1], LANES)]


def pack_tile(atmos, ocean, out_a, out_b, west, east, sea, sems):
    rows, cols, feat = atmos.shape
    sea_rows, sea_cols, _ = ocean.shape
    copies = (
        pltpu.make_async_copy(atmos.at[:, 0:8, :], west, sems.at[0]),
        pltpu.make_async_copy(atmos.at[:, cols - 8 : cols, :], east, sems.at[1]),
        pltpu.make_async_copy(ocean, sea, sems.at[2]),
    )
    for copy in copies:
        copy.start()
    for copy in copies:
        copy.wait()
    to_west, to_east = [], []
    sub = sublane((8, feat))
    for g in range(rows // 4):
        tile_w, tile_e = west[4 * g], turn(east[4 * g], 2)
        for k in range(1, 4):
            tile_w = jnp.where(sub < 2 * k, tile_w, turn(west[4 * g + k], 2 * k))
            tile_e = jnp.where(sub < 2 * k, tile_e, turn(east[4 * g + k], 2 * k + 2))
        to_west += halves_of(tile_w)
        to_east += halves_of(tile_e)
    low = sublane((8, LANES)) < 4
    for r in range(0, sea_rows, 2):
        to_west.append(jnp.where(low, sea[r, 0:8], turn(sea[r + 1, 0:8], 4)))
        to_east.append(
            jnp.where(low, turn(sea[r, sea_cols - 8 :], 4), sea[r + 1, sea_cols - 8 :])
        )
    to_west = jnp.concatenate(to_west, axis=0).astype(bf16)
    to_east = jnp.concatenate(to_east, axis=0).astype(bf16)
    even = lax.axis_index("tile") % 2 == 0
    out_a[...] = jnp.where(even, to_east, to_west)
    out_b[...] = jnp.where(even, to_west, to_east)


class Sides:
    def __init__(self, tiles, rows, feat, tile_a, tile_b):
        t = lax.axis_index("tile")
        even = t % 2 == 0
        a, b = tile_a[...].astype(f32), tile_b[...].astype(f32)
        self.west = jnp.where(t > 0, jnp.where(even, b, a), 0.0)
        self.east = jnp.where(t < tiles - 1, jnp.where(even, a, b), 0.0)
        self.halves = feat // LANES
        self.sea_at = rows // 4 * self.halves
        self.low = sublane((8, LANES)) < 4

    def merge(self, tile, shift_w, shift_e):
        span = slice(8 * tile, 8 * tile + 8)
        return jnp.where(self.low, turn(self.east[span], shift_e), turn(self.west[span], shift_w))

    def air(self, r):
        g, k = r // 4, r % 4
        return jnp.concatenate(
            [self.merge(g * self.halves + h, -2 * k - 2, -2 * k) for h in range(self.halves)],
            axis=1,
        )

    def sea(self, r):
        return self.merge(self.sea_at + r // 2, 4 if r % 2 == 0 else 0, 4 * (r % 2))


def pack_sec(tiles, atmos, ocean, tile_a, tile_b, out_a, out_b):
    rows, cols, feat = atmos.shape
    sea_rows, sea_cols, _ = ocean.shape
    sides = Sides(tiles, rows, feat, tile_a, tile_b)

    def payload(first, corner, sea_first):
        parts = []
        for r in range(ASTEPS):
            parts += halves_of(atmos[first + r])
        parts += halves_of(sides.air(corner))
        parts += [ocean[sea_first + r] for r in range(OSTEPS)]
        parts += [sides.sea(sea_first + r) for r in range(OSTEPS)]
        return jnp.concatenate(parts, axis=0).astype(bf16)

    to_north = payload(0, 0, 0)
    to_south = payload(rows - ASTEPS, rows - 1, sea_rows - OSTEPS)
    even = lax.axis_index("sec") % 2 == 0
    out_a[...] = jnp.where(even, to_south, to_north)
    out_b[...] = jnp.where(even, to_north, to_south)


class Ends:
    def __init__(self, secs, cols, feat, sea_cols, sec_a, sec_b):
        s = lax.axis_index("sec")
        even = s % 2 == 0
        a, b = sec_a[...].astype(f32), sec_b[...].astype(f32)
        self.north = jnp.where(s > 0, jnp.where(even, b, a), 0.0)
        self.south = jnp.where(s < secs - 1, jnp.where(even, a, b), 0.0)
        self.halves, self.cols, self.sea_cols = feat // LANES, cols, sea_cols
        self.corner = ASTEPS * self.halves * cols
        self.sea_at = self.corner + 8 * self.halves
        self.side_at = self.sea_at + OSTEPS * sea_cols

    def air(self, piece, k):
        cut = [(k * self.halves + h) * self.cols for h in range(self.halves)]
        return jnp.concatenate([piece[at : at + self.cols] for at in cut], axis=1)

    def air_side(self, piece):
        cut = [self.corner + 8 * h for h in range(self.halves)]
        return jnp.concatenate([piece[at : at + 8] for at in cut], axis=1)

    def sea(self, piece, k):
        core = piece[self.sea_at + k * self.sea_cols : self.sea_at + (k + 1) * self.sea_cols]
        side = piece[self.side_at + 8 * k : self.side_at + 8 * k + 8]
        return core, side


def five(up, mid, down):
    axis = mid.ndim - 2
    return mid + up + down + (pltpu.roll(mid, 1, axis) + pltpu.roll(mid, mid.shape[axis] - 1, axis))


def on_grid(tiles, row, own):
    t = lax.axis_index("tile")
    side = row[own:]
    sub = sublane(side.shape)
    ok = ((sub >= 4) | (t < tiles - 1)) & ((sub < 4) | (t > 0))
    return jnp.concatenate([row[:own], jnp.where(ok, side, 0.0)], axis=0)


def silu(v):
    return v * (0.5 + 0.5 * jnp.tanh(0.5 * v))


def physics(x, w_in, w_out, c_in, c_out, hid):
    width = w_in.shape[1]
    block = 256
    for which, first in enumerate((w_in, c_in)):
        for j in range(0, width, block):
            h = jnp.dot(x, first[:, j : j + block], preferred_element_type=f32)
            hid[which, :, j : j + block] = silu(h).astype(bf16)
    clear = jnp.dot(hid[0], w_out[...], preferred_element_type=f32)
    cloud = jnp.dot(hid[1], c_out[...], preferred_element_type=f32)
    return clear, cloud


def upright(line):
    n = line.shape[1]
    shape = (n, n)
    eye = sublane(shape) == lax.broadcasted_iota(jnp.int32, shape, 1)
    return jnp.sum(jnp.where(eye, jnp.broadcast_to(line, shape), 0.0), axis=1, keepdims=True)


def tile_iotas():
    return lax.broadcasted_iota(jnp.int32, (8, LANES), 1), sublane((8, LANES))


def add_row(means, new, r):
    lane, sub = tile_iotas()
    cols = new.shape[0]
    for k in range(cols // 8):
        hit = lane == (r // 2) * (cols // 2) + 4 * k + sub // 2
        for q in range(2):
            value = new[8 * k : 8 * k + 8, q * LANES : q * LANES + 1]
            means[q] = means[q] + jnp.where(hit, value, 0.0)


def inner(
    secs, tiles, tile_map, atmos, cloudy, w_in, w_out, c_in, c_out, ocean, tile_a, tile_b,
    field, sums, blend, present, spots, cells, spread, xs, hid, place, place_sem,
):
    map_copy = pltpu.make_async_copy(tile_map, place, place_sem)
    map_copy.start()
    rows, cols, feat = atmos.shape
    sea_rows, sea_cols, sea_feat = ocean.shape
    sides = Sides(tiles, rows, feat, tile_a, tile_b)

    def line(r):
        return jnp.concatenate([atmos[r], sides.air(r)], axis=0)

    lines, ones = [line(0), line(1)], []
    for r in range(1, rows - 1):
        lines.append(line(r + 1))
        ones.append(on_grid(tiles, five(*lines[-3:]), cols))
        if len(ones) >= 3:
            two = kappa_air**ASTEPS * five(*ones[-3:])[:cols]
            field[r - 3] = two
            xs[(r - 3) * cols : (r - 2) * cols, :] = two.astype(bf16)
    clear, cloud = physics(xs[...], w_in, w_out, c_in, c_out, hid)
    flags = cloudy[...].astype(f32)
    means = [jnp.zeros((8, LANES), f32) for _ in range(2)]
    for k in range(rows - 4):
        span = slice(k * cols, (k + 1) * cols)
        flag = upright(flags[k + 2 : k + 3, :])
        new = field[k] + (clear[span] + flag * cloud[span]).astype(bf16).astype(f32)
        field[k] = new
        add_row(means, new, k + 2)
    lane, sub = tile_iotas()
    tops = [jnp.zeros((8, LANES), f32) for _ in range(2)]
    for r in range(sea_rows):
        for k in range(sea_cols // 8):
            hit = lane == r * sea_cols + 8 * k + sub
            for q in range(2):
                at = q * (sea_feat // 2)
                value = ocean[r, 8 * k : 8 * k + 8, at : at + 1]
                tops[q] = tops[q] + jnp.where(hit, value, 0.0)
    for q, part in enumerate(means + tops):
        sums[q] = part
    half_cols = cols // 2
    cell = sublane(spots.shape)
    at = lax.broadcasted_iota(jnp.int32, spots.shape, 1) % LANES
    spots[...] = (at == cell // cols * half_cols + cell % cols // 2).astype(f32).astype(bf16)
    at = lax.broadcasted_iota(jnp.int32, cells.shape, 1) % LANES
    cells[...] = (at == sublane(cells.shape)).astype(f32).astype(bf16)
    at = lax.broadcasted_iota(jnp.int32, spread.shape, 1) // 2
    spread[...] = (at == sublane(spread.shape) % half_cols).astype(f32).astype(bf16)
    count = secs * tiles
    s, t = lax.axis_index("sec"), lax.axis_index("tile")
    map_copy.wait()
    under = jnp.int32(0)
    for k in range(tiles):
        under = jnp.where(place[k] == t, k, under)

    def device(shape):
        row = sublane(shape)
        block, kind = row // 8, row % 8
        at_s = s + block // 3 - 1
        at_t = jnp.where(kind < 2, t, under) + block % 3 - 1
        ok = (at_s >= 0) & (at_s < secs) & (at_t >= 0) & (at_t < tiles)
        return kind, at_s * tiles, at_t, ok

    present[...] = device(present.shape)[3].astype(f32)
    shape = (blend.shape[0], blend.shape[1] // 3)
    kind, base, at_t, ok = device(shape)
    above = jnp.zeros(shape, jnp.int32)
    for k in range(tiles):
        above = jnp.where(at_t == k, place[k], above)
    column = lax.broadcasted_iota(jnp.int32, shape, 1)
    which, column = column // count, column % count
    here = jnp.where(column == base + at_t, 1.0, 0.0)
    there = jnp.where(column == base + above, 1.0, 0.0)
    top = jnp.where(kind == 1, 0.2, jnp.where(kind == 3, 1.0, 1.4))
    parts = (
        jnp.where((kind == 0) | (kind == 2), -0.4, 0.0) * there,
        jnp.where(kind == 1, -0.4, 0.0) * there,
        top * here,
        jnp.where(kind == 1, 1.0, 0.0) * here,
    )
    total = jnp.zeros(shape, f32)
    for q, part in enumerate(parts):
        total = jnp.where(which == q, part, total)
    high, low = parts_of(jnp.where(ok & (kind < 4), total, 0.0), 2)
    blend[...] = jnp.concatenate([high, high, low], axis=1)


def border(
    secs, tiles, atmos, cloudy, w_in, w_out, c_in, c_out, tile_a, tile_b, sec_b, sec_a, sums,
    field, pay, xs, hid,
):
    rows, cols, feat = atmos.shape
    s = lax.axis_index("sec")
    sides = Sides(tiles, rows, feat, tile_a, tile_b)
    ends = Ends(secs, cols, feat, sums.shape[2] // (rows // 2), sec_a, sec_b)

    def line(r):
        if 0 <= r < rows:
            core, side = atmos[r], sides.air(r)
        else:
            piece = ends.north if r < 0 else ends.south
            core = ends.air(piece, r + ASTEPS if r < 0 else r - rows)
            side = ends.air_side(piece)
        return jnp.concatenate([core, side], axis=0)

    at = 0
    for first in (0, rows - 2):
        lines = [line(r) for r in range(first - 2, first + 4)]
        ones = [on_grid(tiles, five(*lines[k : k + 3]), cols) for k in range(4)]
        if first == 0:
            ones[0] = jnp.where(s > 0, ones[0], 0.0)
        else:
            ones[3] = jnp.where(s < secs - 1, ones[3], 0.0)
        for k in range(2):
            two = kappa_air**ASTEPS * five(*ones[k : k + 3])[:cols]
            field[at] = two
            xs[at * cols : (at + 1) * cols, :] = two.astype(bf16)
            at += 1
    clear, cloud = physics(xs[...], w_in, w_out, c_in, c_out, hid)
    flags = cloudy[...].astype(f32)
    means = [sums[0], sums[1]]
    for at, r in enumerate((0, 1, rows - 2, rows - 1)):
        span = slice(at * cols, (at + 1) * cols)
        flag = upright(flags[r : r + 1, :])
        new = field[at] + (clear[span] + flag * cloud[span]).astype(bf16).astype(f32)
        field[at] = new
        add_row(means, new, r)
    for q, part in enumerate((0.25 * means[0], 0.25 * means[1], sums[2], sums[3])):
        total = jnp.sum(part, axis=0, keepdims=True)
        pay[:, q, :] = jnp.broadcast_to(total, (pay.shape[0], LANES))


def sea_steps(secs, tiles, rows, cols, feat, ocean, tile_a, tile_b, sec_b, sec_a, out):
    sea_rows, sea_cols, sea_feat = ocean.shape
    s = lax.axis_index("sec")
    sides = Sides(tiles, rows, feat, tile_a, tile_b)
    ends = Ends(secs, cols, feat, sea_cols, sec_a, sec_b)
    state = []
    for r in range(-OSTEPS, sea_rows + OSTEPS):
        if 0 <= r < sea_rows:
            core, side = ocean[r], sides.sea(r)
        elif r < 0:
            core, side = ends.sea(ends.north, r + OSTEPS)
        else:
            core, side = ends.sea(ends.south, r - sea_rows)
        state.append(jnp.concatenate([core, side], axis=0))
    for depth in reversed(range(OSTEPS)):
        state = [five(*state[k : k + 3]) for k in range(len(state) - 2)]
        if depth == 0:
            break
        for k, new in enumerate(state):
            new = on_grid(tiles, new, sea_cols)
            if k < depth:
                new = jnp.where(s > 0, new, 0.0)
            elif k >= depth + sea_rows:
                new = jnp.where(s < secs - 1, new, 0.0)
            state[k] = new
    for r in range(sea_rows):
        out[r] = kappa_sea**OSTEPS * state[r][:sea_cols]


def fetch(*refs):
    count = (len(refs) - 2) // 2
    sems = refs[-1]
    copies = [
        pltpu.make_async_copy(refs[1 + k], refs[1 + count + k], sems.at[k]) for k in range(count)
    ]
    for copy in copies:
        copy.start()
    for copy in copies:
        copy.wait()


def parts_of(v, count):
    parts = []
    for _ in range(count):
        part = v.astype(bf16)
        v = v - part.astype(f32)
        parts.append(part)
    return parts


def final(
    secs, tiles, gathered, blend, inside, spots, cells, spread, inner_rows, border_rows,
    ocean, tile_a, tile_b, sec_b, sec_a,
    air_out, sea_out, back, stage, sea, sea_stage, back_stage, sems,
):
    rows, cols, feat = air_out.shape
    sea_rows, sea_cols, sea_feat = sea.shape
    halves = feat // LANES
    half_cols = cols // 2

    def upright_at(lines, *lanes):
        first = sublane((16, LANES)) == 0
        groups = [jnp.zeros((16, 2 * LANES), bf16)] * (LANES // 16)
        for line, at in zip(lines, lanes):
            whole = jnp.where(first, jnp.broadcast_to(line, first.shape), 0.0)
            groups[at // 16] = jnp.concatenate(parts_of(whole, 2), axis=1)
        return jnp.concatenate(groups, axis=0)

    def against(one_hot, values):
        return lax.dot_general(
            one_hot, values, (((1,), (1,)), ((), ())), preferred_element_type=f32
        )

    everything = jnp.concatenate([gathered[:, q, :] for q in range(4)], axis=0)
    high, low = parts_of(everything, 2)
    blocks = jnp.dot(
        blend[...],
        jnp.concatenate([high, low, high], axis=0),
        preferred_element_type=f32,
    )
    keep = inside[...]
    blocks = {
        (k // 3, k % 3): (blocks[8 * k : 8 * k + 8], keep[8 * k : 8 * k + 8] > 0.0)
        for k in range(9)
    }
    landing = blocks[1, 1][0][3:4]
    patch = against(spots[...], upright_at([0.4 * landing], 0))
    rest = jnp.where(lax.broadcasted_iota(jnp.int32, (cols, LANES), 1) == 0, 0.6, 1.0)

    step_rows = 4
    copies = []
    for first in range(0, rows, step_rows):
        for r in range(first, first + step_rows):
            if r % 2 == 0:
                value = patch[(r // 2) * cols : (r // 2 + 1) * cols]
                added = (value, 0.5 * value)
            for h in range(halves):
                lanes = slice(h * LANES, (h + 1) * LANES)
                if r < 2:
                    old = border_rows[r, :, lanes]
                elif r >= rows - 2:
                    old = border_rows[r - rows + 4, :, lanes]
                else:
                    old = inner_rows[r - 2, :, lanes]
                stage[r, :, lanes] = old * rest + added[h]
        copies.append(
            pltpu.make_async_copy(
                stage.at[first : first + step_rows],
                air_out.at[first : first + step_rows],
                sems.at[first // step_rows],
            )
        )
        copies[-1].start()

    sea_steps(secs, tiles, rows, cols, feat, ocean, tile_a, tile_b, sec_b, sec_a, sea)
    lane = tile_iotas()[0]
    first_c, last_c = lane % sea_cols == 0, lane % sea_cols == sea_cols - 1
    first_r, last_r = lane < sea_cols, lane >= LANES - sea_cols

    def roll(v, shift):
        return pltpu.roll(v, shift % LANES, 1)

    def step(old, wanted):
        def side(at, edge, shift, cross):
            near = roll(old[at][0], shift)
            return lambda other: (
                jnp.where(edge, roll(old[other][0], cross), near) if other in old else near
            )

        new = {}
        for i, j in wanted:
            v, ok = old[i, j]
            up = side((i, j), first_r, sea_cols, sea_cols)((i - 1, j))
            down = side((i, j), last_r, -sea_cols, -sea_cols)((i + 1, j))
            west = side((i, j), first_c, 1, 1 - sea_cols)((i, j - 1))
            east = side((i, j), last_c, -1, sea_cols - 1)((i, j + 1))
            v = v + (up + down) + (west + east)
            new[i, j] = jnp.where(ok, v, 0.0), ok
        return new

    plus = [(0, 1), (1, 0), (1, 1), (1, 2), (2, 1)]
    for wanted in [list(blocks)] * (OSTEPS - 2) + [plus, [(1, 1)]]:
        blocks = step(blocks, wanted)
    mine = kappa_sea**OSTEPS * blocks[1, 1][0]
    own = upright_at([mine[0:1], mine[1:2]], 0, sea_feat // 2)
    own = against(cells[...], own)
    lane_s = lax.broadcasted_iota(jnp.int32, (sea_cols, sea_feat), 1)
    surface = jnp.logical_or(lane_s == 0, lane_s == sea_feat // 2)
    for r in range(sea_rows):
        new = own[r * sea_cols : (r + 1) * sea_cols]
        sea_stage[r] = jnp.where(surface, new, sea[r])
    copies.append(pltpu.make_async_copy(sea_stage, sea_out, sems.at[rows // step_rows]))
    copies[-1].start()

    returned = jnp.broadcast_to(mine[2:3], (rows, LANES))
    lane_b = lax.broadcasted_iota(jnp.int32, (rows, LANES), 1)
    lines = jnp.where(lane_b // half_cols == sublane((rows, LANES)) // 2, returned, 0.0)
    lines = jnp.concatenate(parts_of(lines, 2), axis=1)
    back_stage[...] = jnp.dot(lines, spread[...], preferred_element_type=f32)
    copies.append(pltpu.make_async_copy(back_stage, back, sems.at[rows // step_rows + 1]))
    copies[-1].start()
    for copy in copies:
        copy.wait()


def local(atmos, cloudy, weight_in, weight_out, cloud_in, cloud_out, ocean, tile_map):
    rows, cols, feat = atmos.shape
    sea_rows, sea_cols, sea_feat = ocean.shape
    secs, tiles = lax.axis_size("sec"), lax.axis_size("tile")
    count = secs * tiles
    halves = feat // LANES
    width = weight_in.shape[1]
    sec_even, sec_odd, tile_even, tile_odd = exchanges(secs, tiles)
    shape = jax.ShapeDtypeStruct

    def call(body, name, out_shape, in_specs, out_specs, scratch=(), flops=0, args=()):
        return pl.pallas_call(
            body,
            out_shape=out_shape,
            in_specs=in_specs,
            out_specs=out_specs,
            scratch_shapes=scratch,
            compiler_params=pltpu.CompilerParams(vmem_limit_bytes=8 * 1024 * 1024),
            cost_estimate=pl.CostEstimate(flops=flops, bytes_accessed=0, transcendentals=0),
            name=name,
        )(*args)

    def hbm(a):
        return pltpu.with_memory_space_constraint(a, pltpu.HBM)

    out = shape((8 * (rows // 4 * halves + sea_rows // 2), LANES), bf16)
    send_a, send_b = call(
        pack_tile, "pack_tile", (out, out), [HBM] * 2, (VMEM, VMEM),
        [
            pltpu.VMEM((rows, 8, feat), f32),
            pltpu.VMEM((rows, 8, feat), f32),
            pltpu.VMEM(ocean.shape, f32),
            pltpu.SemaphoreType.DMA((3,)),
        ],
        args=(hbm(atmos), hbm(ocean)),
    )
    tile_a = lax.ppermute(send_a, AXES, tile_even)
    tile_b = lax.ppermute(send_b, AXES, tile_odd)
    wanted = (weight_in, cloud_in, weight_out, cloud_out, atmos, ocean, cloudy)
    weight_in, cloud_in, weight_out, cloud_out, atmos, ocean, cloudy = call(
        fetch, "fetch",
        tuple(pltpu.VMEM(a.shape, a.dtype) for a in wanted),
        [pl.BlockSpec(memory_space=pl.ANY)] + [HBM] * len(wanted),
        (VMEM,) * len(wanted),
        [pltpu.SemaphoreType.DMA((len(wanted),))],
        flops=1 << 30,
        args=(send_a, *(hbm(a) for a in wanted)),
    )

    lines = halves * (ASTEPS * cols + 8) + OSTEPS * (sea_cols + 8)
    out = shape((lines, LANES), bf16)
    send_a, send_b = call(
        functools.partial(pack_sec, tiles), "pack_sec", (out, out), [VMEM] * 4, (VMEM, VMEM),
        args=(atmos, ocean, tile_a, tile_b),
    )
    sec_a = lax.ppermute(send_a, AXES, sec_even)
    sec_b = lax.ppermute(send_b, AXES, sec_odd)

    weights = (weight_in, weight_out, cloud_in, cloud_out)
    within = (rows - 4) * cols
    inner_rows, sums, *plan = call(
        functools.partial(inner, secs, tiles), "inner",
        (
            shape((rows - 4, cols, feat), f32),
            shape((4, 8, LANES), f32),
            shape((80, 12 * count), bf16),
            shape((72, LANES), f32),
            shape((rows // 2 * cols, 2 * LANES), bf16),
            shape((LANES, 2 * LANES), bf16),
            shape((2 * LANES, cols), bf16),
        ),
        [HBM] + [VMEM] * 9,
        (VMEM,) * 7,
        [
            pltpu.VMEM((within, feat), bf16),
            pltpu.VMEM((2, within, width), bf16),
            pltpu.SMEM(tile_map.shape, jnp.int32),
            pltpu.SemaphoreType.DMA,
        ],
        flops=within * feat * width * 8,
        args=(hbm(tile_map), atmos, cloudy, *weights, ocean, tile_a, tile_b),
    )
    border_rows, pay = call(
        functools.partial(border, secs, tiles), "border",
        (shape((4, cols, feat), f32), shape((count, 4, LANES), f32)),
        [VMEM] * 11,
        (VMEM,) * 2,
        [pltpu.VMEM((4 * cols, feat), bf16), pltpu.VMEM((2, 4 * cols, width), bf16)],
        flops=4 * cols * feat * width * 8,
        args=(atmos, cloudy, *weights, tile_a, tile_b, sec_b, sec_a, sums),
    )
    gathered = lax.all_to_all(pay, AXES, 0, 0)
    return call(
        functools.partial(final, secs, tiles), "final",
        (shape(atmos.shape, f32), shape(ocean.shape, f32), shape((rows, cols), f32)),
        [VMEM] * 13,
        (HBM,) * 3,
        [
            pltpu.VMEM(atmos.shape, f32),
            pltpu.VMEM(ocean.shape, f32),
            pltpu.VMEM(ocean.shape, f32),
            pltpu.VMEM((rows, cols), f32),
            pltpu.SemaphoreType.DMA((rows // 4 + 2,)),
        ],
        args=(gathered, *plan, inner_rows, border_rows, ocean, tile_a, tile_b, sec_b, sec_a),
    )


def solution(mesh):
    placed = (
        P("sec", "tile", None),
        P("sec", "tile"),
        P(),
        P(),
        P(),
        P(),
        P("sec", "tile", None),
        P(),
    )
    return jax.shard_map(
        local,
        mesh=mesh,
        in_specs=placed,
        out_specs=(P("sec", "tile", None), P("sec", "tile", None), P("sec", "tile")),
        check_vma=False,
    )
```

```python
import functools

import jax
import jax.numpy as jnp
from jax import lax
from jax.experimental import pallas as pl
from jax.experimental.pallas import tpu as pltpu
from jax.sharding import PartitionSpec as P

ASTEPS = 2
OSTEPS = 4
LANES = 128

kappa_air = 0.2
kappa_sea = 0.2

f32 = jnp.float32
bf16 = jnp.bfloat16
VMEM = pl.BlockSpec(memory_space=pltpu.VMEM)
HBM = pl.BlockSpec(memory_space=pltpu.HBM)
AXES = ("sec", "tile")


def exchanges(secs, tiles):
    def whole(partner):
        return [
            (s * tiles + t, partner(s, t)[0] * tiles + partner(s, t)[1])
            for s in range(secs)
            for t in range(tiles)
        ]

    def odd_sec(s, t):
        if s in (0, secs - 1):
            return secs - 1 - s, t
        return (s + 1 if s % 2 else s - 1), t

    def odd_tile(s, t):
        if t in (0, tiles - 1):
            return s ^ 1, t
        return s, (t + 1 if t % 2 else t - 1)

    return (
        whole(lambda s, t: (s ^ 1, t)),
        whole(odd_sec),
        whole(lambda s, t: (s, t ^ 1)),
        whole(odd_tile),
    )


def sublane(shape):
    return lax.broadcasted_iota(jnp.int32, shape, len(shape) - 2)


def turn(v, shift):
    return v if shift % 8 == 0 else pltpu.roll(v, shift % 8, 0)


def halves_of(v):
    return [v[:, at : at + LANES] for at in range(0, v.shape[1], LANES)]


def pack_first(atmos, ocean, out_a, out_b, rows_a, rows_b, west, east, ends, sea, sems):
    rows, cols, feat = atmos.shape
    sea_rows, sea_cols, _ = ocean.shape
    copies = (
        pltpu.make_async_copy(atmos.at[0:ASTEPS], ends.at[0], sems.at[3]),
        pltpu.make_async_copy(atmos.at[rows - ASTEPS : rows], ends.at[1], sems.at[4]),
        pltpu.make_async_copy(atmos.at[:, 0:8, :], west, sems.at[0]),
        pltpu.make_async_copy(atmos.at[:, cols - 8 : cols, :], east, sems.at[1]),
        pltpu.make_async_copy(ocean, sea, sems.at[2]),
    )
    for copy in copies:
        copy.start()
    for copy in copies:
        copy.wait()
    to_west, to_east = [], []
    sub = sublane((8, feat))
    for g in range(rows // 4):
        tile_w, tile_e = west[4 * g], turn(east[4 * g], 2)
        for k in range(1, 4):
            tile_w = jnp.where(sub < 2 * k, tile_w, turn(west[4 * g + k], 2 * k))
            tile_e = jnp.where(sub < 2 * k, tile_e, turn(east[4 * g + k], 2 * k + 2))
        to_west += halves_of(tile_w)
        to_east += halves_of(tile_e)
    low = sublane((8, LANES)) < 4
    for r in range(0, sea_rows, 2):
        to_west.append(jnp.where(low, sea[r, 0:8], turn(sea[r + 1, 0:8], 4)))
        to_east.append(
            jnp.where(low, turn(sea[r, sea_cols - 8 :], 4), sea[r + 1, sea_cols - 8 :])
        )
    to_west = jnp.concatenate(to_west, axis=0).astype(bf16)
    to_east = jnp.concatenate(to_east, axis=0).astype(bf16)
    even = lax.axis_index("tile") % 2 == 0
    out_a[...] = jnp.where(even, to_east, to_west)
    out_b[...] = jnp.where(even, to_west, to_east)
    south = 1 - lax.axis_index("sec") % 2
    for out, end in ((rows_a, south), (rows_b, 1 - south)):
        parts = []
        for r in range(ASTEPS):
            parts += halves_of(ends[end, r])
        parts += [sea[end * (sea_rows - OSTEPS) + r] for r in range(OSTEPS)]
        out[...] = jnp.concatenate(parts, axis=0).astype(bf16)


class Sides:
    def __init__(self, tiles, rows, feat, tile_a, tile_b):
        t = lax.axis_index("tile")
        even = t % 2 == 0
        a, b = tile_a[...].astype(f32), tile_b[...].astype(f32)
        self.west = jnp.where(t > 0, jnp.where(even, b, a), 0.0)
        self.east = jnp.where(t < tiles - 1, jnp.where(even, a, b), 0.0)
        self.halves = feat // LANES
        self.sea_at = rows // 4 * self.halves
        self.low = sublane((8, LANES)) < 4

    def merge(self, tile, shift_w, shift_e):
        span = slice(8 * tile, 8 * tile + 8)
        return jnp.where(self.low, turn(self.east[span], shift_e), turn(self.west[span], shift_w))

    def air(self, r):
        g, k = r // 4, r % 4
        return jnp.concatenate(
            [self.merge(g * self.halves + h, -2 * k - 2, -2 * k) for h in range(self.halves)],
            axis=1,
        )

    def sea(self, r):
        return self.merge(self.sea_at + r // 2, 4 if r % 2 == 0 else 0, 4 * (r % 2))


def pack_sec(tiles, rows, feat, sea_rows, tile_a, tile_b, rows_a, last, out_a, out_b):
    sides = Sides(tiles, rows, feat, tile_a, tile_b)

    def corners(corner, sea_first):
        sea = [sides.sea(sea_first + r) for r in range(OSTEPS)]
        return jnp.concatenate(halves_of(sides.air(corner)) + sea, axis=0).astype(bf16)

    even = lax.axis_index("sec") % 2 == 0
    north, south = corners(0, 0), corners(rows - 1, sea_rows - OSTEPS)
    out_b[...] = jnp.where(even, north, south)
    lines = rows_a.shape[0]
    out_a[:lines, :] = rows_a[...]
    out_a[lines:, :] = jnp.where(even, south, north)


class Ends:
    def __init__(self, secs, cols, feat, sea_cols, sec_a, sec_b, sec_rows):
        s = lax.axis_index("sec")
        even = s % 2 == 0
        a = sec_a[...].astype(f32)
        b = jnp.concatenate([sec_rows[...].astype(f32), sec_b[...].astype(f32)], axis=0)
        self.north = jnp.where(s > 0, jnp.where(even, b, a), 0.0)
        self.south = jnp.where(s < secs - 1, jnp.where(even, a, b), 0.0)
        self.halves, self.cols, self.sea_cols = feat // LANES, cols, sea_cols
        self.sea_at = ASTEPS * self.halves * cols
        self.corner = self.sea_at + OSTEPS * sea_cols
        self.side_at = self.corner + 8 * self.halves

    def air(self, piece, k):
        cut = [(k * self.halves + h) * self.cols for h in range(self.halves)]
        return jnp.concatenate([piece[at : at + self.cols] for at in cut], axis=1)

    def air_side(self, piece):
        cut = [self.corner + 8 * h for h in range(self.halves)]
        return jnp.concatenate([piece[at : at + 8] for at in cut], axis=1)

    def sea(self, piece, k):
        core = piece[self.sea_at + k * self.sea_cols : self.sea_at + (k + 1) * self.sea_cols]
        side = piece[self.side_at + 8 * k : self.side_at + 8 * k + 8]
        return core, side


def five(up, mid, down):
    axis = mid.ndim - 2
    return mid + up + down + (pltpu.roll(mid, 1, axis) + pltpu.roll(mid, mid.shape[axis] - 1, axis))


def on_grid(tiles, row, own):
    t = lax.axis_index("tile")
    side = row[own:]
    sub = sublane(side.shape)
    ok = ((sub >= 4) | (t < tiles - 1)) & ((sub < 4) | (t > 0))
    return jnp.concatenate([row[:own], jnp.where(ok, side, 0.0)], axis=0)


def silu(v):
    return v * (0.5 + 0.5 * jnp.tanh(0.5 * v))


def physics(x, w_in, w_out, c_in, c_out, hid):
    width = w_in.shape[1]
    block = 256
    for which, first in enumerate((w_in, c_in)):
        for j in range(0, width, block):
            h = jnp.dot(x, first[:, j : j + block], preferred_element_type=f32)
            hid[which, :, j : j + block] = silu(h).astype(bf16)
    clear = jnp.dot(hid[0], w_out[...], preferred_element_type=f32)
    cloud = jnp.dot(hid[1], c_out[...], preferred_element_type=f32)
    return clear, cloud


def upright(line):
    n = line.shape[1]
    shape = (n, n)
    eye = sublane(shape) == lax.broadcasted_iota(jnp.int32, shape, 1)
    return jnp.sum(jnp.where(eye, jnp.broadcast_to(line, shape), 0.0), axis=1, keepdims=True)


def tile_iotas():
    return lax.broadcasted_iota(jnp.int32, (8, LANES), 1), sublane((8, LANES))


def add_row(means, new, r):
    lane, sub = tile_iotas()
    cols = new.shape[0]
    for k in range(cols // 8):
        hit = lane == (r // 2) * (cols // 2) + 4 * k + sub // 2
        for q in range(2):
            value = new[8 * k : 8 * k + 8, q * LANES : q * LANES + 1]
            means[q] = means[q] + jnp.where(hit, value, 0.0)


def plan(
    secs, tiles, cols, first, tile_map, blend, present, spots, cells, spread, place, place_sem
):
    map_copy = pltpu.make_async_copy(tile_map, place, place_sem)
    map_copy.start()
    half_cols = cols // 2
    cell = sublane(spots.shape)
    at = lax.broadcasted_iota(jnp.int32, spots.shape, 1) % LANES
    spots[...] = (at == cell // cols * half_cols + cell % cols // 2).astype(f32).astype(bf16)
    at = lax.broadcasted_iota(jnp.int32, cells.shape, 1) % LANES
    cells[...] = (at == sublane(cells.shape)).astype(f32).astype(bf16)
    at = lax.broadcasted_iota(jnp.int32, spread.shape, 1) // 2
    spread[...] = (at == sublane(spread.shape) % half_cols).astype(f32).astype(bf16)
    count = secs * tiles
    s, t = lax.axis_index("sec"), lax.axis_index("tile")
    map_copy.wait()
    under = jnp.int32(0)
    for k in range(tiles):
        under = jnp.where(place[k] == t, k, under)

    def device(shape):
        row = sublane(shape)
        block, kind = row // 8, row % 8
        at_s = s + block // 3 - 1
        at_t = jnp.where(kind < 2, t, under) + block % 3 - 1
        ok = (at_s >= 0) & (at_s < secs) & (at_t >= 0) & (at_t < tiles)
        return kind, at_s * tiles, at_t, ok

    present[...] = device(present.shape)[3].astype(f32)
    shape = (blend.shape[0], blend.shape[1] // 3)
    kind, base, at_t, ok = device(shape)
    above = jnp.zeros(shape, jnp.int32)
    for k in range(tiles):
        above = jnp.where(at_t == k, place[k], above)
    column = lax.broadcasted_iota(jnp.int32, shape, 1)
    which, column = column // count, column % count
    here = jnp.where(column == base + at_t, 1.0, 0.0)
    there = jnp.where(column == base + above, 1.0, 0.0)
    top = jnp.where(kind == 1, 0.2, jnp.where(kind == 3, 1.0, 1.4))
    parts = (
        jnp.where((kind == 0) | (kind == 2), -0.4, 0.0) * there,
        jnp.where(kind == 1, -0.4, 0.0) * there,
        top * here,
        jnp.where(kind == 1, 1.0, 0.0) * here,
    )
    total = jnp.zeros(shape, f32)
    for q, part in enumerate(parts):
        total = jnp.where(which == q, part, total)
    high, low = parts_of(jnp.where(ok & (kind < 4), total, 0.0), 2)
    blend[...] = jnp.concatenate([high, high, low], axis=1)


def inner(
    tiles, atmos, cloudy, w_in, w_out, c_in, c_out, ocean, tile_a, tile_b, field, sums, xs, hid
):
    rows, cols, feat = atmos.shape
    sea_rows, sea_cols, sea_feat = ocean.shape
    sides = Sides(tiles, rows, feat, tile_a, tile_b)

    def line(r):
        return jnp.concatenate([atmos[r], sides.air(r)], axis=0)

    lines, ones = [line(0), line(1)], []
    for r in range(1, rows - 1):
        lines.append(line(r + 1))
        ones.append(on_grid(tiles, five(*lines[-3:]), cols))
        if len(ones) >= 3:
            two = kappa_air**ASTEPS * five(*ones[-3:])[:cols]
            field[r - 3] = two
            xs[(r - 3) * cols : (r - 2) * cols, :] = two.astype(bf16)
    clear, cloud = physics(xs[...], w_in, w_out, c_in, c_out, hid)
    flags = cloudy[...].astype(f32)
    means = [jnp.zeros((8, LANES), f32) for _ in range(2)]
    for k in range(rows - 4):
        span = slice(k * cols, (k + 1) * cols)
        flag = upright(flags[k + 2 : k + 3, :])
        new = field[k] + (clear[span] + flag * cloud[span]).astype(bf16).astype(f32)
        field[k] = new
        add_row(means, new, k + 2)
    lane, sub = tile_iotas()
    tops = [jnp.zeros((8, LANES), f32) for _ in range(2)]
    for r in range(sea_rows):
        for k in range(sea_cols // 8):
            hit = lane == r * sea_cols + 8 * k + sub
            for q in range(2):
                at = q * (sea_feat // 2)
                value = ocean[r, 8 * k : 8 * k + 8, at : at + 1]
                tops[q] = tops[q] + jnp.where(hit, value, 0.0)
    for q, part in enumerate(means + tops):
        sums[q] = part


def border(
    secs, tiles, atmos, cloudy, w_in, w_out, c_in, c_out, tile_a, tile_b, sec_b, sec_a, sec_rows, sums,
    field, pay, xs, hid,
):
    rows, cols, feat = atmos.shape
    s = lax.axis_index("sec")
    sides = Sides(tiles, rows, feat, tile_a, tile_b)
    ends = Ends(secs, cols, feat, sums.shape[2] // (rows // 2), sec_a, sec_b, sec_rows)

    def line(r):
        if 0 <= r < rows:
            core, side = atmos[r], sides.air(r)
        else:
            piece = ends.north if r < 0 else ends.south
            core = ends.air(piece, r + ASTEPS if r < 0 else r - rows)
            side = ends.air_side(piece)
        return jnp.concatenate([core, side], axis=0)

    at = 0
    for first in (0, rows - 2):
        lines = [line(r) for r in range(first - 2, first + 4)]
        ones = [on_grid(tiles, five(*lines[k : k + 3]), cols) for k in range(4)]
        if first == 0:
            ones[0] = jnp.where(s > 0, ones[0], 0.0)
        else:
            ones[3] = jnp.where(s < secs - 1, ones[3], 0.0)
        for k in range(2):
            two = kappa_air**ASTEPS * five(*ones[k : k + 3])[:cols]
            field[at] = two
            xs[at * cols : (at + 1) * cols, :] = two.astype(bf16)
            at += 1
    clear, cloud = physics(xs[...], w_in, w_out, c_in, c_out, hid)
    flags = cloudy[...].astype(f32)
    means = [sums[0], sums[1]]
    for at, r in enumerate((0, 1, rows - 2, rows - 1)):
        span = slice(at * cols, (at + 1) * cols)
        flag = upright(flags[r : r + 1, :])
        new = field[at] + (clear[span] + flag * cloud[span]).astype(bf16).astype(f32)
        field[at] = new
        add_row(means, new, r)
    for q, part in enumerate((0.25 * means[0], 0.25 * means[1], sums[2], sums[3])):
        total = jnp.sum(part, axis=0, keepdims=True)
        pay[:, q, :] = jnp.broadcast_to(total, (pay.shape[0], LANES))


def sea_steps(secs, tiles, rows, cols, feat, ocean, tile_a, tile_b, sec_b, sec_a, sec_rows, out):
    sea_rows, sea_cols, sea_feat = ocean.shape
    s = lax.axis_index("sec")
    sides = Sides(tiles, rows, feat, tile_a, tile_b)
    ends = Ends(secs, cols, feat, sea_cols, sec_a, sec_b, sec_rows)
    state = []
    for r in range(-OSTEPS, sea_rows + OSTEPS):
        if 0 <= r < sea_rows:
            core, side = ocean[r], sides.sea(r)
        elif r < 0:
            core, side = ends.sea(ends.north, r + OSTEPS)
        else:
            core, side = ends.sea(ends.south, r - sea_rows)
        state.append(jnp.concatenate([core, side], axis=0))
    for depth in reversed(range(OSTEPS)):
        state = [five(*state[k : k + 3]) for k in range(len(state) - 2)]
        if depth == 0:
            break
        for k, new in enumerate(state):
            new = on_grid(tiles, new, sea_cols)
            if k < depth:
                new = jnp.where(s > 0, new, 0.0)
            elif k >= depth + sea_rows:
                new = jnp.where(s < secs - 1, new, 0.0)
            state[k] = new
    for r in range(sea_rows):
        out[r] = kappa_sea**OSTEPS * state[r][:sea_cols]


def parts_of(v, count):
    parts = []
    for _ in range(count):
        part = v.astype(bf16)
        v = v - part.astype(f32)
        parts.append(part)
    return parts


def final(
    secs, tiles, gathered, blend, inside, spots, cells, spread, inner_rows, border_rows,
    ocean, tile_a, tile_b, sec_b, sec_a, sec_rows,
    air_out, sea_out, back, stage, sea, sea_stage, back_stage, sems,
):
    rows, cols, feat = air_out.shape
    sea_rows, sea_cols, sea_feat = sea.shape
    halves = feat // LANES
    half_cols = cols // 2

    def upright_at(lines, *lanes):
        first = sublane((16, LANES)) == 0
        groups = [jnp.zeros((16, 2 * LANES), bf16)] * (LANES // 16)
        for line, at in zip(lines, lanes):
            whole = jnp.where(first, jnp.broadcast_to(line, first.shape), 0.0)
            groups[at // 16] = jnp.concatenate(parts_of(whole, 2), axis=1)
        return jnp.concatenate(groups, axis=0)

    def against(one_hot, values):
        return lax.dot_general(
            one_hot, values, (((1,), (1,)), ((), ())), preferred_element_type=f32
        )

    everything = jnp.concatenate([gathered[:, q, :] for q in range(4)], axis=0)
    high, low = parts_of(everything, 2)
    blocks = jnp.dot(
        blend[...],
        jnp.concatenate([high, low, high], axis=0),
        preferred_element_type=f32,
    )
    keep = inside[...]
    blocks = {
        (k // 3, k % 3): (blocks[8 * k : 8 * k + 8], keep[8 * k : 8 * k + 8] > 0.0)
        for k in range(9)
    }
    landing = blocks[1, 1][0][3:4]
    patch = against(spots[...], upright_at([0.4 * landing], 0))
    rest = jnp.where(lax.broadcasted_iota(jnp.int32, (cols, LANES), 1) == 0, 0.6, 1.0)

    step_rows = 4
    copies = []
    for first in range(0, rows, step_rows):
        for r in range(first, first + step_rows):
            if r % 2 == 0:
                value = patch[(r // 2) * cols : (r // 2 + 1) * cols]
                added = (value, 0.5 * value)
            for h in range(halves):
                lanes = slice(h * LANES, (h + 1) * LANES)
                if r < 2:
                    old = border_rows[r, :, lanes]
                elif r >= rows - 2:
                    old = border_rows[r - rows + 4, :, lanes]
                else:
                    old = inner_rows[r - 2, :, lanes]
                stage[r, :, lanes] = old * rest + added[h]
        copies.append(
            pltpu.make_async_copy(
                stage.at[first : first + step_rows],
                air_out.at[first : first + step_rows],
                sems.at[first // step_rows],
            )
        )
        copies[-1].start()

    sea_steps(secs, tiles, rows, cols, feat, ocean, tile_a, tile_b, sec_b, sec_a, sec_rows, sea)
    lane = tile_iotas()[0]
    first_c, last_c = lane % sea_cols == 0, lane % sea_cols == sea_cols - 1
    first_r, last_r = lane < sea_cols, lane >= LANES - sea_cols

    def roll(v, shift):
        return pltpu.roll(v, shift % LANES, 1)

    def step(old, wanted):
        def side(at, edge, shift, cross):
            near = roll(old[at][0], shift)
            return lambda other: (
                jnp.where(edge, roll(old[other][0], cross), near) if other in old else near
            )

        new = {}
        for i, j in wanted:
            v, ok = old[i, j]
            up = side((i, j), first_r, sea_cols, sea_cols)((i - 1, j))
            down = side((i, j), last_r, -sea_cols, -sea_cols)((i + 1, j))
            west = side((i, j), first_c, 1, 1 - sea_cols)((i, j - 1))
            east = side((i, j), last_c, -1, sea_cols - 1)((i, j + 1))
            v = v + (up + down) + (west + east)
            new[i, j] = jnp.where(ok, v, 0.0), ok
        return new

    plus = [(0, 1), (1, 0), (1, 1), (1, 2), (2, 1)]
    for wanted in [list(blocks)] * (OSTEPS - 2) + [plus, [(1, 1)]]:
        blocks = step(blocks, wanted)
    mine = kappa_sea**OSTEPS * blocks[1, 1][0]
    own = upright_at([mine[0:1], mine[1:2]], 0, sea_feat // 2)
    own = against(cells[...], own)
    lane_s = lax.broadcasted_iota(jnp.int32, (sea_cols, sea_feat), 1)
    surface = jnp.logical_or(lane_s == 0, lane_s == sea_feat // 2)
    for r in range(sea_rows):
        new = own[r * sea_cols : (r + 1) * sea_cols]
        sea_stage[r] = jnp.where(surface, new, sea[r])
    copies.append(pltpu.make_async_copy(sea_stage, sea_out, sems.at[rows // step_rows]))
    copies[-1].start()

    returned = jnp.broadcast_to(mine[2:3], (rows, LANES))
    lane_b = lax.broadcasted_iota(jnp.int32, (rows, LANES), 1)
    lines = jnp.where(lane_b // half_cols == sublane((rows, LANES)) // 2, returned, 0.0)
    lines = jnp.concatenate(parts_of(lines, 2), axis=1)
    back_stage[...] = jnp.dot(lines, spread[...], preferred_element_type=f32)
    copies.append(pltpu.make_async_copy(back_stage, back, sems.at[rows // step_rows + 1]))
    copies[-1].start()
    for copy in copies:
        copy.wait()


def local(atmos, cloudy, weight_in, weight_out, cloud_in, cloud_out, ocean, tile_map):
    rows, cols, feat = atmos.shape
    sea_rows, sea_cols, sea_feat = ocean.shape
    secs, tiles = lax.axis_size("sec"), lax.axis_size("tile")
    count = secs * tiles
    halves = feat // LANES
    width = weight_in.shape[1]
    sec_even, sec_odd, tile_even, tile_odd = exchanges(secs, tiles)
    shape = jax.ShapeDtypeStruct

    def call(body, name, out_shape, in_specs, out_specs, scratch=(), flops=0, args=()):
        return pl.pallas_call(
            body,
            out_shape=out_shape,
            in_specs=in_specs,
            out_specs=out_specs,
            scratch_shapes=scratch,
            compiler_params=pltpu.CompilerParams(vmem_limit_bytes=8 * 1024 * 1024),
            cost_estimate=pl.CostEstimate(flops=flops, bytes_accessed=0, transcendentals=0),
            name=name,
        )(*args)

    def hbm(a):
        return pltpu.with_memory_space_constraint(a, pltpu.HBM)

    lines = ASTEPS * halves * cols + OSTEPS * sea_cols
    out = shape((8 * (rows // 4 * halves + sea_rows // 2), LANES), bf16)
    ends = shape((lines, LANES), bf16)
    send_a, send_b, rows_a, rows_b = call(
        pack_first, "pack_first", (out, out, ends, ends),
        [HBM] * 2, (VMEM,) * 4,
        [
            pltpu.VMEM((rows, 8, feat), f32),
            pltpu.VMEM((rows, 8, feat), f32),
            pltpu.VMEM((2, ASTEPS, cols, feat), f32),
            pltpu.VMEM(ocean.shape, f32),
            pltpu.SemaphoreType.DMA((5,)),
        ],
        args=(hbm(atmos), hbm(ocean)),
    )
    tile_a = lax.ppermute(send_a, AXES, tile_even)
    tile_b = lax.ppermute(send_b, AXES, tile_odd)
    sec_rows = lax.ppermute(rows_b, AXES, sec_odd)
    planned = call(
        functools.partial(plan, secs, tiles, cols), "plan",
        (
            shape((80, 12 * count), bf16),
            shape((72, LANES), f32),
            shape((rows // 2 * cols, 2 * LANES), bf16),
            shape((LANES, 2 * LANES), bf16),
            shape((2 * LANES, cols), bf16),
        ),
        [pl.BlockSpec(memory_space=pl.ANY), HBM],
        (VMEM,) * 5,
        [pltpu.SMEM(tile_map.shape, jnp.int32), pltpu.SemaphoreType.DMA],
        flops=1 << 30,
        args=(send_a, hbm(tile_map)),
    )
    corners = 8 * (halves + OSTEPS)
    send_a, send_b = call(
        functools.partial(pack_sec, tiles, rows, feat, sea_rows), "pack_sec",
        (shape((lines + corners, LANES), bf16), shape((corners, LANES), bf16)),
        [VMEM] * 3 + [pl.BlockSpec(memory_space=pl.ANY)], (VMEM, VMEM),
        args=(tile_a, tile_b, rows_a, planned[1]),
    )
    sec_a = lax.ppermute(send_a, AXES, sec_even)
    sec_b = lax.ppermute(send_b, AXES, sec_odd)

    weights = (weight_in, weight_out, cloud_in, cloud_out)
    within = (rows - 4) * cols
    inner_rows, sums = call(
        functools.partial(inner, tiles), "inner",
        (
            shape((rows - 4, cols, feat), f32),
            shape((4, 8, LANES), f32),
        ),
        [VMEM] * 9,
        (VMEM,) * 2,
        [pltpu.VMEM((within, feat), bf16), pltpu.VMEM((2, within, width), bf16)],
        flops=within * feat * width * 8,
        args=(atmos, cloudy, *weights, ocean, tile_a, tile_b),
    )
    border_rows, pay = call(
        functools.partial(border, secs, tiles), "border",
        (shape((4, cols, feat), f32), shape((count, 4, LANES), f32)),
        [VMEM] * 12,
        (VMEM,) * 2,
        [pltpu.VMEM((4 * cols, feat), bf16), pltpu.VMEM((2, 4 * cols, width), bf16)],
        flops=4 * cols * feat * width * 8,
        args=(atmos, cloudy, *weights, tile_a, tile_b, sec_b, sec_a, sec_rows, sums),
    )
    gathered = lax.all_to_all(pay, AXES, 0, 0)
    return call(
        functools.partial(final, secs, tiles), "final",
        (shape(atmos.shape, f32), shape(ocean.shape, f32), shape((rows, cols), f32)),
        [VMEM] * 14,
        (HBM,) * 3,
        [
            pltpu.VMEM(atmos.shape, f32),
            pltpu.VMEM(ocean.shape, f32),
            pltpu.VMEM(ocean.shape, f32),
            pltpu.VMEM((rows, cols), f32),
            pltpu.SemaphoreType.DMA((rows // 4 + 2,)),
        ],
        args=(gathered, *planned, inner_rows, border_rows, ocean, tile_a, tile_b, sec_b, sec_a, sec_rows),
    )


def solution(mesh):
    placed = (
        P("sec", "tile", None),
        P("sec", "tile"),
        P(),
        P(),
        P(),
        P(),
        P("sec", "tile", None),
        P(),
    )
    return jax.shard_map(
        local,
        mesh=mesh,
        in_specs=placed,
        out_specs=(P("sec", "tile", None), P("sec", "tile", None), P("sec", "tile")),
        check_vma=False,
    )
```

```python
import functools

import jax
import jax.numpy as jnp
from jax import lax
from jax.experimental import pallas as pl
from jax.experimental.pallas import tpu as pltpu
from jax.sharding import PartitionSpec as P

ASTEPS = 2
OSTEPS = 4
LANES = 128

kappa_air = 0.2
kappa_sea = 0.2

f32 = jnp.float32
bf16 = jnp.bfloat16
VMEM = pl.BlockSpec(memory_space=pltpu.VMEM)
HBM = pl.BlockSpec(memory_space=pltpu.HBM)
AXES = ("sec", "tile")


def exchanges(secs, tiles):
    def whole(partner):
        return [
            (s * tiles + t, partner(s, t)[0] * tiles + partner(s, t)[1])
            for s in range(secs)
            for t in range(tiles)
        ]

    def odd_sec(s, t):
        if s in (0, secs - 1):
            return secs - 1 - s, t
        return (s + 1 if s % 2 else s - 1), t

    def odd_tile(s, t):
        if t in (0, tiles - 1):
            return s ^ 1, t
        return s, (t + 1 if t % 2 else t - 1)

    return (
        whole(lambda s, t: (s ^ 1, t)),
        whole(odd_sec),
        whole(lambda s, t: (s, t ^ 1)),
        whole(odd_tile),
    )


def sublane(shape):
    return lax.broadcasted_iota(jnp.int32, shape, len(shape) - 2)


def turn(v, shift):
    return v if shift % 8 == 0 else pltpu.roll(v, shift % 8, 0)


def halves_of(v):
    return [v[:, at : at + LANES] for at in range(0, v.shape[1], LANES)]


def pack_first(atmos, ocean, out_a, out_b, rows_a, rows_b, west, east, ends, sea, sems):
    rows, cols, feat = atmos.shape
    sea_rows, sea_cols, _ = ocean.shape
    copies = (
        pltpu.make_async_copy(atmos.at[0:ASTEPS], ends.at[0], sems.at[3]),
        pltpu.make_async_copy(atmos.at[rows - ASTEPS : rows], ends.at[1], sems.at[4]),
        pltpu.make_async_copy(atmos.at[:, 0:ASTEPS], west.at[:, 0:ASTEPS], sems.at[0]),
        pltpu.make_async_copy(
            atmos.at[:, cols - ASTEPS : cols], east.at[:, 8 - ASTEPS : 8], sems.at[1]
        ),
        pltpu.make_async_copy(ocean, sea, sems.at[2]),
    )
    for copy in copies:
        copy.start()
    for copy in copies:
        copy.wait()
    to_west, to_east = [], []
    sub = sublane((8, feat))
    for g in range(rows // 4):
        tile_w, tile_e = west[4 * g], turn(east[4 * g], 2)
        for k in range(1, 4):
            tile_w = jnp.where(sub < 2 * k, tile_w, turn(west[4 * g + k], 2 * k))
            tile_e = jnp.where(sub < 2 * k, tile_e, turn(east[4 * g + k], 2 * k + 2))
        to_west += halves_of(tile_w)
        to_east += halves_of(tile_e)
    low = sublane((8, LANES)) < 4
    for r in range(0, sea_rows, 2):
        to_west.append(jnp.where(low, sea[r, 0:8], turn(sea[r + 1, 0:8], 4)))
        to_east.append(
            jnp.where(low, turn(sea[r, sea_cols - 8 :], 4), sea[r + 1, sea_cols - 8 :])
        )
    to_west = jnp.concatenate(to_west, axis=0).astype(bf16)
    to_east = jnp.concatenate(to_east, axis=0).astype(bf16)
    even = lax.axis_index("tile") % 2 == 0
    out_a[...] = jnp.where(even, to_east, to_west)
    out_b[...] = jnp.where(even, to_west, to_east)
    south = 1 - lax.axis_index("sec") % 2
    for out, end in ((rows_a, south), (rows_b, 1 - south)):
        parts = []
        for r in range(ASTEPS):
            parts += halves_of(ends[end, r])
        parts += [sea[end * (sea_rows - OSTEPS) + r] for r in range(OSTEPS)]
        out[...] = jnp.concatenate(parts, axis=0).astype(bf16)


class Sides:
    def __init__(self, tiles, rows, feat, tile_a, tile_b):
        t = lax.axis_index("tile")
        even = t % 2 == 0
        a, b = tile_a[...].astype(f32), tile_b[...].astype(f32)
        self.west = jnp.where(t > 0, jnp.where(even, b, a), 0.0)
        self.east = jnp.where(t < tiles - 1, jnp.where(even, a, b), 0.0)
        self.halves = feat // LANES
        self.sea_at = rows // 4 * self.halves
        self.low = sublane((8, LANES)) < 4

    def merge(self, tile, shift_w, shift_e):
        span = slice(8 * tile, 8 * tile + 8)
        return jnp.where(self.low, turn(self.east[span], shift_e), turn(self.west[span], shift_w))

    def air(self, r):
        g, k = r // 4, r % 4
        return jnp.concatenate(
            [self.merge(g * self.halves + h, -2 * k - 2, -2 * k) for h in range(self.halves)],
            axis=1,
        )

    def sea(self, r):
        return self.merge(self.sea_at + r // 2, 4 if r % 2 == 0 else 0, 4 * (r % 2))


def pack_corners(tiles, rows, feat, sea_rows, tile_a, tile_b, last, out_a, out_b):
    sides = Sides(tiles, rows, feat, tile_a, tile_b)

    def corners(corner, sea_first):
        sea = [sides.sea(sea_first + r) for r in range(OSTEPS)]
        return jnp.concatenate(halves_of(sides.air(corner)) + sea, axis=0).astype(bf16)

    even = lax.axis_index("sec") % 2 == 0
    north, south = corners(0, 0), corners(rows - 1, sea_rows - OSTEPS)
    out_a[...] = jnp.where(even, south, north)
    out_b[...] = jnp.where(even, north, south)


def from_ends(secs, a, b):
    s = lax.axis_index("sec")
    even = s % 2 == 0
    a, b = a[...].astype(f32), b[...].astype(f32)
    north = jnp.where(s > 0, jnp.where(even, b, a), 0.0)
    south = jnp.where(s < secs - 1, jnp.where(even, a, b), 0.0)
    return north, south


def halves_beside(piece, at, count, halves):
    cut = [piece[at + h * count : at + (h + 1) * count] for h in range(halves)]
    return jnp.concatenate(cut, axis=1)


def five(up, mid, down):
    axis = mid.ndim - 2
    return mid + up + down + (pltpu.roll(mid, 1, axis) + pltpu.roll(mid, mid.shape[axis] - 1, axis))


def on_grid(tiles, row, own):
    t = lax.axis_index("tile")
    side = row[own:]
    sub = sublane(side.shape)
    ok = ((sub >= 4) | (t < tiles - 1)) & ((sub < 4) | (t > 0))
    return jnp.concatenate([row[:own], jnp.where(ok, side, 0.0)], axis=0)


def silu(v):
    return v * (0.5 + 0.5 * jnp.tanh(0.5 * v))


def physics(x, w_in, w_out, c_in, c_out, hid):
    width = w_in.shape[1]
    block = 256
    for which, first in enumerate((w_in, c_in)):
        for j in range(0, width, block):
            h = jnp.dot(x, first[:, j : j + block], preferred_element_type=f32)
            hid[which, :, j : j + block] = silu(h).astype(bf16)
    clear = jnp.dot(hid[0], w_out[...], preferred_element_type=f32)
    cloud = jnp.dot(hid[1], c_out[...], preferred_element_type=f32)
    return clear, cloud


def upright(line):
    n = line.shape[1]
    shape = (n, n)
    eye = sublane(shape) == lax.broadcasted_iota(jnp.int32, shape, 1)
    return jnp.sum(jnp.where(eye, jnp.broadcast_to(line, shape), 0.0), axis=1, keepdims=True)


def tile_iotas():
    return lax.broadcasted_iota(jnp.int32, (8, LANES), 1), sublane((8, LANES))


def add_row(means, new, r):
    lane, sub = tile_iotas()
    cols = new.shape[0]
    for k in range(cols // 8):
        hit = lane == (r // 2) * (cols // 2) + 4 * k + sub // 2
        for q in range(2):
            value = new[8 * k : 8 * k + 8, q * LANES : q * LANES + 1]
            means[q] = means[q] + jnp.where(hit, value, 0.0)


def plan(
    secs, tiles, cols, first, tile_map, blend, present, spots, cells, spread, place, place_sem
):
    map_copy = pltpu.make_async_copy(tile_map, place, place_sem)
    map_copy.start()
    half_cols = cols // 2
    cell = sublane(spots.shape)
    at = lax.broadcasted_iota(jnp.int32, spots.shape, 1) % LANES
    spots[...] = (at == cell // cols * half_cols + cell % cols // 2).astype(f32).astype(bf16)
    at = lax.broadcasted_iota(jnp.int32, cells.shape, 1) % LANES
    cells[...] = (at == sublane(cells.shape)).astype(f32).astype(bf16)
    at = lax.broadcasted_iota(jnp.int32, spread.shape, 1) // 2
    spread[...] = (at == sublane(spread.shape) % half_cols).astype(f32).astype(bf16)
    count = secs * tiles
    s, t = lax.axis_index("sec"), lax.axis_index("tile")
    map_copy.wait()
    under = jnp.int32(0)
    for k in range(tiles):
        under = jnp.where(place[k] == t, k, under)

    def device(shape):
        row = sublane(shape)
        block, kind = row // 8, row % 8
        at_s = s + block // 3 - 1
        at_t = jnp.where(kind < 2, t, under) + block % 3 - 1
        ok = (at_s >= 0) & (at_s < secs) & (at_t >= 0) & (at_t < tiles)
        return kind, at_s * tiles, at_t, ok

    present[...] = device(present.shape)[3].astype(f32)
    shape = (blend.shape[0], blend.shape[1] // 3)
    kind, base, at_t, ok = device(shape)
    above = jnp.zeros(shape, jnp.int32)
    for k in range(tiles):
        above = jnp.where(at_t == k, place[k], above)
    column = lax.broadcasted_iota(jnp.int32, shape, 1)
    which, column = column // count, column % count
    here = jnp.where(column == base + at_t, 1.0, 0.0)
    there = jnp.where(column == base + above, 1.0, 0.0)
    top = jnp.where(kind == 1, 0.2, jnp.where(kind == 3, 1.0, 1.4))
    parts = (
        jnp.where((kind == 0) | (kind == 2), -0.4, 0.0) * there,
        jnp.where(kind == 1, -0.4, 0.0) * there,
        top * here,
        jnp.where(kind == 1, 1.0, 0.0) * here,
    )
    total = jnp.zeros(shape, f32)
    for q, part in enumerate(parts):
        total = jnp.where(which == q, part, total)
    high, low = parts_of(jnp.where(ok & (kind < 4), total, 0.0), 2)
    blend[...] = jnp.concatenate([high, high, low], axis=1)


def main(
    secs, tiles, atmos, cloudy, w_in, w_out, c_in, c_out, ocean, tile_a, tile_b, rows_b, rows_a,
    field, sums, ends, xs, hid,
):
    rows, cols, feat = atmos.shape
    sea_rows, sea_cols, sea_feat = ocean.shape
    halves = feat // LANES
    s = lax.axis_index("sec")
    sides = Sides(tiles, rows, feat, tile_a, tile_b)
    north, south = from_ends(secs, rows_a, rows_b)

    def line(r):
        if 0 <= r < rows:
            return jnp.concatenate([atmos[r], sides.air(r)], axis=0)
        piece, k = (north, r + ASTEPS) if r < 0 else (south, r - rows)
        core = halves_beside(piece, k * halves * cols, cols, halves)
        return jnp.concatenate([core, jnp.zeros((8, feat), f32)], axis=0)

    lines, ones = [line(-2), line(-1)], []
    for r in range(-1, rows + 1):
        lines.append(line(r + 1))
        one = on_grid(tiles, five(*lines[-3:]), cols)
        if r == -1:
            one = jnp.where(s > 0, one, 0.0)
        if r == rows:
            one = jnp.where(s < secs - 1, one, 0.0)
        ones.append(one)
        if len(ones) >= 3:
            two = kappa_air**ASTEPS * five(*ones[-3:])[:cols]
            field[r - 1] = two
            xs[(r - 1) * cols : r * cols, :] = two.astype(bf16)
    ends[...] = jnp.zeros(ends.shape, f32)
    for k, r in enumerate((0, rows - 1)):
        ends[2 * k : 2 * k + 1, :] = field[r, 0:1, :]
        ends[2 * k + 1 : 2 * k + 2, :] = field[r, cols - 1 : cols, :]
    clear, cloud = physics(xs[...], w_in, w_out, c_in, c_out, hid)
    flags = cloudy[...].astype(f32)
    means = [jnp.zeros((8, LANES), f32) for _ in range(2)]
    for r in range(rows):
        span = slice(r * cols, (r + 1) * cols)
        flag = upright(flags[r : r + 1, :])
        new = field[r] + (clear[span] + flag * cloud[span]).astype(bf16).astype(f32)
        field[r] = new
        if r in (0, rows - 1):
            sub = sublane(new.shape)
            new = jnp.where((sub > 0) & (sub < cols - 1), new, 0.0)
        add_row(means, new, r)
    lane, sub = tile_iotas()
    tops = [jnp.zeros((8, LANES), f32) for _ in range(2)]
    for r in range(sea_rows):
        for k in range(sea_cols // 8):
            hit = lane == r * sea_cols + 8 * k + sub
            for q in range(2):
                at = q * (sea_feat // 2)
                value = ocean[r, 8 * k : 8 * k + 8, at : at + 1]
                tops[q] = tops[q] + jnp.where(hit, value, 0.0)
    for q, part in enumerate(means + tops):
        sums[q] = part


def finish(
    secs, old, cloudy, w_in, w_out, c_in, c_out, ends, corner_b, corner_a, sums,
    field, pay, hid,
):
    rows, cols, feat = field.shape
    halves = feat // LANES
    half_cols = cols // 2
    north, south = from_ends(secs, corner_a, corner_b)
    north = halves_beside(north, 0, 8, halves)
    south = halves_beside(south, 0, 8, halves)
    sub = sublane((8, feat))
    diagonal = jnp.zeros((8, feat), f32)
    for k, cell in enumerate((north[7:8], north[0:1], south[7:8], south[0:1])):
        diagonal = jnp.where(sub == k, cell, diagonal)
    state = ends[...] + 2.0 * kappa_air**ASTEPS * diagonal
    x = jnp.concatenate([state, jnp.zeros((8, feat), f32)], axis=0).astype(bf16)
    clear, cloud = physics(x, w_in, w_out, c_in, c_out, hid)
    places = ((0, 0), (0, cols - 1), (rows - 1, 0), (rows - 1, cols - 1))
    flags = cloudy[...].astype(f32)
    flag = jnp.zeros((8, feat), f32)
    lane, sub_lane = tile_iotas()
    at = jnp.zeros((8, LANES), jnp.int32)
    for k, (r, c) in enumerate(places):
        flag = jnp.where(sub == k, flags[r : r + 1, c : c + 1], flag)
        at = jnp.where(sub_lane == k, (r // 2) * half_cols + c // 2, at)
    new = state + (clear[:8] + flag * cloud[:8]).astype(bf16).astype(f32)
    for k, (r, c) in enumerate(places):
        field[r, c : c + 1, :] = new[k : k + 1]
    hit = (lane == at) & (sub_lane < 4)
    means = [
        sums[q] + jnp.where(hit, new[:, q * LANES : q * LANES + 1], 0.0) for q in range(2)
    ]
    for q, part in enumerate((0.25 * means[0], 0.25 * means[1], sums[2], sums[3])):
        total = jnp.sum(part, axis=0, keepdims=True)
        pay[:, q, :] = jnp.broadcast_to(total, (pay.shape[0], LANES))


def sea_steps(secs, tiles, rows, cols, feat, ocean, halos, out):
    sea_rows, sea_cols, sea_feat = ocean.shape
    tile_a, tile_b, rows_a, rows_b, corner_a, corner_b = halos
    s = lax.axis_index("sec")
    sides = Sides(tiles, rows, feat, tile_a, tile_b)
    cores = from_ends(secs, rows_a, rows_b)
    corners = from_ends(secs, corner_a, corner_b)
    halves = feat // LANES
    state = []
    for r in range(-OSTEPS, sea_rows + OSTEPS):
        if 0 <= r < sea_rows:
            core, side = ocean[r], sides.sea(r)
        else:
            end, k = (0, r + OSTEPS) if r < 0 else (1, r - sea_rows)
            at = ASTEPS * halves * cols + k * sea_cols
            core = cores[end][at : at + sea_cols]
            at = 8 * (halves + k)
            side = corners[end][at : at + 8]
        state.append(jnp.concatenate([core, side], axis=0))
    for depth in reversed(range(OSTEPS)):
        state = [five(*state[k : k + 3]) for k in range(len(state) - 2)]
        if depth == 0:
            break
        for k, new in enumerate(state):
            new = on_grid(tiles, new, sea_cols)
            if k < depth:
                new = jnp.where(s > 0, new, 0.0)
            elif k >= depth + sea_rows:
                new = jnp.where(s < secs - 1, new, 0.0)
            state[k] = new
    for r in range(sea_rows):
        out[r] = kappa_sea**OSTEPS * state[r][:sea_cols]


def parts_of(v, count):
    parts = []
    for _ in range(count):
        part = v.astype(bf16)
        v = v - part.astype(f32)
        parts.append(part)
    return parts


def final(
    secs, tiles, gathered, blend, inside, spots, cells, spread, field, ocean,
    tile_a, tile_b, rows_b, rows_a, corner_b, corner_a,
    air_out, sea_out, back, stage, sea, sea_stage, back_stage, sems,
):
    rows, cols, feat = air_out.shape
    sea_rows, sea_cols, sea_feat = sea.shape
    halves = feat // LANES
    half_cols = cols // 2

    def upright_at(lines, *lanes):
        first = sublane((16, LANES)) == 0
        groups = [jnp.zeros((16, 2 * LANES), bf16)] * (LANES // 16)
        for line, at in zip(lines, lanes):
            whole = jnp.where(first, jnp.broadcast_to(line, first.shape), 0.0)
            groups[at // 16] = jnp.concatenate(parts_of(whole, 2), axis=1)
        return jnp.concatenate(groups, axis=0)

    def against(one_hot, values):
        return lax.dot_general(
            one_hot, values, (((1,), (1,)), ((), ())), preferred_element_type=f32
        )

    everything = jnp.concatenate([gathered[:, q, :] for q in range(4)], axis=0)
    high, low = parts_of(everything, 2)
    blocks = jnp.dot(
        blend[...],
        jnp.concatenate([high, low, high], axis=0),
        preferred_element_type=f32,
    )
    keep = inside[...]
    blocks = {
        (k // 3, k % 3): (blocks[8 * k : 8 * k + 8], keep[8 * k : 8 * k + 8] > 0.0)
        for k in range(9)
    }
    landing = blocks[1, 1][0][3:4]
    patch = against(spots[...], upright_at([0.4 * landing], 0))
    rest = jnp.where(lax.broadcasted_iota(jnp.int32, (cols, LANES), 1) == 0, 0.6, 1.0)

    step_rows = 4
    copies = []
    for first in range(0, rows, step_rows):
        for r in range(first, first + step_rows):
            if r % 2 == 0:
                value = patch[(r // 2) * cols : (r // 2 + 1) * cols]
                added = (value, 0.5 * value)
            for h in range(halves):
                lanes = slice(h * LANES, (h + 1) * LANES)
                stage[r, :, lanes] = field[r, :, lanes] * rest + added[h]
        copies.append(
            pltpu.make_async_copy(
                stage.at[first : first + step_rows],
                air_out.at[first : first + step_rows],
                sems.at[first // step_rows],
            )
        )
        copies[-1].start()

    halos = tile_a, tile_b, rows_a, rows_b, corner_a, corner_b
    sea_steps(secs, tiles, rows, cols, feat, ocean, halos, sea)
    lane = tile_iotas()[0]
    first_c, last_c = lane % sea_cols == 0, lane % sea_cols == sea_cols - 1
    first_r, last_r = lane < sea_cols, lane >= LANES - sea_cols

    def roll(v, shift):
        return pltpu.roll(v, shift % LANES, 1)

    def step(old, wanted):
        def side(at, edge, shift, cross):
            near = roll(old[at][0], shift)
            return lambda other: (
                jnp.where(edge, roll(old[other][0], cross), near) if other in old else near
            )

        new = {}
        for i, j in wanted:
            v, ok = old[i, j]
            up = side((i, j), first_r, sea_cols, sea_cols)((i - 1, j))
            down = side((i, j), last_r, -sea_cols, -sea_cols)((i + 1, j))
            west = side((i, j), first_c, 1, 1 - sea_cols)((i, j - 1))
            east = side((i, j), last_c, -1, sea_cols - 1)((i, j + 1))
            v = v + (up + down) + (west + east)
            new[i, j] = jnp.where(ok, v, 0.0), ok
        return new

    plus = [(0, 1), (1, 0), (1, 1), (1, 2), (2, 1)]
    for wanted in [list(blocks)] * (OSTEPS - 2) + [plus, [(1, 1)]]:
        blocks = step(blocks, wanted)
    mine = kappa_sea**OSTEPS * blocks[1, 1][0]
    own = upright_at([mine[0:1], mine[1:2]], 0, sea_feat // 2)
    own = against(cells[...], own)
    lane_s = lax.broadcasted_iota(jnp.int32, (sea_cols, sea_feat), 1)
    surface = jnp.logical_or(lane_s == 0, lane_s == sea_feat // 2)
    for r in range(sea_rows):
        new = own[r * sea_cols : (r + 1) * sea_cols]
        sea_stage[r] = jnp.where(surface, new, sea[r])
    copies.append(pltpu.make_async_copy(sea_stage, sea_out, sems.at[rows // step_rows]))
    copies[-1].start()

    returned = jnp.broadcast_to(mine[2:3], (rows, LANES))
    lane_b = lax.broadcasted_iota(jnp.int32, (rows, LANES), 1)
    lines = jnp.where(lane_b // half_cols == sublane((rows, LANES)) // 2, returned, 0.0)
    lines = jnp.concatenate(parts_of(lines, 2), axis=1)
    back_stage[...] = jnp.dot(lines, spread[...], preferred_element_type=f32)
    copies.append(pltpu.make_async_copy(back_stage, back, sems.at[rows // step_rows + 1]))
    copies[-1].start()
    for copy in copies:
        copy.wait()


def local(atmos, cloudy, weight_in, weight_out, cloud_in, cloud_out, ocean, tile_map):
    rows, cols, feat = atmos.shape
    sea_rows, sea_cols, sea_feat = ocean.shape
    secs, tiles = lax.axis_size("sec"), lax.axis_size("tile")
    count = secs * tiles
    halves = feat // LANES
    width = weight_in.shape[1]
    sec_even, sec_odd, tile_even, tile_odd = exchanges(secs, tiles)
    shape = jax.ShapeDtypeStruct

    def call(
        body, name, out_shape, in_specs, out_specs, scratch=(), flops=0, args=(), aliases={}
    ):
        return pl.pallas_call(
            body,
            out_shape=out_shape,
            in_specs=in_specs,
            out_specs=out_specs,
            scratch_shapes=scratch,
            input_output_aliases=aliases,
            compiler_params=pltpu.CompilerParams(vmem_limit_bytes=8 * 1024 * 1024),
            cost_estimate=pl.CostEstimate(flops=flops, bytes_accessed=0, transcendentals=0),
            name=name,
        )(*args)

    def hbm(a):
        return pltpu.with_memory_space_constraint(a, pltpu.HBM)

    lines = ASTEPS * halves * cols + OSTEPS * sea_cols
    out = shape((8 * (rows // 4 * halves + sea_rows // 2), LANES), bf16)
    ends = shape((lines, LANES), bf16)
    send_a, send_b, ends_a, ends_b = call(
        pack_first, "pack_first", (out, out, ends, ends),
        [HBM] * 2, (VMEM,) * 4,
        [
            pltpu.VMEM((rows, 8, feat), f32),
            pltpu.VMEM((rows, 8, feat), f32),
            pltpu.VMEM((2, ASTEPS, cols, feat), f32),
            pltpu.VMEM(ocean.shape, f32),
            pltpu.SemaphoreType.DMA((5,)),
        ],
        args=(hbm(atmos), hbm(ocean)),
    )
    tile_a = lax.ppermute(send_a, AXES, tile_even)
    tile_b = lax.ppermute(send_b, AXES, tile_odd)
    rows_b = lax.ppermute(ends_b, AXES, sec_odd)
    rows_a = lax.ppermute(ends_a, AXES, sec_even)
    planned = call(
        functools.partial(plan, secs, tiles, cols), "plan",
        (
            shape((80, 12 * count), bf16),
            shape((72, LANES), f32),
            shape((rows // 2 * cols, 2 * LANES), bf16),
            shape((LANES, 2 * LANES), bf16),
            shape((2 * LANES, cols), bf16),
        ),
        [pl.BlockSpec(memory_space=pl.ANY), HBM],
        (VMEM,) * 5,
        [pltpu.SMEM(tile_map.shape, jnp.int32), pltpu.SemaphoreType.DMA],
        flops=1 << 30,
        args=(send_a, hbm(tile_map)),
    )
    out = shape((8 * (halves + OSTEPS), LANES), bf16)
    send_a, send_b = call(
        functools.partial(pack_corners, tiles, rows, feat, sea_rows), "pack_corners", (out, out),
        [VMEM] * 2 + [pl.BlockSpec(memory_space=pl.ANY)], (VMEM, VMEM),
        args=(tile_a, tile_b, planned[1]),
    )
    corner_b = lax.ppermute(send_b, AXES, sec_odd)
    corner_a = lax.ppermute(send_a, AXES, sec_even)

    weights = (weight_in, weight_out, cloud_in, cloud_out)
    field, sums, ends = call(
        functools.partial(main, secs, tiles), "main",
        (shape(atmos.shape, f32), shape((4, 8, LANES), f32), shape((8, feat), f32)),
        [VMEM] * 11,
        (VMEM,) * 3,
        [pltpu.VMEM((rows * cols, feat), bf16), pltpu.VMEM((2, rows * cols, width), bf16)],
        flops=rows * cols * feat * width * 8,
        args=(atmos, cloudy, *weights, ocean, tile_a, tile_b, rows_b, rows_a),
    )
    field, pay = call(
        functools.partial(finish, secs), "finish",
        (shape(atmos.shape, f32), shape((count, 4, LANES), f32)),
        [VMEM] * 10,
        (VMEM,) * 2,
        [pltpu.VMEM((2, 16, width), bf16)],
        flops=16 * feat * width * 8,
        args=(field, cloudy, *weights, ends, corner_b, corner_a, sums),
        aliases={0: 0},
    )
    gathered = lax.all_to_all(pay, AXES, 0, 0)
    return call(
        functools.partial(final, secs, tiles), "final",
        (shape(atmos.shape, f32), shape(ocean.shape, f32), shape((rows, cols), f32)),
        [VMEM] * 14,
        (HBM,) * 3,
        [
            pltpu.VMEM(atmos.shape, f32),
            pltpu.VMEM(ocean.shape, f32),
            pltpu.VMEM(ocean.shape, f32),
            pltpu.VMEM((rows, cols), f32),
            pltpu.SemaphoreType.DMA((rows // 4 + 2,)),
        ],
        args=(gathered, *planned, field, ocean, tile_a, tile_b, rows_b, rows_a, corner_b, corner_a),
    )


def solution(mesh):
    placed = (
        P("sec", "tile", None),
        P("sec", "tile"),
        P(),
        P(),
        P(),
        P(),
        P("sec", "tile", None),
        P(),
    )
    return jax.shard_map(
        local,
        mesh=mesh,
        in_specs=placed,
        out_specs=(P("sec", "tile", None), P("sec", "tile", None), P("sec", "tile")),
        check_vma=False,
    )
```

```python
import functools

import jax
import jax.numpy as jnp
from jax import lax
from jax.experimental import pallas as pl
from jax.experimental.pallas import tpu as pltpu
from jax.sharding import PartitionSpec as P

ASTEPS = 2
OSTEPS = 4
LANES = 128

kappa_air = 0.2
kappa_sea = 0.2

f32 = jnp.float32
bf16 = jnp.bfloat16
VMEM = pl.BlockSpec(memory_space=pltpu.VMEM)
HBM = pl.BlockSpec(memory_space=pltpu.HBM)
AXES = ("sec", "tile")


def exchanges(secs, tiles):
    def whole(partner):
        return [
            (s * tiles + t, partner(s, t)[0] * tiles + partner(s, t)[1])
            for s in range(secs)
            for t in range(tiles)
        ]

    def odd_sec(s, t):
        if s in (0, secs - 1):
            return secs - 1 - s, t
        return (s + 1 if s % 2 else s - 1), t

    def odd_tile(s, t):
        if t in (0, tiles - 1):
            return s ^ 1, t
        return s, (t + 1 if t % 2 else t - 1)

    return (
        whole(lambda s, t: (s ^ 1, t)),
        whole(odd_sec),
        whole(lambda s, t: (s, t ^ 1)),
        whole(odd_tile),
    )


def sublane(shape):
    return lax.broadcasted_iota(jnp.int32, shape, len(shape) - 2)


def turn(v, shift):
    return v if shift % 8 == 0 else pltpu.roll(v, shift % 8, 0)


def halves_of(v):
    return [v[:, at : at + LANES] for at in range(0, v.shape[1], LANES)]


def pack_first(atmos, ocean, out_a, out_b, rows_a, rows_b, west, east, ends, sea, sems):
    rows, cols, feat = atmos.shape
    sea_rows, sea_cols, _ = ocean.shape
    copies = (
        pltpu.make_async_copy(atmos.at[0:ASTEPS], ends.at[0], sems.at[3]),
        pltpu.make_async_copy(atmos.at[rows - ASTEPS : rows], ends.at[1], sems.at[4]),
        pltpu.make_async_copy(atmos.at[:, 0:ASTEPS], west.at[:, 0:ASTEPS], sems.at[0]),
        pltpu.make_async_copy(
            atmos.at[:, cols - ASTEPS : cols], east.at[:, 8 - ASTEPS : 8], sems.at[1]
        ),
        pltpu.make_async_copy(ocean, sea, sems.at[2]),
    )
    for copy in copies:
        copy.start()
    for copy in copies:
        copy.wait()
    to_west, to_east = [], []
    sub = sublane((8, feat))
    for g in range(rows // 4):
        tile_w, tile_e = west[4 * g], turn(east[4 * g], 2)
        for k in range(1, 4):
            tile_w = jnp.where(sub < 2 * k, tile_w, turn(west[4 * g + k], 2 * k))
            tile_e = jnp.where(sub < 2 * k, tile_e, turn(east[4 * g + k], 2 * k + 2))
        to_west += halves_of(tile_w)
        to_east += halves_of(tile_e)
    low = sublane((8, LANES)) < 4
    for r in range(0, sea_rows, 2):
        to_west.append(jnp.where(low, sea[r, 0:8], turn(sea[r + 1, 0:8], 4)))
        to_east.append(
            jnp.where(low, turn(sea[r, sea_cols - 8 :], 4), sea[r + 1, sea_cols - 8 :])
        )
    to_west = jnp.concatenate(to_west, axis=0).astype(bf16)
    to_east = jnp.concatenate(to_east, axis=0).astype(bf16)
    even = lax.axis_index("tile") % 2 == 0
    out_a[...] = jnp.where(even, to_east, to_west)
    out_b[...] = jnp.where(even, to_west, to_east)
    south = 1 - lax.axis_index("sec") % 2
    for out, end in ((rows_a, south), (rows_b, 1 - south)):
        parts = []
        for r in range(ASTEPS):
            parts += halves_of(ends[end, r])
        parts += [sea[end * (sea_rows - OSTEPS) + r] for r in range(OSTEPS)]
        out[...] = jnp.concatenate(parts, axis=0).astype(bf16)


class Sides:
    def __init__(self, tiles, rows, feat, tile_a, tile_b):
        t = lax.axis_index("tile")
        even = t % 2 == 0
        a, b = tile_a[...].astype(f32), tile_b[...].astype(f32)
        self.west = jnp.where(t > 0, jnp.where(even, b, a), 0.0)
        self.east = jnp.where(t < tiles - 1, jnp.where(even, a, b), 0.0)
        self.halves = feat // LANES
        self.sea_at = rows // 4 * self.halves
        self.low = sublane((8, LANES)) < 4

    def merge(self, tile, shift_w, shift_e):
        span = slice(8 * tile, 8 * tile + 8)
        return jnp.where(self.low, turn(self.east[span], shift_e), turn(self.west[span], shift_w))

    def air(self, r):
        g, k = r // 4, r % 4
        return jnp.concatenate(
            [self.merge(g * self.halves + h, -2 * k - 2, -2 * k) for h in range(self.halves)],
            axis=1,
        )

    def sea(self, r):
        return self.merge(self.sea_at + r // 2, 4 if r % 2 == 0 else 0, 4 * (r % 2))


def pack_corners(tiles, rows, feat, sea_rows, tile_a, tile_b, last, out_a, out_b):
    sides = Sides(tiles, rows, feat, tile_a, tile_b)

    def corners(corner, sea_first):
        sea = [sides.sea(sea_first + r) for r in range(OSTEPS)]
        return jnp.concatenate(halves_of(sides.air(corner)) + sea, axis=0).astype(bf16)

    even = lax.axis_index("sec") % 2 == 0
    north, south = corners(0, 0), corners(rows - 1, sea_rows - OSTEPS)
    out_a[...] = jnp.where(even, south, north)
    out_b[...] = jnp.where(even, north, south)


def from_ends(secs, a, b):
    s = lax.axis_index("sec")
    even = s % 2 == 0
    a, b = a[...].astype(f32), b[...].astype(f32)
    north = jnp.where(s > 0, jnp.where(even, b, a), 0.0)
    south = jnp.where(s < secs - 1, jnp.where(even, a, b), 0.0)
    return north, south


def halves_beside(piece, at, count, halves):
    cut = [piece[at + h * count : at + (h + 1) * count] for h in range(halves)]
    return jnp.concatenate(cut, axis=1)


def five(up, mid, down):
    axis = mid.ndim - 2
    return mid + up + down + (pltpu.roll(mid, 1, axis) + pltpu.roll(mid, mid.shape[axis] - 1, axis))


def on_grid(tiles, row, own):
    t = lax.axis_index("tile")
    side = row[own:]
    sub = sublane(side.shape)
    ok = ((sub >= 4) | (t < tiles - 1)) & ((sub < 4) | (t > 0))
    return jnp.concatenate([row[:own], jnp.where(ok, side, 0.0)], axis=0)


def silu(v):
    return v * (0.5 + 0.5 * jnp.tanh(0.5 * v))


def physics(x, w_in, w_out, c_in, c_out, hid):
    width = w_in.shape[1]
    block = 256
    for which, first in enumerate((w_in, c_in)):
        for j in range(0, width, block):
            h = jnp.dot(x, first[:, j : j + block], preferred_element_type=f32)
            hid[which, :, j : j + block] = silu(h).astype(bf16)
    clear = jnp.dot(hid[0], w_out[...], preferred_element_type=f32)
    cloud = jnp.dot(hid[1], c_out[...], preferred_element_type=f32)
    return clear, cloud


def upright(line):
    n = line.shape[1]
    shape = (n, n)
    eye = sublane(shape) == lax.broadcasted_iota(jnp.int32, shape, 1)
    return jnp.sum(jnp.where(eye, jnp.broadcast_to(line, shape), 0.0), axis=1, keepdims=True)


def tile_iotas():
    return lax.broadcasted_iota(jnp.int32, (8, LANES), 1), sublane((8, LANES))


def add_row(means, new, r):
    lane, sub = tile_iotas()
    cols = new.shape[0]
    for k in range(cols // 8):
        hit = lane == (r // 2) * (cols // 2) + 4 * k + sub // 2
        for q in range(2):
            value = new[8 * k : 8 * k + 8, q * LANES : q * LANES + 1]
            means[q] = means[q] + jnp.where(hit, value, 0.0)


def plan(
    secs, tiles, first, tile_map, cloudy, blend, present, spots, cells, spread, flags,
    place, cloudy_here, sems,
):
    map_copy = pltpu.make_async_copy(tile_map, place, sems.at[0])
    map_copy.start()
    flags_copy = pltpu.make_async_copy(cloudy, cloudy_here, sems.at[1])
    flags_copy.start()
    rows, cols = cloudy.shape
    half_cols = cols // 2
    cell = sublane(spots.shape)
    at = lax.broadcasted_iota(jnp.int32, spots.shape, 1) % LANES
    spots[...] = (at == cell // cols * half_cols + cell % cols // 2).astype(f32).astype(bf16)
    at = lax.broadcasted_iota(jnp.int32, cells.shape, 1) % LANES
    cells[...] = (at == sublane(cells.shape)).astype(f32).astype(bf16)
    at = lax.broadcasted_iota(jnp.int32, spread.shape, 1) // 2
    spread[...] = (at == sublane(spread.shape) % half_cols).astype(f32).astype(bf16)
    count = secs * tiles
    s, t = lax.axis_index("sec"), lax.axis_index("tile")
    map_copy.wait()
    under = jnp.int32(0)
    for k in range(tiles):
        under = jnp.where(place[k] == t, k, under)

    def device(shape):
        row = sublane(shape)
        block, kind = row // 8, row % 8
        at_s = s + block // 3 - 1
        at_t = jnp.where(kind < 2, t, under) + block % 3 - 1
        ok = (at_s >= 0) & (at_s < secs) & (at_t >= 0) & (at_t < tiles)
        return kind, at_s * tiles, at_t, ok

    present[...] = device(present.shape)[3].astype(f32)
    shape = (blend.shape[0], blend.shape[1] // 3)
    kind, base, at_t, ok = device(shape)
    above = jnp.zeros(shape, jnp.int32)
    for k in range(tiles):
        above = jnp.where(at_t == k, place[k], above)
    column = lax.broadcasted_iota(jnp.int32, shape, 1)
    which, column = column // count, column % count
    here = jnp.where(column == base + at_t, 1.0, 0.0)
    there = jnp.where(column == base + above, 1.0, 0.0)
    top = jnp.where(kind == 1, 0.2, jnp.where(kind == 3, 1.0, 1.4))
    parts = (
        jnp.where((kind == 0) | (kind == 2), -0.4, 0.0) * there,
        jnp.where(kind == 1, -0.4, 0.0) * there,
        top * here,
        jnp.where(kind == 1, 1.0, 0.0) * here,
    )
    total = jnp.zeros(shape, f32)
    for q, part in enumerate(parts):
        total = jnp.where(which == q, part, total)
    high, low = parts_of(jnp.where(ok & (kind < 4), total, 0.0), 2)
    blend[...] = jnp.concatenate([high, high, low], axis=1)
    flags_copy.wait()
    values = cloudy_here[...].astype(f32)
    for r in range(rows):
        flag = upright(values[r : r + 1, :])
        flags[r * cols : (r + 1) * cols, :] = jnp.broadcast_to(flag, (cols, LANES))


def main(
    secs, tiles, atmos, flags, w_in, w_out, c_in, c_out, ocean, tile_a, tile_b, rows_b, rows_a,
    field, sums, ends, xs, hid,
):
    rows, cols, feat = atmos.shape
    sea_rows, sea_cols, sea_feat = ocean.shape
    halves = feat // LANES
    s = lax.axis_index("sec")
    sides = Sides(tiles, rows, feat, tile_a, tile_b)
    north, south = from_ends(secs, rows_a, rows_b)

    def line(r):
        if 0 <= r < rows:
            return jnp.concatenate([atmos[r], sides.air(r)], axis=0)
        piece, k = (north, r + ASTEPS) if r < 0 else (south, r - rows)
        core = halves_beside(piece, k * halves * cols, cols, halves)
        return jnp.concatenate([core, jnp.zeros((8, feat), f32)], axis=0)

    lines, ones = [line(-2), line(-1)], []
    for r in range(-1, rows + 1):
        lines.append(line(r + 1))
        one = on_grid(tiles, five(*lines[-3:]), cols)
        if r == -1:
            one = jnp.where(s > 0, one, 0.0)
        if r == rows:
            one = jnp.where(s < secs - 1, one, 0.0)
        ones.append(one)
        if len(ones) >= 3:
            two = kappa_air**ASTEPS * five(*ones[-3:])[:cols]
            field[r - 1] = two
            xs[(r - 1) * cols : r * cols, :] = two.astype(bf16)
    ends[...] = jnp.zeros(ends.shape, f32)
    for k, r in enumerate((0, rows - 1)):
        ends[2 * k : 2 * k + 1, :] = field[r, 0:1, :]
        ends[2 * k + 1 : 2 * k + 2, :] = field[r, cols - 1 : cols, :]
    clear, cloud = physics(xs[...], w_in, w_out, c_in, c_out, hid)
    means = [jnp.zeros((8, LANES), f32) for _ in range(2)]
    for r in range(rows):
        span = slice(r * cols, (r + 1) * cols)
        flag = jnp.concatenate([flags[span, :]] * halves, axis=1)
        new = field[r] + (clear[span] + flag * cloud[span]).astype(bf16).astype(f32)
        field[r] = new
        if r in (0, rows - 1):
            sub = sublane(new.shape)
            new = jnp.where((sub > 0) & (sub < cols - 1), new, 0.0)
        add_row(means, new, r)
    lane, sub = tile_iotas()
    tops = [jnp.zeros((8, LANES), f32) for _ in range(2)]
    for r in range(sea_rows):
        for k in range(sea_cols // 8):
            hit = lane == r * sea_cols + 8 * k + sub
            for q in range(2):
                at = q * (sea_feat // 2)
                value = ocean[r, 8 * k : 8 * k + 8, at : at + 1]
                tops[q] = tops[q] + jnp.where(hit, value, 0.0)
    for q, part in enumerate(means + tops):
        sums[q] = part


def finish(
    secs, old, all_flags, w_in, w_out, c_in, c_out, ends, corner_b, corner_a, sums,
    field, pay, hid,
):
    rows, cols, feat = field.shape
    halves = feat // LANES
    half_cols = cols // 2
    north, south = from_ends(secs, corner_a, corner_b)
    north = halves_beside(north, 0, 8, halves)
    south = halves_beside(south, 0, 8, halves)
    sub = sublane((8, feat))
    diagonal = jnp.zeros((8, feat), f32)
    for k, cell in enumerate((north[7:8], north[0:1], south[7:8], south[0:1])):
        diagonal = jnp.where(sub == k, cell, diagonal)
    state = ends[...] + 2.0 * kappa_air**ASTEPS * diagonal
    x = jnp.concatenate([state, jnp.zeros((8, feat), f32)], axis=0).astype(bf16)
    clear, cloud = physics(x, w_in, w_out, c_in, c_out, hid)
    places = ((0, 0), (0, cols - 1), (rows - 1, 0), (rows - 1, cols - 1))
    flag = jnp.zeros((8, LANES), f32)
    lane, sub_lane = tile_iotas()
    at = jnp.zeros((8, LANES), jnp.int32)
    for k, (r, c) in enumerate(places):
        cell = r * cols + c
        flag = jnp.where(sub_lane == k, all_flags[cell : cell + 1, :], flag)
        at = jnp.where(sub_lane == k, (r // 2) * half_cols + c // 2, at)
    flag = jnp.concatenate([flag] * halves, axis=1)
    new = state + (clear[:8] + flag * cloud[:8]).astype(bf16).astype(f32)
    for k, (r, c) in enumerate(places):
        field[r, c : c + 1, :] = new[k : k + 1]
    hit = (lane == at) & (sub_lane < 4)
    means = [
        sums[q] + jnp.where(hit, new[:, q * LANES : q * LANES + 1], 0.0) for q in range(2)
    ]
    parts = (0.25 * means[0], 0.25 * means[1], sums[2], sums[3])
    total = jnp.concatenate([jnp.sum(part, axis=0, keepdims=True) for part in parts], axis=0)
    pay[...] = jnp.broadcast_to(total[None], pay.shape)


def sea_steps(secs, tiles, rows, cols, feat, ocean, halos, out):
    sea_rows, sea_cols, sea_feat = ocean.shape
    tile_a, tile_b, rows_a, rows_b, corner_a, corner_b = halos
    s = lax.axis_index("sec")
    sides = Sides(tiles, rows, feat, tile_a, tile_b)
    cores = from_ends(secs, rows_a, rows_b)
    corners = from_ends(secs, corner_a, corner_b)
    halves = feat // LANES
    state = []
    for r in range(-OSTEPS, sea_rows + OSTEPS):
        if 0 <= r < sea_rows:
            core, side = ocean[r], sides.sea(r)
        else:
            end, k = (0, r + OSTEPS) if r < 0 else (1, r - sea_rows)
            at = ASTEPS * halves * cols + k * sea_cols
            core = cores[end][at : at + sea_cols]
            at = 8 * (halves + k)
            side = corners[end][at : at + 8]
        state.append(jnp.concatenate([core, side], axis=0))
    for depth in reversed(range(OSTEPS)):
        state = [five(*state[k : k + 3]) for k in range(len(state) - 2)]
        if depth == 0:
            break
        for k, new in enumerate(state):
            new = on_grid(tiles, new, sea_cols)
            if k < depth:
                new = jnp.where(s > 0, new, 0.0)
            elif k >= depth + sea_rows:
                new = jnp.where(s < secs - 1, new, 0.0)
            state[k] = new
    for r in range(sea_rows):
        out[r] = kappa_sea**OSTEPS * state[r][:sea_cols]


def parts_of(v, count):
    parts = []
    for _ in range(count):
        part = v.astype(bf16)
        v = v - part.astype(f32)
        parts.append(part)
    return parts


def final(
    secs, tiles, gathered, blend, inside, spots, cells, spread, field, ocean,
    tile_a, tile_b, rows_b, rows_a, corner_b, corner_a,
    air_out, sea_out, back, stage, sea, sea_stage, back_stage, sems,
):
    rows, cols, feat = air_out.shape
    sea_rows, sea_cols, sea_feat = sea.shape
    halves = feat // LANES
    half_cols = cols // 2

    def upright_at(lines, *lanes):
        first = sublane((16, LANES)) == 0
        groups = [jnp.zeros((16, 2 * LANES), bf16)] * (LANES // 16)
        for line, at in zip(lines, lanes):
            whole = jnp.where(first, jnp.broadcast_to(line, first.shape), 0.0)
            groups[at // 16] = jnp.concatenate(parts_of(whole, 2), axis=1)
        return jnp.concatenate(groups, axis=0)

    def against(one_hot, values):
        return lax.dot_general(
            one_hot, values, (((1,), (1,)), ((), ())), preferred_element_type=f32
        )

    everything = jnp.concatenate([gathered[:, q, :] for q in range(4)], axis=0)
    high, low = parts_of(everything, 2)
    blocks = jnp.dot(
        blend[...],
        jnp.concatenate([high, low, high], axis=0),
        preferred_element_type=f32,
    )
    keep = inside[...]
    blocks = {
        (k // 3, k % 3): (blocks[8 * k : 8 * k + 8], keep[8 * k : 8 * k + 8] > 0.0)
        for k in range(9)
    }
    landing = blocks[1, 1][0][3:4]
    patch = against(spots[...], upright_at([0.4 * landing], 0))
    rest = jnp.where(lax.broadcasted_iota(jnp.int32, (cols, LANES), 1) == 0, 0.6, 1.0)

    step_rows = 4
    copies = []
    for first in range(0, rows, step_rows):
        for r in range(first, first + step_rows):
            if r % 2 == 0:
                value = patch[(r // 2) * cols : (r // 2 + 1) * cols]
                added = (value, 0.5 * value)
            for h in range(halves):
                lanes = slice(h * LANES, (h + 1) * LANES)
                stage[r, :, lanes] = field[r, :, lanes] * rest + added[h]
        copies.append(
            pltpu.make_async_copy(
                stage.at[first : first + step_rows],
                air_out.at[first : first + step_rows],
                sems.at[first // step_rows],
            )
        )
        copies[-1].start()

    halos = tile_a, tile_b, rows_a, rows_b, corner_a, corner_b
    sea_steps(secs, tiles, rows, cols, feat, ocean, halos, sea)
    lane = tile_iotas()[0]
    first_c, last_c = lane % sea_cols == 0, lane % sea_cols == sea_cols - 1
    first_r, last_r = lane < sea_cols, lane >= LANES - sea_cols

    def roll(v, shift):
        return pltpu.roll(v, shift % LANES, 1)

    def step(old, wanted):
        def side(at, edge, shift, cross):
            near = roll(old[at][0], shift)
            return lambda other: (
                jnp.where(edge, roll(old[other][0], cross), near) if other in old else near
            )

        new = {}
        for i, j in wanted:
            v, ok = old[i, j]
            up = side((i, j), first_r, sea_cols, sea_cols)((i - 1, j))
            down = side((i, j), last_r, -sea_cols, -sea_cols)((i + 1, j))
            west = side((i, j), first_c, 1, 1 - sea_cols)((i, j - 1))
            east = side((i, j), last_c, -1, sea_cols - 1)((i, j + 1))
            v = v + (up + down) + (west + east)
            new[i, j] = jnp.where(ok, v, 0.0), ok
        return new

    plus = [(0, 1), (1, 0), (1, 1), (1, 2), (2, 1)]
    for wanted in [list(blocks)] * (OSTEPS - 2) + [plus, [(1, 1)]]:
        blocks = step(blocks, wanted)
    mine = kappa_sea**OSTEPS * blocks[1, 1][0]
    own = upright_at([mine[0:1], mine[1:2]], 0, sea_feat // 2)
    own = against(cells[...], own)
    lane_s = lax.broadcasted_iota(jnp.int32, (sea_cols, sea_feat), 1)
    surface = jnp.logical_or(lane_s == 0, lane_s == sea_feat // 2)
    for r in range(sea_rows):
        new = own[r * sea_cols : (r + 1) * sea_cols]
        sea_stage[r] = jnp.where(surface, new, sea[r])
    copies.append(pltpu.make_async_copy(sea_stage, sea_out, sems.at[rows // step_rows]))
    copies[-1].start()

    returned = jnp.broadcast_to(mine[2:3], (rows, LANES))
    lane_b = lax.broadcasted_iota(jnp.int32, (rows, LANES), 1)
    lines = jnp.where(lane_b // half_cols == sublane((rows, LANES)) // 2, returned, 0.0)
    lines = jnp.concatenate(parts_of(lines, 2), axis=1)
    back_stage[...] = jnp.dot(lines, spread[...], preferred_element_type=f32)
    copies.append(pltpu.make_async_copy(back_stage, back, sems.at[rows // step_rows + 1]))
    copies[-1].start()
    for copy in copies:
        copy.wait()


def local(atmos, cloudy, weight_in, weight_out, cloud_in, cloud_out, ocean, tile_map):
    rows, cols, feat = atmos.shape
    sea_rows, sea_cols, sea_feat = ocean.shape
    secs, tiles = lax.axis_size("sec"), lax.axis_size("tile")
    count = secs * tiles
    halves = feat // LANES
    width = weight_in.shape[1]
    sec_even, sec_odd, tile_even, tile_odd = exchanges(secs, tiles)
    shape = jax.ShapeDtypeStruct

    def call(
        body, name, out_shape, in_specs, out_specs, scratch=(), flops=0, args=(), aliases={}
    ):
        return pl.pallas_call(
            body,
            out_shape=out_shape,
            in_specs=in_specs,
            out_specs=out_specs,
            scratch_shapes=scratch,
            input_output_aliases=aliases,
            compiler_params=pltpu.CompilerParams(vmem_limit_bytes=8 * 1024 * 1024),
            cost_estimate=pl.CostEstimate(flops=flops, bytes_accessed=0, transcendentals=0),
            name=name,
        )(*args)

    def hbm(a):
        return pltpu.with_memory_space_constraint(a, pltpu.HBM)

    lines = ASTEPS * halves * cols + OSTEPS * sea_cols
    out = shape((8 * (rows // 4 * halves + sea_rows // 2), LANES), bf16)
    ends = shape((lines, LANES), bf16)
    send_a, send_b, ends_a, ends_b = call(
        pack_first, "pack_first", (out, out, ends, ends),
        [HBM] * 2, (VMEM,) * 4,
        [
            pltpu.VMEM((rows, 8, feat), f32),
            pltpu.VMEM((rows, 8, feat), f32),
            pltpu.VMEM((2, ASTEPS, cols, feat), f32),
            pltpu.VMEM(ocean.shape, f32),
            pltpu.SemaphoreType.DMA((5,)),
        ],
        args=(hbm(atmos), hbm(ocean)),
    )
    tile_a = lax.ppermute(send_a, AXES, tile_even)
    tile_b = lax.ppermute(send_b, AXES, tile_odd)
    rows_b = lax.ppermute(ends_b, AXES, sec_odd)
    rows_a = lax.ppermute(ends_a, AXES, sec_even)
    *planned, flags = call(
        functools.partial(plan, secs, tiles), "plan",
        (
            shape((80, 12 * count), bf16),
            shape((72, LANES), f32),
            shape((rows // 2 * cols, 2 * LANES), bf16),
            shape((LANES, 2 * LANES), bf16),
            shape((2 * LANES, cols), bf16),
            shape((rows * cols, LANES), f32),
        ),
        [pl.BlockSpec(memory_space=pl.ANY), HBM, HBM],
        (VMEM,) * 6,
        [
            pltpu.SMEM(tile_map.shape, jnp.int32),
            pltpu.VMEM(cloudy.shape, jnp.int32),
            pltpu.SemaphoreType.DMA((2,)),
        ],
        flops=1 << 30,
        args=(send_a, hbm(tile_map), hbm(cloudy)),
    )
    out = shape((8 * (halves + OSTEPS), LANES), bf16)
    send_a, send_b = call(
        functools.partial(pack_corners, tiles, rows, feat, sea_rows), "pack_corners", (out, out),
        [VMEM] * 2 + [pl.BlockSpec(memory_space=pl.ANY)], (VMEM, VMEM),
        args=(tile_a, tile_b, planned[1]),
    )
    corner_b = lax.ppermute(send_b, AXES, sec_odd)
    corner_a = lax.ppermute(send_a, AXES, sec_even)

    weights = (weight_in, weight_out, cloud_in, cloud_out)
    field, sums, ends = call(
        functools.partial(main, secs, tiles), "main",
        (shape(atmos.shape, f32), shape((4, 8, LANES), f32), shape((8, feat), f32)),
        [VMEM] * 11,
        (VMEM,) * 3,
        [pltpu.VMEM((rows * cols, feat), bf16), pltpu.VMEM((2, rows * cols, width), bf16)],
        flops=rows * cols * feat * width * 8,
        args=(atmos, flags, *weights, ocean, tile_a, tile_b, rows_b, rows_a),
    )
    field, pay = call(
        functools.partial(finish, secs), "finish",
        (shape(atmos.shape, f32), shape((count, 4, LANES), f32)),
        [VMEM] * 10,
        (VMEM,) * 2,
        [pltpu.VMEM((2, 16, width), bf16)],
        flops=16 * feat * width * 8,
        args=(field, flags, *weights, ends, corner_b, corner_a, sums),
        aliases={0: 0},
    )
    gathered = lax.all_to_all(pay, AXES, 0, 0)
    return call(
        functools.partial(final, secs, tiles), "final",
        (shape(atmos.shape, f32), shape(ocean.shape, f32), shape((rows, cols), f32)),
        [VMEM] * 14,
        (HBM,) * 3,
        [
            pltpu.VMEM(atmos.shape, f32),
            pltpu.VMEM(ocean.shape, f32),
            pltpu.VMEM(ocean.shape, f32),
            pltpu.VMEM((rows, cols), f32),
            pltpu.SemaphoreType.DMA((rows // 4 + 2,)),
        ],
        args=(gathered, *planned, field, ocean, tile_a, tile_b, rows_b, rows_a, corner_b, corner_a),
    )


def solution(mesh):
    placed = (
        P("sec", "tile", None),
        P("sec", "tile"),
        P(),
        P(),
        P(),
        P(),
        P("sec", "tile", None),
        P(),
    )
    return jax.shard_map(
        local,
        mesh=mesh,
        in_specs=placed,
        out_specs=(P("sec", "tile", None), P("sec", "tile", None), P("sec", "tile")),
        check_vma=False,
    )
```

```python
import functools

import jax
import jax.numpy as jnp
from jax import lax
from jax.experimental import pallas as pl
from jax.experimental.pallas import tpu as pltpu
from jax.sharding import PartitionSpec as P

ASTEPS = 2
OSTEPS = 4
LANES = 128

kappa_air = 0.2
kappa_sea = 0.2

f32 = jnp.float32
bf16 = jnp.bfloat16
VMEM = pl.BlockSpec(memory_space=pltpu.VMEM)
HBM = pl.BlockSpec(memory_space=pltpu.HBM)
AXES = ("sec", "tile")


def exchanges(secs, tiles):
    def whole(partner):
        return [
            (s * tiles + t, partner(s, t)[0] * tiles + partner(s, t)[1])
            for s in range(secs)
            for t in range(tiles)
        ]

    def odd_sec(s, t):
        if s in (0, secs - 1):
            return secs - 1 - s, t
        return (s + 1 if s % 2 else s - 1), t

    def odd_tile(s, t):
        if t in (0, tiles - 1):
            return s ^ 1, t
        return s, (t + 1 if t % 2 else t - 1)

    return (
        whole(lambda s, t: (s ^ 1, t)),
        whole(odd_sec),
        whole(lambda s, t: (s, t ^ 1)),
        whole(odd_tile),
    )


def sublane(shape):
    return lax.broadcasted_iota(jnp.int32, shape, len(shape) - 2)


def turn(v, shift):
    return v if shift % 8 == 0 else pltpu.roll(v, shift % 8, 0)


def halves_of(v):
    return [v[:, at : at + LANES] for at in range(0, v.shape[1], LANES)]


def pack_first(atmos, ocean, out_a, out_b, rows_a, rows_b, west, east, ends, sea, sems):
    rows, cols, feat = atmos.shape
    sea_rows, sea_cols, _ = ocean.shape
    copies = (
        pltpu.make_async_copy(atmos.at[0:ASTEPS], ends.at[0], sems.at[3]),
        pltpu.make_async_copy(atmos.at[rows - ASTEPS : rows], ends.at[1], sems.at[4]),
        pltpu.make_async_copy(atmos.at[:, 0:ASTEPS], west.at[:, 0:ASTEPS], sems.at[0]),
        pltpu.make_async_copy(
            atmos.at[:, cols - ASTEPS : cols], east.at[:, 8 - ASTEPS : 8], sems.at[1]
        ),
        pltpu.make_async_copy(ocean, sea, sems.at[2]),
    )
    for copy in copies:
        copy.start()
    for copy in copies:
        copy.wait()
    to_west, to_east = [], []
    sub = sublane((8, feat))
    for g in range(rows // 4):
        tile_w, tile_e = west[4 * g], turn(east[4 * g], 2)
        for k in range(1, 4):
            tile_w = jnp.where(sub < 2 * k, tile_w, turn(west[4 * g + k], 2 * k))
            tile_e = jnp.where(sub < 2 * k, tile_e, turn(east[4 * g + k], 2 * k + 2))
        to_west += halves_of(tile_w)
        to_east += halves_of(tile_e)
    low = sublane((8, LANES)) < 4
    for r in range(0, sea_rows, 2):
        to_west.append(jnp.where(low, sea[r, 0:8], turn(sea[r + 1, 0:8], 4)))
        to_east.append(
            jnp.where(low, turn(sea[r, sea_cols - 8 :], 4), sea[r + 1, sea_cols - 8 :])
        )
    to_west = jnp.concatenate(to_west, axis=0).astype(bf16)
    to_east = jnp.concatenate(to_east, axis=0).astype(bf16)
    even = lax.axis_index("tile") % 2 == 0
    out_a[...] = jnp.where(even, to_east, to_west)
    out_b[...] = jnp.where(even, to_west, to_east)
    south = 1 - lax.axis_index("sec") % 2
    for out, end in ((rows_a, south), (rows_b, 1 - south)):
        parts = []
        for r in range(ASTEPS):
            parts += halves_of(ends[end, r])
        parts += [sea[end * (sea_rows - OSTEPS) + r] for r in range(OSTEPS)]
        out[...] = jnp.concatenate(parts, axis=0).astype(bf16)


class Sides:
    def __init__(self, tiles, rows, feat, tile_a, tile_b):
        t = lax.axis_index("tile")
        even = t % 2 == 0
        a, b = tile_a[...].astype(f32), tile_b[...].astype(f32)
        self.west = jnp.where(t > 0, jnp.where(even, b, a), 0.0)
        self.east = jnp.where(t < tiles - 1, jnp.where(even, a, b), 0.0)
        self.halves = feat // LANES
        self.sea_at = rows // 4 * self.halves
        self.low = sublane((8, LANES)) < 4

    def merge(self, tile, shift_w, shift_e):
        span = slice(8 * tile, 8 * tile + 8)
        return jnp.where(self.low, turn(self.east[span], shift_e), turn(self.west[span], shift_w))

    def air(self, r):
        g, k = r // 4, r % 4
        return jnp.concatenate(
            [self.merge(g * self.halves + h, -2 * k - 2, -2 * k) for h in range(self.halves)],
            axis=1,
        )

    def sea(self, r):
        return self.merge(self.sea_at + r // 2, 4 if r % 2 == 0 else 0, 4 * (r % 2))


def pack_corners(tiles, rows, feat, sea_rows, tile_a, tile_b, last, out_a, out_b):
    sides = Sides(tiles, rows, feat, tile_a, tile_b)

    def corners(corner, sea_first):
        sea = [sides.sea(sea_first + r) for r in range(OSTEPS)]
        return jnp.concatenate(halves_of(sides.air(corner)) + sea, axis=0).astype(bf16)

    even = lax.axis_index("sec") % 2 == 0
    north, south = corners(0, 0), corners(rows - 1, sea_rows - OSTEPS)
    out_a[...] = jnp.where(even, south, north)
    out_b[...] = jnp.where(even, north, south)


def from_ends(secs, a, b):
    s = lax.axis_index("sec")
    even = s % 2 == 0
    a, b = a[...].astype(f32), b[...].astype(f32)
    north = jnp.where(s > 0, jnp.where(even, b, a), 0.0)
    south = jnp.where(s < secs - 1, jnp.where(even, a, b), 0.0)
    return north, south


def halves_beside(piece, at, count, halves):
    cut = [piece[at + h * count : at + (h + 1) * count] for h in range(halves)]
    return jnp.concatenate(cut, axis=1)


def five(up, mid, down):
    axis = mid.ndim - 2
    return mid + up + down + (pltpu.roll(mid, 1, axis) + pltpu.roll(mid, mid.shape[axis] - 1, axis))


def on_grid(tiles, row, own):
    t = lax.axis_index("tile")
    side = row[own:]
    sub = sublane(side.shape)
    ok = ((sub >= 4) | (t < tiles - 1)) & ((sub < 4) | (t > 0))
    return jnp.concatenate([row[:own], jnp.where(ok, side, 0.0)], axis=0)


def physics(x, layers, hid):
    first, second = layers
    block = 256
    for j in range(0, first.shape[1], block):
        u = jnp.dot(x, first[:, j : j + block], preferred_element_type=f32)
        hid[:, j : j + block] = (u + u * jnp.tanh(u)).astype(bf16)
    return lambda: jnp.dot(hid[...], second[...], preferred_element_type=f32)


def upright(line):
    n = line.shape[1]
    shape = (n, n)
    eye = sublane(shape) == lax.broadcasted_iota(jnp.int32, shape, 1)
    return jnp.sum(jnp.where(eye, jnp.broadcast_to(line, shape), 0.0), axis=1, keepdims=True)


def tile_iotas():
    return lax.broadcasted_iota(jnp.int32, (8, LANES), 1), sublane((8, LANES))


def add_row(means, new, r):
    lane, sub = tile_iotas()
    cols = new.shape[0]
    for k in range(cols // 8):
        hit = lane == (r // 2) * (cols // 2) + 4 * k + sub // 2
        for q in range(2):
            value = new[8 * k : 8 * k + 8, q * LANES : q * LANES + 1]
            means[q] = means[q] + jnp.where(hit, value, 0.0)


def plan(
    secs, tiles, first, tile_map, cloudy, blend, present, spots, cells, spread, flags,
    place, cloudy_here, sems,
):
    map_copy = pltpu.make_async_copy(tile_map, place, sems.at[0])
    map_copy.start()
    flags_copy = pltpu.make_async_copy(cloudy, cloudy_here, sems.at[1])
    flags_copy.start()
    rows, cols = cloudy.shape
    half_cols = cols // 2
    cell = sublane(spots.shape)
    at = lax.broadcasted_iota(jnp.int32, spots.shape, 1) % LANES
    spots[...] = (at == cell // cols * half_cols + cell % cols // 2).astype(f32).astype(bf16)
    at = lax.broadcasted_iota(jnp.int32, cells.shape, 1) % LANES
    cells[...] = (at == sublane(cells.shape)).astype(f32).astype(bf16)
    at = lax.broadcasted_iota(jnp.int32, spread.shape, 1) // 2
    spread[...] = (at == sublane(spread.shape) % half_cols).astype(f32).astype(bf16)
    count = secs * tiles
    s, t = lax.axis_index("sec"), lax.axis_index("tile")
    map_copy.wait()
    under = jnp.int32(0)
    for k in range(tiles):
        under = jnp.where(place[k] == t, k, under)

    def device(shape):
        row = sublane(shape)
        block, kind = row // 8, row % 8
        at_s = s + block // 3 - 1
        at_t = jnp.where(kind < 2, t, under) + block % 3 - 1
        ok = (at_s >= 0) & (at_s < secs) & (at_t >= 0) & (at_t < tiles)
        return kind, at_s * tiles, at_t, ok

    present[...] = device(present.shape)[3].astype(f32)
    shape = (blend.shape[0], blend.shape[1] // 3)
    kind, base, at_t, ok = device(shape)
    above = jnp.zeros(shape, jnp.int32)
    for k in range(tiles):
        above = jnp.where(at_t == k, place[k], above)
    column = lax.broadcasted_iota(jnp.int32, shape, 1)
    which, column = column // count, column % count
    here = jnp.where(column == base + at_t, 1.0, 0.0)
    there = jnp.where(column == base + above, 1.0, 0.0)
    top = jnp.where(kind == 1, 0.2, jnp.where(kind == 3, 1.0, 1.4))
    parts = (
        jnp.where((kind == 0) | (kind == 2), -0.4, 0.0) * there,
        jnp.where(kind == 1, -0.4, 0.0) * there,
        top * here,
        jnp.where(kind == 1, 1.0, 0.0) * here,
    )
    total = jnp.zeros(shape, f32)
    for q, part in enumerate(parts):
        total = jnp.where(which == q, part, total)
    high, low = parts_of(jnp.where(ok & (kind < 4), total, 0.0), 2)
    blend[...] = jnp.concatenate([high, high, low], axis=1)
    flags_copy.wait()
    values = cloudy_here[...].astype(f32)
    for r in range(rows):
        flag = upright(values[r : r + 1, :])
        flags[r * cols : (r + 1) * cols, :] = jnp.broadcast_to(flag, (cols, LANES))


def main(
    secs, tiles, atmos, flags, w_in, w_out, c_in, c_out, ocean, tile_a, tile_b, rows_b, rows_a,
    field, sums, ends, xs, hid,
):
    rows, cols, feat = atmos.shape
    sea_rows, sea_cols, sea_feat = ocean.shape
    halves = feat // LANES
    s = lax.axis_index("sec")
    sides = Sides(tiles, rows, feat, tile_a, tile_b)
    north, south = from_ends(secs, rows_a, rows_b)

    def line(r):
        if 0 <= r < rows:
            return jnp.concatenate([atmos[r], sides.air(r)], axis=0)
        piece, k = (north, r + ASTEPS) if r < 0 else (south, r - rows)
        core = halves_beside(piece, k * halves * cols, cols, halves)
        return jnp.concatenate([core, jnp.zeros((8, feat), f32)], axis=0)

    lines, ones = [line(-2), line(-1)], []
    for r in range(-1, rows + 1):
        lines.append(line(r + 1))
        one = on_grid(tiles, five(*lines[-3:]), cols)
        if r == -1:
            one = jnp.where(s > 0, one, 0.0)
        if r == rows:
            one = jnp.where(s < secs - 1, one, 0.0)
        ones.append(one)
        if len(ones) >= 3:
            two = kappa_air**ASTEPS * five(*ones[-3:])[:cols]
            field[r - 1] = two
            xs[(r - 1) * cols : r * cols, :] = (0.5 * two).astype(bf16)
    ends[...] = jnp.zeros(ends.shape, f32)
    for k, r in enumerate((0, rows - 1)):
        ends[2 * k : 2 * k + 1, :] = field[r, 0:1, :]
        ends[2 * k + 1 : 2 * k + 2, :] = field[r, cols - 1 : cols, :]
    clear = physics(xs[...], (w_in, w_out), hid.at[0])()
    cloud = physics(xs[...], (c_in, c_out), hid.at[1])()
    means = [jnp.zeros((8, LANES), f32) for _ in range(2)]
    for r in range(rows):
        span = slice(r * cols, (r + 1) * cols)
        flag = jnp.concatenate([flags[span, :]] * halves, axis=1)
        new = field[r] + (clear[span] + flag * cloud[span]).astype(bf16).astype(f32)
        field[r] = new
        if r in (0, rows - 1):
            sub = sublane(new.shape)
            new = jnp.where((sub > 0) & (sub < cols - 1), new, 0.0)
        add_row(means, new, r)
    lane, sub = tile_iotas()
    tops = [jnp.zeros((8, LANES), f32) for _ in range(2)]
    for r in range(sea_rows):
        for k in range(sea_cols // 8):
            hit = lane == r * sea_cols + 8 * k + sub
            for q in range(2):
                at = q * (sea_feat // 2)
                value = ocean[r, 8 * k : 8 * k + 8, at : at + 1]
                tops[q] = tops[q] + jnp.where(hit, value, 0.0)
    for q, part in enumerate(means + tops):
        sums[q] = part


def finish(
    secs, old, all_flags, w_in, w_out, c_in, c_out, ends, corner_b, corner_a, sums,
    field, pay, hid,
):
    rows, cols, feat = field.shape
    halves = feat // LANES
    half_cols = cols // 2
    north, south = from_ends(secs, corner_a, corner_b)
    north = halves_beside(north, 0, 8, halves)
    south = halves_beside(south, 0, 8, halves)
    sub = sublane((8, feat))
    diagonal = jnp.zeros((8, feat), f32)
    for k, cell in enumerate((north[7:8], north[0:1], south[7:8], south[0:1])):
        diagonal = jnp.where(sub == k, cell, diagonal)
    state = ends[...] + 2.0 * kappa_air**ASTEPS * diagonal
    x = (0.5 * jnp.concatenate([state, jnp.zeros((8, feat), f32)], axis=0)).astype(bf16)
    clear = physics(x, (w_in, w_out), hid.at[0])
    cloud = physics(x, (c_in, c_out), hid.at[1])
    clear, cloud = clear(), cloud()
    places = ((0, 0), (0, cols - 1), (rows - 1, 0), (rows - 1, cols - 1))
    flag = jnp.zeros((8, LANES), f32)
    lane, sub_lane = tile_iotas()
    at = jnp.zeros((8, LANES), jnp.int32)
    for k, (r, c) in enumerate(places):
        cell = r * cols + c
        flag = jnp.where(sub_lane == k, all_flags[cell : cell + 1, :], flag)
        at = jnp.where(sub_lane == k, (r // 2) * half_cols + c // 2, at)
    flag = jnp.concatenate([flag] * halves, axis=1)
    new = state + (clear[:8] + flag * cloud[:8]).astype(bf16).astype(f32)
    for k, (r, c) in enumerate(places):
        field[r, c : c + 1, :] = new[k : k + 1]
    hit = (lane == at) & (sub_lane < 4)
    means = [
        sums[q] + jnp.where(hit, new[:, q * LANES : q * LANES + 1], 0.0) for q in range(2)
    ]
    parts = (0.25 * means[0], 0.25 * means[1], sums[2], sums[3])
    total = jnp.concatenate([jnp.sum(part, axis=0, keepdims=True) for part in parts], axis=0)
    pay[...] = jnp.broadcast_to(total[None], pay.shape)


def sea_steps(secs, tiles, rows, cols, feat, ocean, halos, out):
    sea_rows, sea_cols, sea_feat = ocean.shape
    tile_a, tile_b, rows_a, rows_b, corner_a, corner_b = halos
    s = lax.axis_index("sec")
    sides = Sides(tiles, rows, feat, tile_a, tile_b)
    cores = from_ends(secs, rows_a, rows_b)
    corners = from_ends(secs, corner_a, corner_b)
    halves = feat // LANES
    state = []
    for r in range(-OSTEPS, sea_rows + OSTEPS):
        if 0 <= r < sea_rows:
            core, side = ocean[r], sides.sea(r)
        else:
            end, k = (0, r + OSTEPS) if r < 0 else (1, r - sea_rows)
            at = ASTEPS * halves * cols + k * sea_cols
            core = cores[end][at : at + sea_cols]
            at = 8 * (halves + k)
            side = corners[end][at : at + 8]
        state.append(jnp.concatenate([core, side], axis=0))
    for depth in reversed(range(OSTEPS)):
        state = [five(*state[k : k + 3]) for k in range(len(state) - 2)]
        if depth == 0:
            break
        for k, new in enumerate(state):
            new = on_grid(tiles, new, sea_cols)
            if k < depth:
                new = jnp.where(s > 0, new, 0.0)
            elif k >= depth + sea_rows:
                new = jnp.where(s < secs - 1, new, 0.0)
            state[k] = new
    for r in range(sea_rows):
        out[r] = kappa_sea**OSTEPS * state[r][:sea_cols]


def parts_of(v, count):
    parts = []
    for _ in range(count):
        part = v.astype(bf16)
        v = v - part.astype(f32)
        parts.append(part)
    return parts


def final(
    secs, tiles, gathered, blend, inside, spots, cells, spread, field, ocean,
    tile_a, tile_b, rows_b, rows_a, corner_b, corner_a,
    air_out, sea_out, back, stage, sea, sea_stage, back_stage, sems,
):
    rows, cols, feat = air_out.shape
    sea_rows, sea_cols, sea_feat = sea.shape
    halves = feat // LANES
    half_cols = cols // 2

    def upright_at(lines, *lanes):
        first = sublane((16, LANES)) == 0
        groups = [jnp.zeros((16, 2 * LANES), bf16)] * (LANES // 16)
        for line, at in zip(lines, lanes):
            whole = jnp.where(first, jnp.broadcast_to(line, first.shape), 0.0)
            groups[at // 16] = jnp.concatenate(parts_of(whole, 2), axis=1)
        return jnp.concatenate(groups, axis=0)

    def against(one_hot, values):
        return lax.dot_general(
            one_hot, values, (((1,), (1,)), ((), ())), preferred_element_type=f32
        )

    everything = jnp.concatenate([gathered[:, q, :] for q in range(4)], axis=0)
    high, low = parts_of(everything, 2)
    blocks = jnp.dot(
        blend[...],
        jnp.concatenate([high, low, high], axis=0),
        preferred_element_type=f32,
    )
    keep = inside[...]
    blocks = {
        (k // 3, k % 3): (blocks[8 * k : 8 * k + 8], keep[8 * k : 8 * k + 8] > 0.0)
        for k in range(9)
    }
    landing = blocks[1, 1][0][3:4]
    patch = against(spots[...], upright_at([0.4 * landing], 0))
    rest = jnp.where(lax.broadcasted_iota(jnp.int32, (cols, LANES), 1) == 0, 0.6, 1.0)

    step_rows = 4
    copies = []
    for first in range(0, rows, step_rows):
        for r in range(first, first + step_rows):
            if r % 2 == 0:
                value = patch[(r // 2) * cols : (r // 2 + 1) * cols]
                added = (value, 0.5 * value)
            for h in range(halves):
                lanes = slice(h * LANES, (h + 1) * LANES)
                stage[r, :, lanes] = field[r, :, lanes] * rest + added[h]
        copies.append(
            pltpu.make_async_copy(
                stage.at[first : first + step_rows],
                air_out.at[first : first + step_rows],
                sems.at[first // step_rows],
            )
        )
        copies[-1].start()

    halos = tile_a, tile_b, rows_a, rows_b, corner_a, corner_b
    sea_steps(secs, tiles, rows, cols, feat, ocean, halos, sea)
    lane = tile_iotas()[0]
    first_c, last_c = lane % sea_cols == 0, lane % sea_cols == sea_cols - 1
    first_r, last_r = lane < sea_cols, lane >= LANES - sea_cols

    def roll(v, shift):
        return pltpu.roll(v, shift % LANES, 1)

    def step(old, wanted):
        def side(at, edge, shift, cross):
            near = roll(old[at][0], shift)
            return lambda other: (
                jnp.where(edge, roll(old[other][0], cross), near) if other in old else near
            )

        new = {}
        for i, j in wanted:
            v, ok = old[i, j]
            up = side((i, j), first_r, sea_cols, sea_cols)((i - 1, j))
            down = side((i, j), last_r, -sea_cols, -sea_cols)((i + 1, j))
            west = side((i, j), first_c, 1, 1 - sea_cols)((i, j - 1))
            east = side((i, j), last_c, -1, sea_cols - 1)((i, j + 1))
            v = v + (up + down) + (west + east)
            new[i, j] = jnp.where(ok, v, 0.0), ok
        return new

    plus = [(0, 1), (1, 0), (1, 1), (1, 2), (2, 1)]
    for wanted in [list(blocks)] * (OSTEPS - 2) + [plus, [(1, 1)]]:
        blocks = step(blocks, wanted)
    mine = kappa_sea**OSTEPS * blocks[1, 1][0]
    own = upright_at([mine[0:1], mine[1:2]], 0, sea_feat // 2)
    own = against(cells[...], own)
    lane_s = lax.broadcasted_iota(jnp.int32, (sea_cols, sea_feat), 1)
    surface = jnp.logical_or(lane_s == 0, lane_s == sea_feat // 2)
    for r in range(sea_rows):
        new = own[r * sea_cols : (r + 1) * sea_cols]
        sea_stage[r] = jnp.where(surface, new, sea[r])
    copies.append(pltpu.make_async_copy(sea_stage, sea_out, sems.at[rows // step_rows]))
    copies[-1].start()

    returned = jnp.broadcast_to(mine[2:3], (rows, LANES))
    lane_b = lax.broadcasted_iota(jnp.int32, (rows, LANES), 1)
    lines = jnp.where(lane_b // half_cols == sublane((rows, LANES)) // 2, returned, 0.0)
    lines = jnp.concatenate(parts_of(lines, 2), axis=1)
    back_stage[...] = jnp.dot(lines, spread[...], preferred_element_type=f32)
    copies.append(pltpu.make_async_copy(back_stage, back, sems.at[rows // step_rows + 1]))
    copies[-1].start()
    for copy in copies:
        copy.wait()


def local(atmos, cloudy, weight_in, weight_out, cloud_in, cloud_out, ocean, tile_map):
    rows, cols, feat = atmos.shape
    sea_rows, sea_cols, sea_feat = ocean.shape
    secs, tiles = lax.axis_size("sec"), lax.axis_size("tile")
    count = secs * tiles
    halves = feat // LANES
    width = weight_in.shape[1]
    sec_even, sec_odd, tile_even, tile_odd = exchanges(secs, tiles)
    shape = jax.ShapeDtypeStruct

    def call(
        body, name, out_shape, in_specs, out_specs, scratch=(), flops=0, args=(), aliases={}
    ):
        return pl.pallas_call(
            body,
            out_shape=out_shape,
            in_specs=in_specs,
            out_specs=out_specs,
            scratch_shapes=scratch,
            input_output_aliases=aliases,
            compiler_params=pltpu.CompilerParams(vmem_limit_bytes=8 * 1024 * 1024),
            cost_estimate=pl.CostEstimate(flops=flops, bytes_accessed=0, transcendentals=0),
            name=name,
        )(*args)

    def hbm(a):
        return pltpu.with_memory_space_constraint(a, pltpu.HBM)

    lines = ASTEPS * halves * cols + OSTEPS * sea_cols
    out = shape((8 * (rows // 4 * halves + sea_rows // 2), LANES), bf16)
    ends = shape((lines, LANES), bf16)
    send_a, send_b, ends_a, ends_b = call(
        pack_first, "pack_first", (out, out, ends, ends),
        [HBM] * 2, (VMEM,) * 4,
        [
            pltpu.VMEM((rows, 8, feat), f32),
            pltpu.VMEM((rows, 8, feat), f32),
            pltpu.VMEM((2, ASTEPS, cols, feat), f32),
            pltpu.VMEM(ocean.shape, f32),
            pltpu.SemaphoreType.DMA((5,)),
        ],
        args=(hbm(atmos), hbm(ocean)),
    )
    tile_a = lax.ppermute(send_a, AXES, tile_even)
    tile_b = lax.ppermute(send_b, AXES, tile_odd)
    rows_b = lax.ppermute(ends_b, AXES, sec_odd)
    rows_a = lax.ppermute(ends_a, AXES, sec_even)
    *planned, flags = call(
        functools.partial(plan, secs, tiles), "plan",
        (
            shape((80, 12 * count), bf16),
            shape((72, LANES), f32),
            shape((rows // 2 * cols, 2 * LANES), bf16),
            shape((LANES, 2 * LANES), bf16),
            shape((2 * LANES, cols), bf16),
            shape((rows * cols, LANES), f32),
        ),
        [pl.BlockSpec(memory_space=pl.ANY), HBM, HBM],
        (VMEM,) * 6,
        [
            pltpu.SMEM(tile_map.shape, jnp.int32),
            pltpu.VMEM(cloudy.shape, jnp.int32),
            pltpu.SemaphoreType.DMA((2,)),
        ],
        flops=1 << 30,
        args=(send_a, hbm(tile_map), hbm(cloudy)),
    )
    out = shape((8 * (halves + OSTEPS), LANES), bf16)
    send_a, send_b = call(
        functools.partial(pack_corners, tiles, rows, feat, sea_rows), "pack_corners", (out, out),
        [VMEM] * 2 + [pl.BlockSpec(memory_space=pl.ANY)], (VMEM, VMEM),
        args=(tile_a, tile_b, planned[1]),
    )
    corner_b = lax.ppermute(send_b, AXES, sec_odd)
    corner_a = lax.ppermute(send_a, AXES, sec_even)

    weights = (weight_in, weight_out, cloud_in, cloud_out)
    field, sums, ends = call(
        functools.partial(main, secs, tiles), "main",
        (shape(atmos.shape, f32), shape((4, 8, LANES), f32), shape((8, feat), f32)),
        [VMEM] * 11,
        (VMEM,) * 3,
        [pltpu.VMEM((rows * cols, feat), bf16), pltpu.VMEM((2, rows * cols, width), bf16)],
        flops=rows * cols * feat * width * 8,
        args=(atmos, flags, *weights, ocean, tile_a, tile_b, rows_b, rows_a),
    )
    field, pay = call(
        functools.partial(finish, secs), "finish",
        (shape(atmos.shape, f32), shape((count, 4, LANES), f32)),
        [VMEM] * 10,
        (VMEM,) * 2,
        [pltpu.VMEM((2, 16, width), bf16)],
        flops=16 * feat * width * 8,
        args=(field, flags, *weights, ends, corner_b, corner_a, sums),
        aliases={0: 0},
    )
    gathered = lax.all_to_all(pay, AXES, 0, 0)
    return call(
        functools.partial(final, secs, tiles), "final",
        (shape(atmos.shape, f32), shape(ocean.shape, f32), shape((rows, cols), f32)),
        [VMEM] * 14,
        (HBM,) * 3,
        [
            pltpu.VMEM(atmos.shape, f32),
            pltpu.VMEM(ocean.shape, f32),
            pltpu.VMEM(ocean.shape, f32),
            pltpu.VMEM((rows, cols), f32),
            pltpu.SemaphoreType.DMA((rows // 4 + 2,)),
        ],
        args=(gathered, *planned, field, ocean, tile_a, tile_b, rows_b, rows_a, corner_b, corner_a),
    )


def solution(mesh):
    placed = (
        P("sec", "tile", None),
        P("sec", "tile"),
        P(),
        P(),
        P(),
        P(),
        P("sec", "tile", None),
        P(),
    )
    return jax.shard_map(
        local,
        mesh=mesh,
        in_specs=placed,
        out_specs=(P("sec", "tile", None), P("sec", "tile", None), P("sec", "tile")),
        check_vma=False,
    )
```

```python
import functools

import jax
import jax.numpy as jnp
from jax import lax
from jax.experimental import pallas as pl
from jax.experimental.pallas import tpu as pltpu
from jax.sharding import PartitionSpec as P

ASTEPS = 2
OSTEPS = 4
LANES = 128

kappa_air = 0.2
kappa_sea = 0.2

f32 = jnp.float32
bf16 = jnp.bfloat16
VMEM = pl.BlockSpec(memory_space=pltpu.VMEM)
HBM = pl.BlockSpec(memory_space=pltpu.HBM)
AXES = ("sec", "tile")


def exchanges(secs, tiles):
    def whole(partner):
        return [
            (s * tiles + t, partner(s, t)[0] * tiles + partner(s, t)[1])
            for s in range(secs)
            for t in range(tiles)
        ]

    def odd_sec(s, t):
        if s in (0, secs - 1):
            return secs - 1 - s, t
        return (s + 1 if s % 2 else s - 1), t

    def odd_tile(s, t):
        if t in (0, tiles - 1):
            return s ^ 1, t
        return s, (t + 1 if t % 2 else t - 1)

    return (
        whole(lambda s, t: (s ^ 1, t)),
        whole(odd_sec),
        whole(lambda s, t: (s, t ^ 1)),
        whole(odd_tile),
    )


def sublane(shape):
    return lax.broadcasted_iota(jnp.int32, shape, len(shape) - 2)


def turn(v, shift):
    return v if shift % 8 == 0 else pltpu.roll(v, shift % 8, 0)


def halves_of(v):
    return [v[:, at : at + LANES] for at in range(0, v.shape[1], LANES)]


def pack_first(atmos, ocean, out_a, out_b, rows_a, rows_b, west, east, ends, sea, sems):
    rows, cols, feat = atmos.shape
    sea_rows, sea_cols, _ = ocean.shape
    copies = (
        pltpu.make_async_copy(atmos.at[0:ASTEPS], ends.at[0], sems.at[3]),
        pltpu.make_async_copy(atmos.at[rows - ASTEPS : rows], ends.at[1], sems.at[4]),
        pltpu.make_async_copy(atmos.at[:, 0:ASTEPS], west.at[:, 0:ASTEPS], sems.at[0]),
        pltpu.make_async_copy(
            atmos.at[:, cols - ASTEPS : cols], east.at[:, 8 - ASTEPS : 8], sems.at[1]
        ),
        pltpu.make_async_copy(ocean, sea, sems.at[2]),
    )
    for copy in copies:
        copy.start()
    for copy in copies:
        copy.wait()
    to_west, to_east = [], []
    sub = sublane((8, feat))
    for g in range(rows // 4):
        tile_w, tile_e = west[4 * g], turn(east[4 * g], 2)
        for k in range(1, 4):
            tile_w = jnp.where(sub < 2 * k, tile_w, turn(west[4 * g + k], 2 * k))
            tile_e = jnp.where(sub < 2 * k, tile_e, turn(east[4 * g + k], 2 * k + 2))
        to_west += halves_of(tile_w)
        to_east += halves_of(tile_e)
    low = sublane((8, LANES)) < 4
    for r in range(0, sea_rows, 2):
        to_west.append(jnp.where(low, sea[r, 0:8], turn(sea[r + 1, 0:8], 4)))
        to_east.append(
            jnp.where(low, turn(sea[r, sea_cols - 8 :], 4), sea[r + 1, sea_cols - 8 :])
        )
    to_west = jnp.concatenate(to_west, axis=0).astype(bf16)
    to_east = jnp.concatenate(to_east, axis=0).astype(bf16)
    even = lax.axis_index("tile") % 2 == 0
    out_a[...] = jnp.where(even, to_east, to_west)
    out_b[...] = jnp.where(even, to_west, to_east)
    south = 1 - lax.axis_index("sec") % 2
    for out, end in ((rows_a, south), (rows_b, 1 - south)):
        parts = []
        for r in range(ASTEPS):
            parts += halves_of(ends[end, r])
        parts += [sea[end * (sea_rows - OSTEPS) + r] for r in range(OSTEPS)]
        out[...] = jnp.concatenate(parts, axis=0).astype(bf16)


class Sides:
    def __init__(self, tiles, rows, feat, tile_a, tile_b):
        t = lax.axis_index("tile")
        even = t % 2 == 0
        a, b = tile_a[...].astype(f32), tile_b[...].astype(f32)
        self.west = jnp.where(t > 0, jnp.where(even, b, a), 0.0)
        self.east = jnp.where(t < tiles - 1, jnp.where(even, a, b), 0.0)
        self.halves = feat // LANES
        self.sea_at = rows // 4 * self.halves
        self.low = sublane((8, LANES)) < 4

    def merge(self, tile, shift_w, shift_e):
        span = slice(8 * tile, 8 * tile + 8)
        return jnp.where(self.low, turn(self.east[span], shift_e), turn(self.west[span], shift_w))

    def air(self, r):
        g, k = r // 4, r % 4
        return jnp.concatenate(
            [self.merge(g * self.halves + h, -2 * k - 2, -2 * k) for h in range(self.halves)],
            axis=1,
        )

    def sea(self, r):
        return self.merge(self.sea_at + r // 2, 4 if r % 2 == 0 else 0, 4 * (r % 2))


def pack_corners(tiles, rows, feat, sea_rows, tile_a, tile_b, last, out_a, out_b):
    sides = Sides(tiles, rows, feat, tile_a, tile_b)

    sub = sublane((8, LANES))

    def corners(corner, near, inward):
        second, third = sides.sea(near + inward), sides.sea(near + 2 * inward)
        shared = jnp.where(sub == 2, turn(third, 2), jnp.where(sub == 5, turn(third, -2), second))
        parts = halves_of(sides.air(corner)) + [sides.sea(near), shared]
        return jnp.concatenate(parts, axis=0).astype(bf16)

    even = lax.axis_index("sec") % 2 == 0
    north, south = corners(0, 0, 1), corners(rows - 1, sea_rows - 1, -1)
    out_a[...] = jnp.where(even, south, north)
    out_b[...] = jnp.where(even, north, south)


def from_ends(secs, a, b):
    s = lax.axis_index("sec")
    even = s % 2 == 0
    a, b = a[...].astype(f32), b[...].astype(f32)
    north = jnp.where(s > 0, jnp.where(even, b, a), 0.0)
    south = jnp.where(s < secs - 1, jnp.where(even, a, b), 0.0)
    return north, south


def halves_beside(piece, at, count, halves):
    cut = [piece[at + h * count : at + (h + 1) * count] for h in range(halves)]
    return jnp.concatenate(cut, axis=1)


def five(up, mid, down):
    axis = mid.ndim - 2
    return mid + up + down + (pltpu.roll(mid, 1, axis) + pltpu.roll(mid, mid.shape[axis] - 1, axis))


def on_grid(tiles, row, own):
    t = lax.axis_index("tile")
    side = row[own:]
    sub = sublane(side.shape)
    ok = ((sub >= 4) | (t < tiles - 1)) & ((sub < 4) | (t > 0))
    return jnp.concatenate([row[:own], jnp.where(ok, side, 0.0)], axis=0)


def silu(v):
    return v * (0.5 + 0.5 * jnp.tanh(0.5 * v))


def physics(x, w_in, w_out, c_in, c_out, hid):
    width = w_in.shape[1]
    block = 256
    for which, first in enumerate((w_in, c_in)):
        for j in range(0, width, block):
            h = jnp.dot(x, first[:, j : j + block], preferred_element_type=f32)
            hid[which, :, j : j + block] = silu(h).astype(bf16)
    clear = jnp.dot(hid[0], w_out[...], preferred_element_type=f32)
    cloud = jnp.dot(hid[1], c_out[...], preferred_element_type=f32)
    return clear, cloud


def upright(line):
    n = line.shape[1]
    shape = (n, n)
    eye = sublane(shape) == lax.broadcasted_iota(jnp.int32, shape, 1)
    return jnp.sum(jnp.where(eye, jnp.broadcast_to(line, shape), 0.0), axis=1, keepdims=True)


def tile_iotas():
    return lax.broadcasted_iota(jnp.int32, (8, LANES), 1), sublane((8, LANES))


def add_row(means, new, r):
    lane, sub = tile_iotas()
    cols = new.shape[0]
    for k in range(cols // 8):
        hit = lane == (r // 2) * (cols // 2) + 4 * k + sub // 2
        for q in range(2):
            value = new[8 * k : 8 * k + 8, q * LANES : q * LANES + 1]
            means[q] = means[q] + jnp.where(hit, value, 0.0)


def plan(
    secs, tiles, first, tile_map, cloudy, blend, present, spots, cells, spread, flags,
    place, cloudy_here, sems,
):
    map_copy = pltpu.make_async_copy(tile_map, place, sems.at[0])
    map_copy.start()
    flags_copy = pltpu.make_async_copy(cloudy, cloudy_here, sems.at[1])
    flags_copy.start()
    rows, cols = cloudy.shape
    half_cols = cols // 2
    cell = sublane(spots.shape)
    at = lax.broadcasted_iota(jnp.int32, spots.shape, 1) % LANES
    spots[...] = (at == cell // cols * half_cols + cell % cols // 2).astype(f32).astype(bf16)
    at = lax.broadcasted_iota(jnp.int32, cells.shape, 1) % LANES
    cells[...] = (at == sublane(cells.shape)).astype(f32).astype(bf16)
    at = lax.broadcasted_iota(jnp.int32, spread.shape, 1) // 2
    spread[...] = (at == sublane(spread.shape) % half_cols).astype(f32).astype(bf16)
    count = secs * tiles
    s, t = lax.axis_index("sec"), lax.axis_index("tile")
    map_copy.wait()
    under = jnp.int32(0)
    for k in range(tiles):
        under = jnp.where(place[k] == t, k, under)

    def device(shape):
        row = sublane(shape)
        block, kind = row // 8, row % 8
        at_s = s + block // 3 - 1
        at_t = jnp.where(kind < 2, t, under) + block % 3 - 1
        ok = (at_s >= 0) & (at_s < secs) & (at_t >= 0) & (at_t < tiles)
        return kind, at_s * tiles, at_t, ok

    present[...] = device(present.shape)[3].astype(f32)
    shape = (blend.shape[0], blend.shape[1] // 2)
    kind, base, at_t, ok = device(shape)
    above = jnp.zeros(shape, jnp.int32)
    for k in range(tiles):
        above = jnp.where(at_t == k, place[k], above)
    column = lax.broadcasted_iota(jnp.int32, shape, 1)
    which, column = column // count, column % count
    here = jnp.where(column == base + at_t, 1.0, 0.0)
    there = jnp.where(column == base + above, 1.0, 0.0)
    top = jnp.where((kind == 1) | (kind == 3), 1.0, 7.0)
    parts = (
        jnp.where((kind == 0) | (kind == 2), -2.0, 0.0) * there,
        jnp.where(kind == 1, -2.0, 0.0) * there,
        top * here,
        jnp.where(kind == 1, 5.0, 0.0) * here,
    )
    total = jnp.zeros(shape, f32)
    for q, part in enumerate(parts):
        total = jnp.where(which == q, part, total)
    total = jnp.where(ok & (kind < 4), total, 0.0)
    blend[...] = jnp.concatenate([total, total], axis=1).astype(bf16)
    flags_copy.wait()
    values = cloudy_here[...].astype(f32)
    for r in range(rows):
        flag = upright(values[r : r + 1, :])
        flags[r * cols : (r + 1) * cols, :] = jnp.broadcast_to(flag, (cols, LANES))


def main(
    secs, tiles, atmos, flags, w_in, w_out, c_in, c_out, ocean, tile_a, tile_b, rows_b, rows_a,
    field, sums, ends, xs, hid,
):
    rows, cols, feat = atmos.shape
    sea_rows, sea_cols, sea_feat = ocean.shape
    halves = feat // LANES
    s = lax.axis_index("sec")
    sides = Sides(tiles, rows, feat, tile_a, tile_b)
    north, south = from_ends(secs, rows_a, rows_b)

    def line(r):
        if 0 <= r < rows:
            return jnp.concatenate([atmos[r], sides.air(r)], axis=0)
        piece, k = (north, r + ASTEPS) if r < 0 else (south, r - rows)
        core = halves_beside(piece, k * halves * cols, cols, halves)
        return jnp.concatenate([core, jnp.zeros((8, feat), f32)], axis=0)

    lines, ones = [line(-2), line(-1)], []
    for r in range(-1, rows + 1):
        lines.append(line(r + 1))
        one = on_grid(tiles, five(*lines[-3:]), cols)
        if r == -1:
            one = jnp.where(s > 0, one, 0.0)
        if r == rows:
            one = jnp.where(s < secs - 1, one, 0.0)
        ones.append(one)
        if len(ones) >= 3:
            two = kappa_air**ASTEPS * five(*ones[-3:])[:cols]
            field[r - 1] = two
            xs[(r - 1) * cols : r * cols, :] = two.astype(bf16)
    ends[...] = jnp.zeros(ends.shape, f32)
    for k, r in enumerate((0, rows - 1)):
        ends[2 * k : 2 * k + 1, :] = field[r, 0:1, :]
        ends[2 * k + 1 : 2 * k + 2, :] = field[r, cols - 1 : cols, :]
    clear, cloud = physics(xs[...], w_in, w_out, c_in, c_out, hid)
    means = [jnp.zeros((8, LANES), f32) for _ in range(2)]
    for r in range(rows):
        span = slice(r * cols, (r + 1) * cols)
        flag = jnp.concatenate([flags[span, :]] * halves, axis=1)
        new = field[r] + (clear[span] + flag * cloud[span]).astype(bf16).astype(f32)
        field[r] = new
        if r in (0, rows - 1):
            sub = sublane(new.shape)
            new = jnp.where((sub > 0) & (sub < cols - 1), new, 0.0)
        add_row(means, new, r)
    lane, sub = tile_iotas()
    tops = [jnp.zeros((8, LANES), f32) for _ in range(2)]
    for r in range(sea_rows):
        for k in range(sea_cols // 8):
            hit = lane == r * sea_cols + 8 * k + sub
            for q in range(2):
                at = q * (sea_feat // 2)
                value = ocean[r, 8 * k : 8 * k + 8, at : at + 1]
                tops[q] = tops[q] + jnp.where(hit, value, 0.0)
    for q, part in enumerate(means + tops):
        sums[q] = part


def finish(
    secs, old, all_flags, w_in, w_out, c_in, c_out, ends, corner_b, corner_a, sums,
    field, pay, hid,
):
    rows, cols, feat = field.shape
    halves = feat // LANES
    half_cols = cols // 2
    north, south = from_ends(secs, corner_a, corner_b)
    north = halves_beside(north, 0, 8, halves)
    south = halves_beside(south, 0, 8, halves)
    sub = sublane((8, feat))
    diagonal = jnp.zeros((8, feat), f32)
    for k, cell in enumerate((north[7:8], north[0:1], south[7:8], south[0:1])):
        diagonal = jnp.where(sub == k, cell, diagonal)
    state = ends[...] + 2.0 * kappa_air**ASTEPS * diagonal
    x = jnp.concatenate([state, jnp.zeros((8, feat), f32)], axis=0).astype(bf16)
    clear, cloud = physics(x, w_in, w_out, c_in, c_out, hid)
    places = ((0, 0), (0, cols - 1), (rows - 1, 0), (rows - 1, cols - 1))
    flag = jnp.zeros((8, LANES), f32)
    lane, sub_lane = tile_iotas()
    at = jnp.zeros((8, LANES), jnp.int32)
    for k, (r, c) in enumerate(places):
        cell = r * cols + c
        flag = jnp.where(sub_lane == k, all_flags[cell : cell + 1, :], flag)
        at = jnp.where(sub_lane == k, (r // 2) * half_cols + c // 2, at)
    flag = jnp.concatenate([flag] * halves, axis=1)
    new = state + (clear[:8] + flag * cloud[:8]).astype(bf16).astype(f32)
    for k, (r, c) in enumerate(places):
        field[r, c : c + 1, :] = new[k : k + 1]
    hit = (lane == at) & (sub_lane < 4)
    means = [
        sums[q] + jnp.where(hit, new[:, q * LANES : q * LANES + 1], 0.0) for q in range(2)
    ]
    parts = (0.25 * means[0], 0.25 * means[1], sums[2], sums[3])
    total = jnp.concatenate([jnp.sum(part, axis=0, keepdims=True) for part in parts], axis=0)
    pay[...] = jnp.broadcast_to(total[None], pay.shape)


def sea_steps(secs, tiles, rows, cols, feat, ocean, halos, out):
    sea_rows, sea_cols, sea_feat = ocean.shape
    tile_a, tile_b, rows_a, rows_b, corner_a, corner_b = halos
    s = lax.axis_index("sec")
    sides = Sides(tiles, rows, feat, tile_a, tile_b)
    cores = from_ends(secs, rows_a, rows_b)
    corners = from_ends(secs, corner_a, corner_b)
    halves = feat // LANES
    state = []
    for r in range(-OSTEPS, sea_rows + OSTEPS):
        if 0 <= r < sea_rows:
            core, side = ocean[r], sides.sea(r)
        else:
            end, k = (0, r + OSTEPS) if r < 0 else (1, r - sea_rows)
            at = ASTEPS * halves * cols + k * sea_cols
            core = cores[end][at : at + sea_cols]
            near, shared = (corners[end][8 * (halves + q) : 8 * (halves + q) + 8] for q in range(2))
            low = sublane(near.shape) < 4
            third = jnp.where(low, turn(shared, -2), turn(shared, 2))
            distance = -r if r < 0 else r - sea_rows + 1
            side = (near, shared, third, jnp.zeros(near.shape, f32))[distance - 1]
        state.append(jnp.concatenate([core, side], axis=0))
    for depth in reversed(range(OSTEPS)):
        state = [five(*state[k : k + 3]) for k in range(len(state) - 2)]
        if depth == 0:
            break
        for k, new in enumerate(state):
            new = on_grid(tiles, new, sea_cols)
            if k < depth:
                new = jnp.where(s > 0, new, 0.0)
            elif k >= depth + sea_rows:
                new = jnp.where(s < secs - 1, new, 0.0)
            state[k] = new
    for r in range(sea_rows):
        out[r] = kappa_sea**OSTEPS * state[r][:sea_cols]


def parts_of(v, count):
    parts = []
    for _ in range(count):
        part = v.astype(bf16)
        v = v - part.astype(f32)
        parts.append(part)
    return parts


def final(
    secs, tiles, gathered, blend, inside, spots, cells, spread, field, ocean,
    tile_a, tile_b, rows_b, rows_a, corner_b, corner_a,
    air_out, sea_out, back, stage, sea, sea_stage, back_stage, sems,
):
    rows, cols, feat = air_out.shape
    sea_rows, sea_cols, sea_feat = sea.shape
    halves = feat // LANES
    half_cols = cols // 2

    def upright_at(lines, *lanes):
        first = sublane((16, LANES)) == 0
        groups = [jnp.zeros((16, 2 * LANES), bf16)] * (LANES // 16)
        for line, at in zip(lines, lanes):
            whole = jnp.where(first, jnp.broadcast_to(line, first.shape), 0.0)
            groups[at // 16] = jnp.concatenate(parts_of(whole, 2), axis=1)
        return jnp.concatenate(groups, axis=0)

    def against(one_hot, values):
        return lax.dot_general(
            one_hot, values, (((1,), (1,)), ((), ())), preferred_element_type=f32
        )

    everything = jnp.concatenate([gathered[:, q, :] for q in range(4)], axis=0)
    everything = jnp.concatenate(parts_of(everything, 2), axis=0)
    blocks = jnp.dot(blend[...], everything, preferred_element_type=f32)
    keep = inside[...]
    blocks = {
        (k // 3, k % 3): (blocks[8 * k : 8 * k + 8], keep[8 * k : 8 * k + 8] > 0.0)
        for k in range(9)
    }
    landing = blocks[1, 1][0][3:4]
    patch = against(spots[...], upright_at([0.4 * landing], 0))
    rest = jnp.where(lax.broadcasted_iota(jnp.int32, (cols, LANES), 1) == 0, 0.6, 1.0)

    step_rows = 4
    copies = []
    for first in range(0, rows, step_rows):
        for r in range(first, first + step_rows):
            if r % 2 == 0:
                value = patch[(r // 2) * cols : (r // 2 + 1) * cols]
                added = (value, 0.5 * value)
            for h in range(halves):
                lanes = slice(h * LANES, (h + 1) * LANES)
                stage[r, :, lanes] = field[r, :, lanes] * rest + added[h]
        copies.append(
            pltpu.make_async_copy(
                stage.at[first : first + step_rows],
                air_out.at[first : first + step_rows],
                sems.at[first // step_rows],
            )
        )
        copies[-1].start()

    halos = tile_a, tile_b, rows_a, rows_b, corner_a, corner_b
    sea_steps(secs, tiles, rows, cols, feat, ocean, halos, sea)
    lane = tile_iotas()[0]
    first_c, last_c = lane % sea_cols == 0, lane % sea_cols == sea_cols - 1
    first_r, last_r = lane < sea_cols, lane >= LANES - sea_cols

    def roll(v, shift):
        return pltpu.roll(v, shift % LANES, 1)

    def step(old, wanted):
        def side(at, edge, shift, cross):
            near = roll(old[at][0], shift)
            return lambda other: (
                jnp.where(edge, roll(old[other][0], cross), near) if other in old else near
            )

        new = {}
        for i, j in wanted:
            v, ok = old[i, j]
            up = side((i, j), first_r, sea_cols, sea_cols)((i - 1, j))
            down = side((i, j), last_r, -sea_cols, -sea_cols)((i + 1, j))
            west = side((i, j), first_c, 1, 1 - sea_cols)((i, j - 1))
            east = side((i, j), last_c, -1, sea_cols - 1)((i, j + 1))
            v = v + (up + down) + (west + east)
            new[i, j] = jnp.where(ok, v, 0.0), ok
        return new

    plus = [(0, 1), (1, 0), (1, 1), (1, 2), (2, 1)]
    for wanted in [list(blocks)] * (OSTEPS - 2) + [plus, [(1, 1)]]:
        blocks = step(blocks, wanted)
    mine = kappa_sea ** (OSTEPS + 1) * blocks[1, 1][0]
    own = upright_at([mine[0:1], mine[1:2]], 0, sea_feat // 2)
    own = against(cells[...], own)
    lane_s = lax.broadcasted_iota(jnp.int32, (sea_cols, sea_feat), 1)
    surface = jnp.logical_or(lane_s == 0, lane_s == sea_feat // 2)
    for r in range(sea_rows):
        new = own[r * sea_cols : (r + 1) * sea_cols]
        sea_stage[r] = jnp.where(surface, new, sea[r])
    copies.append(pltpu.make_async_copy(sea_stage, sea_out, sems.at[rows // step_rows]))
    copies[-1].start()

    returned = jnp.broadcast_to(mine[2:3], (rows, LANES))
    lane_b = lax.broadcasted_iota(jnp.int32, (rows, LANES), 1)
    lines = jnp.where(lane_b // half_cols == sublane((rows, LANES)) // 2, returned, 0.0)
    lines = jnp.concatenate(parts_of(lines, 2), axis=1)
    back_stage[...] = jnp.dot(lines, spread[...], preferred_element_type=f32)
    copies.append(pltpu.make_async_copy(back_stage, back, sems.at[rows // step_rows + 1]))
    copies[-1].start()
    for copy in copies:
        copy.wait()


def local(atmos, cloudy, weight_in, weight_out, cloud_in, cloud_out, ocean, tile_map):
    rows, cols, feat = atmos.shape
    sea_rows, sea_cols, sea_feat = ocean.shape
    secs, tiles = lax.axis_size("sec"), lax.axis_size("tile")
    count = secs * tiles
    halves = feat // LANES
    width = weight_in.shape[1]
    sec_even, sec_odd, tile_even, tile_odd = exchanges(secs, tiles)
    shape = jax.ShapeDtypeStruct

    def call(
        body, name, out_shape, in_specs, out_specs, scratch=(), flops=0, args=(), aliases={}
    ):
        return pl.pallas_call(
            body,
            out_shape=out_shape,
            in_specs=in_specs,
            out_specs=out_specs,
            scratch_shapes=scratch,
            input_output_aliases=aliases,
            compiler_params=pltpu.CompilerParams(vmem_limit_bytes=8 * 1024 * 1024),
            cost_estimate=pl.CostEstimate(flops=flops, bytes_accessed=0, transcendentals=0),
            name=name,
        )(*args)

    def hbm(a):
        return pltpu.with_memory_space_constraint(a, pltpu.HBM)

    lines = ASTEPS * halves * cols + OSTEPS * sea_cols
    out = shape((8 * (rows // 4 * halves + sea_rows // 2), LANES), bf16)
    ends = shape((lines, LANES), bf16)
    send_a, send_b, ends_a, ends_b = call(
        pack_first, "pack_first", (out, out, ends, ends),
        [HBM] * 2, (VMEM,) * 4,
        [
            pltpu.VMEM((rows, 8, feat), f32),
            pltpu.VMEM((rows, 8, feat), f32),
            pltpu.VMEM((2, ASTEPS, cols, feat), f32),
            pltpu.VMEM(ocean.shape, f32),
            pltpu.SemaphoreType.DMA((5,)),
        ],
        args=(hbm(atmos), hbm(ocean)),
    )
    tile_a = lax.ppermute(send_a, AXES, tile_even)
    tile_b = lax.ppermute(send_b, AXES, tile_odd)
    rows_b = lax.ppermute(ends_b, AXES, sec_odd)
    rows_a = lax.ppermute(ends_a, AXES, sec_even)
    *planned, flags = call(
        functools.partial(plan, secs, tiles), "plan",
        (
            shape((80, 8 * count), bf16),
            shape((72, LANES), f32),
            shape((rows // 2 * cols, 2 * LANES), bf16),
            shape((LANES, 2 * LANES), bf16),
            shape((2 * LANES, cols), bf16),
            shape((rows * cols, LANES), f32),
        ),
        [pl.BlockSpec(memory_space=pl.ANY), HBM, HBM],
        (VMEM,) * 6,
        [
            pltpu.SMEM(tile_map.shape, jnp.int32),
            pltpu.VMEM(cloudy.shape, jnp.int32),
            pltpu.SemaphoreType.DMA((2,)),
        ],
        flops=1 << 30,
        args=(send_a, hbm(tile_map), hbm(cloudy)),
    )
    out = shape((8 * (halves + 2), LANES), bf16)
    send_a, send_b = call(
        functools.partial(pack_corners, tiles, rows, feat, sea_rows), "pack_corners", (out, out),
        [VMEM] * 2 + [pl.BlockSpec(memory_space=pl.ANY)], (VMEM, VMEM),
        args=(tile_a, tile_b, planned[1]),
    )
    corner_b = lax.ppermute(send_b, AXES, sec_odd)
    corner_a = lax.ppermute(send_a, AXES, sec_even)

    weights = (weight_in, weight_out, cloud_in, cloud_out)
    field, sums, ends = call(
        functools.partial(main, secs, tiles), "main",
        (shape(atmos.shape, f32), shape((4, 8, LANES), f32), shape((8, feat), f32)),
        [VMEM] * 11,
        (VMEM,) * 3,
        [pltpu.VMEM((rows * cols, feat), bf16), pltpu.VMEM((2, rows * cols, width), bf16)],
        flops=rows * cols * feat * width * 8,
        args=(atmos, flags, *weights, ocean, tile_a, tile_b, rows_b, rows_a),
    )
    field, pay = call(
        functools.partial(finish, secs), "finish",
        (shape(atmos.shape, f32), shape((count, 4, LANES), f32)),
        [VMEM] * 10,
        (VMEM,) * 2,
        [pltpu.VMEM((2, 16, width), bf16)],
        flops=16 * feat * width * 8,
        args=(field, flags, *weights, ends, corner_b, corner_a, sums),
        aliases={0: 0},
    )
    gathered = lax.all_to_all(pay, AXES, 0, 0)
    return call(
        functools.partial(final, secs, tiles), "final",
        (shape(atmos.shape, f32), shape(ocean.shape, f32), shape((rows, cols), f32)),
        [VMEM] * 14,
        (HBM,) * 3,
        [
            pltpu.VMEM(atmos.shape, f32),
            pltpu.VMEM(ocean.shape, f32),
            pltpu.VMEM(ocean.shape, f32),
            pltpu.VMEM((rows, cols), f32),
            pltpu.SemaphoreType.DMA((rows // 4 + 2,)),
        ],
        args=(gathered, *planned, field, ocean, tile_a, tile_b, rows_b, rows_a, corner_b, corner_a),
    )


def solution(mesh):
    placed = (
        P("sec", "tile", None),
        P("sec", "tile"),
        P(),
        P(),
        P(),
        P(),
        P("sec", "tile", None),
        P(),
    )
    return jax.shard_map(
        local,
        mesh=mesh,
        in_specs=placed,
        out_specs=(P("sec", "tile", None), P("sec", "tile", None), P("sec", "tile")),
        check_vma=False,
    )
```

```python
import functools

import jax
import jax.numpy as jnp
from jax import lax
from jax.experimental import pallas as pl
from jax.experimental.pallas import tpu as pltpu
from jax.sharding import PartitionSpec as P

ASTEPS = 2
OSTEPS = 4
LANES = 128

kappa_air = 0.2
kappa_sea = 0.2

f32 = jnp.float32
bf16 = jnp.bfloat16
VMEM = pl.BlockSpec(memory_space=pltpu.VMEM)
HBM = pl.BlockSpec(memory_space=pltpu.HBM)
AXES = ("sec", "tile")


def exchanges(secs, tiles):
    def whole(partner):
        return [
            (s * tiles + t, partner(s, t)[0] * tiles + partner(s, t)[1])
            for s in range(secs)
            for t in range(tiles)
        ]

    def odd_sec(s, t):
        if s in (0, secs - 1):
            return secs - 1 - s, t
        return (s + 1 if s % 2 else s - 1), t

    def odd_tile(s, t):
        if t in (0, tiles - 1):
            return s ^ 1, t
        return s, (t + 1 if t % 2 else t - 1)

    return (
        whole(lambda s, t: (s ^ 1, t)),
        whole(odd_sec),
        whole(lambda s, t: (s, t ^ 1)),
        whole(odd_tile),
    )


def sublane(shape):
    return lax.broadcasted_iota(jnp.int32, shape, len(shape) - 2)


def turn(v, shift):
    return v if shift % 8 == 0 else pltpu.roll(v, shift % 8, 0)


def halves_of(v):
    return [v[:, at : at + LANES] for at in range(0, v.shape[1], LANES)]


def pack_first(atmos, ocean, out_a, out_b, rows_a, rows_b, west, east, ends, sea, sems):
    rows, cols, feat = atmos.shape
    sea_rows, sea_cols, _ = ocean.shape
    copies = (
        pltpu.make_async_copy(atmos.at[:, 0:ASTEPS], west.at[:, 0:ASTEPS], sems.at[0]),
        pltpu.make_async_copy(
            atmos.at[:, cols - ASTEPS : cols], east.at[:, 8 - ASTEPS : 8], sems.at[1]
        ),
        pltpu.make_async_copy(ocean, sea, sems.at[2]),
        pltpu.make_async_copy(atmos.at[0:ASTEPS], ends.at[0], sems.at[3]),
        pltpu.make_async_copy(atmos.at[rows - ASTEPS : rows], ends.at[1], sems.at[4]),
    )
    for copy in copies:
        copy.start()
    for copy in copies[:3]:
        copy.wait()
    to_west, to_east = [], []
    sub = sublane((8, feat))
    for g in range(rows // 4):
        tile_w, tile_e = west[4 * g], turn(east[4 * g], 2)
        for k in range(1, 4):
            tile_w = jnp.where(sub < 2 * k, tile_w, turn(west[4 * g + k], 2 * k))
            tile_e = jnp.where(sub < 2 * k, tile_e, turn(east[4 * g + k], 2 * k + 2))
        to_west += halves_of(tile_w)
        to_east += halves_of(tile_e)
    low = sublane((8, LANES)) < 4
    for r in range(0, sea_rows, 2):
        to_west.append(jnp.where(low, sea[r, 0:8], turn(sea[r + 1, 0:8], 4)))
        to_east.append(
            jnp.where(low, turn(sea[r, sea_cols - 8 :], 4), sea[r + 1, sea_cols - 8 :])
        )
    to_west = jnp.concatenate(to_west, axis=0).astype(bf16)
    to_east = jnp.concatenate(to_east, axis=0).astype(bf16)
    even = lax.axis_index("tile") % 2 == 0
    out_a[...] = jnp.where(even, to_east, to_west)
    out_b[...] = jnp.where(even, to_west, to_east)
    for copy in copies[3:]:
        copy.wait()
    south = 1 - lax.axis_index("sec") % 2
    for out, end in ((rows_a, south), (rows_b, 1 - south)):
        parts = []
        for r in range(ASTEPS):
            parts += halves_of(ends[end, r])
        parts += [sea[end * (sea_rows - OSTEPS) + r] for r in range(OSTEPS)]
        out[...] = jnp.concatenate(parts, axis=0).astype(bf16)


class Sides:
    def __init__(self, tiles, rows, feat, tile_a, tile_b):
        t = lax.axis_index("tile")
        even = t % 2 == 0
        a, b = tile_a[...].astype(f32), tile_b[...].astype(f32)
        self.west = jnp.where(t > 0, jnp.where(even, b, a), 0.0)
        self.east = jnp.where(t < tiles - 1, jnp.where(even, a, b), 0.0)
        self.halves = feat // LANES
        self.sea_at = rows // 4 * self.halves
        self.low = sublane((8, LANES)) < 4

    def merge(self, tile, shift_w, shift_e):
        span = slice(8 * tile, 8 * tile + 8)
        return jnp.where(self.low, turn(self.east[span], shift_e), turn(self.west[span], shift_w))

    def air(self, r):
        g, k = r // 4, r % 4
        return jnp.concatenate(
            [self.merge(g * self.halves + h, -2 * k - 2, -2 * k) for h in range(self.halves)],
            axis=1,
        )

    def sea(self, r):
        return self.merge(self.sea_at + r // 2, 4 if r % 2 == 0 else 0, 4 * (r % 2))


def pack_corners(tiles, rows, feat, sea_rows, tile_a, tile_b, last, out_a, out_b):
    sides = Sides(tiles, rows, feat, tile_a, tile_b)

    sub = sublane((8, LANES))

    def corners(corner, near, inward):
        second, third = sides.sea(near + inward), sides.sea(near + 2 * inward)
        shared = jnp.where(sub == 2, turn(third, 2), jnp.where(sub == 5, turn(third, -2), second))
        parts = halves_of(sides.air(corner)) + [sides.sea(near), shared]
        return jnp.concatenate(parts, axis=0).astype(bf16)

    even = lax.axis_index("sec") % 2 == 0
    north, south = corners(0, 0, 1), corners(rows - 1, sea_rows - 1, -1)
    out_a[...] = jnp.where(even, south, north)
    out_b[...] = jnp.where(even, north, south)


def from_ends(secs, a, b):
    s = lax.axis_index("sec")
    even = s % 2 == 0
    a, b = a[...].astype(f32), b[...].astype(f32)
    north = jnp.where(s > 0, jnp.where(even, b, a), 0.0)
    south = jnp.where(s < secs - 1, jnp.where(even, a, b), 0.0)
    return north, south


def halves_beside(piece, at, count, halves):
    cut = [piece[at + h * count : at + (h + 1) * count] for h in range(halves)]
    return jnp.concatenate(cut, axis=1)


def five(up, mid, down):
    axis = mid.ndim - 2
    return mid + up + down + (pltpu.roll(mid, 1, axis) + pltpu.roll(mid, mid.shape[axis] - 1, axis))


def on_grid(tiles, row, own):
    t = lax.axis_index("tile")
    side = row[own:]
    sub = sublane(side.shape)
    ok = ((sub >= 4) | (t < tiles - 1)) & ((sub < 4) | (t > 0))
    return jnp.concatenate([row[:own], jnp.where(ok, side, 0.0)], axis=0)


def physics(x, layers, hid):
    first, second = layers
    block = 256
    for j in range(0, first.shape[1], block):
        u = jnp.dot(x, first[:, j : j + block], preferred_element_type=f32)
        hid[:, j : j + block] = (u + u * jnp.tanh(u)).astype(bf16)
    return lambda: jnp.dot(hid[...], second[...], preferred_element_type=f32)


def upright(line):
    n = line.shape[1]
    shape = (n, n)
    eye = sublane(shape) == lax.broadcasted_iota(jnp.int32, shape, 1)
    return jnp.sum(jnp.where(eye, jnp.broadcast_to(line, shape), 0.0), axis=1, keepdims=True)


def tile_iotas():
    return lax.broadcasted_iota(jnp.int32, (8, LANES), 1), sublane((8, LANES))


def add_row(means, new, r):
    lane, sub = tile_iotas()
    cols = new.shape[0]
    for k in range(cols // 8):
        hit = lane == (r // 2) * (cols // 2) + 4 * k + sub // 2
        for q in range(2):
            value = new[8 * k : 8 * k + 8, q * LANES : q * LANES + 1]
            means[q] = means[q] + jnp.where(hit, value, 0.0)


def plan(
    secs, tiles, first, tile_map, cloudy, blend, present, spots, cells, spread, flags,
    place, sems,
):
    map_copy = pltpu.make_async_copy(tile_map, place, sems.at[0])
    map_copy.start()
    rows, cols = cloudy.shape
    half_cols = cols // 2
    cell = sublane(spots.shape)
    at = lax.broadcasted_iota(jnp.int32, spots.shape, 1) % LANES
    spots[...] = (at == cell // cols * half_cols + cell % cols // 2).astype(f32).astype(bf16)
    at = lax.broadcasted_iota(jnp.int32, cells.shape, 1) % LANES
    cells[...] = (at == sublane(cells.shape)).astype(f32).astype(bf16)
    at = lax.broadcasted_iota(jnp.int32, spread.shape, 1) // 2
    spread[...] = (at == sublane(spread.shape) % half_cols).astype(f32).astype(bf16)
    count = secs * tiles
    s, t = lax.axis_index("sec"), lax.axis_index("tile")
    map_copy.wait()
    under = jnp.int32(0)
    for k in range(tiles):
        under = jnp.where(place[k] == t, k, under)

    def device(shape):
        row = sublane(shape)
        block, kind = row // 8, row % 8
        at_s = s + block // 3 - 1
        at_t = jnp.where(kind < 2, t, under) + block % 3 - 1
        ok = (at_s >= 0) & (at_s < secs) & (at_t >= 0) & (at_t < tiles)
        return kind, at_s * tiles, at_t, ok

    present[...] = device(present.shape)[3].astype(f32)
    shape = (blend.shape[0], blend.shape[1] // 2)
    kind, base, at_t, ok = device(shape)
    above = jnp.zeros(shape, jnp.int32)
    for k in range(tiles):
        above = jnp.where(at_t == k, place[k], above)
    column = lax.broadcasted_iota(jnp.int32, shape, 1)
    which, column = column // count, column % count
    here = jnp.where(column == base + at_t, 1.0, 0.0)
    there = jnp.where(column == base + above, 1.0, 0.0)
    top = jnp.where((kind == 1) | (kind == 3), 1.0, 7.0)
    parts = (
        jnp.where((kind == 0) | (kind == 2), -2.0, 0.0) * there,
        jnp.where(kind == 1, -2.0, 0.0) * there,
        top * here,
        jnp.where(kind == 1, 5.0, 0.0) * here,
    )
    total = jnp.zeros(shape, f32)
    for q, part in enumerate(parts):
        total = jnp.where(which == q, part, total)
    total = jnp.where(ok & (kind < 4), total, 0.0)
    blend[...] = jnp.concatenate([total, total], axis=1).astype(bf16)
    values = cloudy[...].astype(f32)
    for r in range(rows):
        flag = upright(values[r : r + 1, :])
        flags[r * cols : (r + 1) * cols, :] = jnp.broadcast_to(flag, (cols, LANES))


def main(
    secs, tiles, atmos, flags, w_in, w_out, c_in, c_out, ocean, tile_a, tile_b, rows_b, rows_a,
    field, sums, ends, xs, hid,
):
    rows, cols, feat = atmos.shape
    sea_rows, sea_cols, sea_feat = ocean.shape
    halves = feat // LANES
    s = lax.axis_index("sec")
    sides = Sides(tiles, rows, feat, tile_a, tile_b)
    north, south = from_ends(secs, rows_a, rows_b)

    def line(r):
        if 0 <= r < rows:
            return jnp.concatenate([atmos[r], sides.air(r)], axis=0)
        piece, k = (north, r + ASTEPS) if r < 0 else (south, r - rows)
        core = halves_beside(piece, k * halves * cols, cols, halves)
        return jnp.concatenate([core, jnp.zeros((8, feat), f32)], axis=0)

    lines, ones = [line(-2), line(-1)], []
    for r in range(-1, rows + 1):
        lines.append(line(r + 1))
        one = on_grid(tiles, five(*lines[-3:]), cols)
        if r == -1:
            one = jnp.where(s > 0, one, 0.0)
        if r == rows:
            one = jnp.where(s < secs - 1, one, 0.0)
        ones.append(one)
        if len(ones) >= 3:
            two = kappa_air**ASTEPS * five(*ones[-3:])[:cols]
            field[r - 1] = two
            xs[(r - 1) * cols : r * cols, :] = (0.5 * two).astype(bf16)
    ends[...] = jnp.zeros(ends.shape, f32)
    for k, r in enumerate((0, rows - 1)):
        ends[2 * k : 2 * k + 1, :] = field[r, 0:1, :]
        ends[2 * k + 1 : 2 * k + 2, :] = field[r, cols - 1 : cols, :]
    clear = physics(xs[...], (w_in, w_out), hid.at[0])()
    cloud = physics(xs[...], (c_in, c_out), hid.at[1])()
    means = [jnp.zeros((8, LANES), f32) for _ in range(2)]
    for r in range(rows):
        span = slice(r * cols, (r + 1) * cols)
        flag = jnp.concatenate([flags[span, :]] * halves, axis=1)
        new = field[r] + (clear[span] + flag * cloud[span]).astype(bf16).astype(f32)
        field[r] = new
        if r in (0, rows - 1):
            sub = sublane(new.shape)
            new = jnp.where((sub > 0) & (sub < cols - 1), new, 0.0)
        add_row(means, new, r)
    lane, sub = tile_iotas()
    tops = [jnp.zeros((8, LANES), f32) for _ in range(2)]
    for r in range(sea_rows):
        for k in range(sea_cols // 8):
            hit = lane == r * sea_cols + 8 * k + sub
            for q in range(2):
                at = q * (sea_feat // 2)
                value = ocean[r, 8 * k : 8 * k + 8, at : at + 1]
                tops[q] = tops[q] + jnp.where(hit, value, 0.0)
    for q, part in enumerate(means + tops):
        sums[q] = part


def finish(
    secs, old, all_flags, w_in, w_out, c_in, c_out, ends, corner_b, corner_a, sums,
    field, pay, hid,
):
    rows, cols, feat = field.shape
    halves = feat // LANES
    half_cols = cols // 2
    north, south = from_ends(secs, corner_a, corner_b)
    north = halves_beside(north, 0, 8, halves)
    south = halves_beside(south, 0, 8, halves)
    sub = sublane((8, feat))
    diagonal = jnp.zeros((8, feat), f32)
    for k, cell in enumerate((north[7:8], north[0:1], south[7:8], south[0:1])):
        diagonal = jnp.where(sub == k, cell, diagonal)
    state = ends[...] + 2.0 * kappa_air**ASTEPS * diagonal
    x = (0.5 * jnp.concatenate([state, jnp.zeros((8, feat), f32)], axis=0)).astype(bf16)
    clear = physics(x, (w_in, w_out), hid.at[0])
    cloud = physics(x, (c_in, c_out), hid.at[1])
    clear, cloud = clear(), cloud()
    places = ((0, 0), (0, cols - 1), (rows - 1, 0), (rows - 1, cols - 1))
    flag = jnp.zeros((8, LANES), f32)
    lane, sub_lane = tile_iotas()
    at = jnp.zeros((8, LANES), jnp.int32)
    for k, (r, c) in enumerate(places):
        cell = r * cols + c
        flag = jnp.where(sub_lane == k, all_flags[cell : cell + 1, :], flag)
        at = jnp.where(sub_lane == k, (r // 2) * half_cols + c // 2, at)
    flag = jnp.concatenate([flag] * halves, axis=1)
    new = state + (clear[:8] + flag * cloud[:8]).astype(bf16).astype(f32)
    for k, (r, c) in enumerate(places):
        field[r, c : c + 1, :] = new[k : k + 1]
    hit = (lane == at) & (sub_lane < 4)
    means = [
        sums[q] + jnp.where(hit, new[:, q * LANES : q * LANES + 1], 0.0) for q in range(2)
    ]
    parts = (0.25 * means[0], 0.25 * means[1], sums[2], sums[3])
    total = jnp.concatenate([jnp.sum(part, axis=0, keepdims=True) for part in parts], axis=0)
    pay[...] = jnp.broadcast_to(total[None], pay.shape)


def sea_steps(secs, tiles, rows, cols, feat, ocean, halos, out):
    sea_rows, sea_cols, sea_feat = ocean.shape
    tile_a, tile_b, rows_a, rows_b, corner_a, corner_b = halos
    s = lax.axis_index("sec")
    sides = Sides(tiles, rows, feat, tile_a, tile_b)
    cores = from_ends(secs, rows_a, rows_b)
    corners = from_ends(secs, corner_a, corner_b)
    halves = feat // LANES
    state = []
    for r in range(-OSTEPS, sea_rows + OSTEPS):
        if 0 <= r < sea_rows:
            core, side = ocean[r], sides.sea(r)
        else:
            end, k = (0, r + OSTEPS) if r < 0 else (1, r - sea_rows)
            at = ASTEPS * halves * cols + k * sea_cols
            core = cores[end][at : at + sea_cols]
            near, shared = (corners[end][8 * (halves + q) : 8 * (halves + q) + 8] for q in range(2))
            low = sublane(near.shape) < 4
            third = jnp.where(low, turn(shared, -2), turn(shared, 2))
            distance = -r if r < 0 else r - sea_rows + 1
            side = (near, shared, third, jnp.zeros(near.shape, f32))[distance - 1]
        state.append(jnp.concatenate([core, side], axis=0))
    for depth in reversed(range(OSTEPS)):
        state = [five(*state[k : k + 3]) for k in range(len(state) - 2)]
        if depth == 0:
            break
        for k, new in enumerate(state):
            new = on_grid(tiles, new, sea_cols)
            if k < depth:
                new = jnp.where(s > 0, new, 0.0)
            elif k >= depth + sea_rows:
                new = jnp.where(s < secs - 1, new, 0.0)
            state[k] = new
    for r in range(sea_rows):
        out[r] = kappa_sea**OSTEPS * state[r][:sea_cols]


def parts_of(v, count):
    parts = []
    for _ in range(count):
        part = v.astype(bf16)
        v = v - part.astype(f32)
        parts.append(part)
    return parts


def final(
    secs, tiles, gathered, blend, inside, spots, cells, spread, field, ocean,
    tile_a, tile_b, rows_b, rows_a, corner_b, corner_a,
    air_out, sea_out, back, stage, sea, sea_stage, back_stage, sems,
):
    rows, cols, feat = air_out.shape
    sea_rows, sea_cols, sea_feat = sea.shape
    halves = feat // LANES
    half_cols = cols // 2

    def upright_at(lines, *lanes):
        first = sublane((16, LANES)) == 0
        groups = [jnp.zeros((16, 2 * LANES), bf16)] * (LANES // 16)
        for line, at in zip(lines, lanes):
            whole = jnp.where(first, jnp.broadcast_to(line, first.shape), 0.0)
            groups[at // 16] = jnp.concatenate(parts_of(whole, 2), axis=1)
        return jnp.concatenate(groups, axis=0)

    def against(one_hot, values):
        return lax.dot_general(
            one_hot, values, (((1,), (1,)), ((), ())), preferred_element_type=f32
        )

    everything = jnp.concatenate([gathered[:, q, :] for q in range(4)], axis=0)
    everything = jnp.concatenate(parts_of(everything, 2), axis=0)
    blocks = jnp.dot(blend[...], everything, preferred_element_type=f32)
    keep = inside[...]
    blocks = {
        (k // 3, k % 3): (blocks[8 * k : 8 * k + 8], keep[8 * k : 8 * k + 8] > 0.0)
        for k in range(9)
    }
    landing = blocks[1, 1][0][3:4]
    patch = against(spots[...], upright_at([0.4 * landing], 0))
    rest = jnp.where(lax.broadcasted_iota(jnp.int32, (cols, LANES), 1) == 0, 0.6, 1.0)

    step_rows = 4
    copies = []
    for first in range(0, rows, step_rows):
        for r in range(first, first + step_rows):
            if r % 2 == 0:
                value = patch[(r // 2) * cols : (r // 2 + 1) * cols]
                added = (value, 0.5 * value)
            for h in range(halves):
                lanes = slice(h * LANES, (h + 1) * LANES)
                stage[r, :, lanes] = field[r, :, lanes] * rest + added[h]
        copies.append(
            pltpu.make_async_copy(
                stage.at[first : first + step_rows],
                air_out.at[first : first + step_rows],
                sems.at[first // step_rows],
            )
        )
        copies[-1].start()

    halos = tile_a, tile_b, rows_a, rows_b, corner_a, corner_b
    sea_steps(secs, tiles, rows, cols, feat, ocean, halos, sea)
    lane = tile_iotas()[0]
    first_c, last_c = lane % sea_cols == 0, lane % sea_cols == sea_cols - 1
    first_r, last_r = lane < sea_cols, lane >= LANES - sea_cols

    def roll(v, shift):
        return pltpu.roll(v, shift % LANES, 1)

    def step(old, wanted):
        def side(at, edge, shift, cross):
            near = roll(old[at][0], shift)
            return lambda other: (
                jnp.where(edge, roll(old[other][0], cross), near) if other in old else near
            )

        new = {}
        for i, j in wanted:
            v, ok = old[i, j]
            up = side((i, j), first_r, sea_cols, sea_cols)((i - 1, j))
            down = side((i, j), last_r, -sea_cols, -sea_cols)((i + 1, j))
            west = side((i, j), first_c, 1, 1 - sea_cols)((i, j - 1))
            east = side((i, j), last_c, -1, sea_cols - 1)((i, j + 1))
            v = v + (up + down) + (west + east)
            new[i, j] = (v if (i, j) == (1, 1) else jnp.where(ok, v, 0.0)), ok
        return new

    plus = [(0, 1), (1, 0), (1, 1), (1, 2), (2, 1)]
    for wanted in [list(blocks)] * (OSTEPS - 2) + [plus, [(1, 1)]]:
        blocks = step(blocks, wanted)
    mine = kappa_sea ** (OSTEPS + 1) * blocks[1, 1][0]
    own = upright_at([mine[0:1], mine[1:2]], 0, sea_feat // 2)
    own = against(cells[...], own)
    lane_s = lax.broadcasted_iota(jnp.int32, (sea_cols, sea_feat), 1)
    surface = jnp.logical_or(lane_s == 0, lane_s == sea_feat // 2)
    for r in range(sea_rows):
        new = own[r * sea_cols : (r + 1) * sea_cols]
        sea_stage[r] = jnp.where(surface, new, sea[r])
    copies.append(pltpu.make_async_copy(sea_stage, sea_out, sems.at[rows // step_rows]))
    copies[-1].start()

    returned = jnp.broadcast_to(mine[2:3], (rows, LANES))
    lane_b = lax.broadcasted_iota(jnp.int32, (rows, LANES), 1)
    lines = jnp.where(lane_b // half_cols == sublane((rows, LANES)) // 2, returned, 0.0)
    lines = jnp.concatenate(parts_of(lines, 2), axis=1)
    back_stage[...] = jnp.dot(lines, spread[...], preferred_element_type=f32)
    copies.append(pltpu.make_async_copy(back_stage, back, sems.at[rows // step_rows + 1]))
    copies[-1].start()
    for copy in copies:
        copy.wait()


def local(atmos, cloudy, weight_in, weight_out, cloud_in, cloud_out, ocean, tile_map):
    rows, cols, feat = atmos.shape
    sea_rows, sea_cols, sea_feat = ocean.shape
    secs, tiles = lax.axis_size("sec"), lax.axis_size("tile")
    count = secs * tiles
    halves = feat // LANES
    width = weight_in.shape[1]
    sec_even, sec_odd, tile_even, tile_odd = exchanges(secs, tiles)
    shape = jax.ShapeDtypeStruct

    def call(
        body, name, out_shape, in_specs, out_specs, scratch=(), flops=0, args=(), aliases={}
    ):
        return pl.pallas_call(
            body,
            out_shape=out_shape,
            in_specs=in_specs,
            out_specs=out_specs,
            scratch_shapes=scratch,
            input_output_aliases=aliases,
            compiler_params=pltpu.CompilerParams(vmem_limit_bytes=8 * 1024 * 1024),
            cost_estimate=pl.CostEstimate(flops=flops, bytes_accessed=0, transcendentals=0),
            name=name,
        )(*args)

    def hbm(a):
        return pltpu.with_memory_space_constraint(a, pltpu.HBM)

    lines = ASTEPS * halves * cols + OSTEPS * sea_cols
    out = shape((8 * (rows // 4 * halves + sea_rows // 2), LANES), bf16)
    ends = shape((lines, LANES), bf16)
    send_a, send_b, ends_a, ends_b = call(
        pack_first, "pack_first", (out, out, ends, ends),
        [HBM] * 2, (VMEM,) * 4,
        [
            pltpu.VMEM((rows, 8, feat), f32),
            pltpu.VMEM((rows, 8, feat), f32),
            pltpu.VMEM((2, ASTEPS, cols, feat), f32),
            pltpu.VMEM(ocean.shape, f32),
            pltpu.SemaphoreType.DMA((5,)),
        ],
        args=(hbm(atmos), hbm(ocean)),
    )
    tile_a = lax.ppermute(send_a, AXES, tile_even)
    tile_b = lax.ppermute(send_b, AXES, tile_odd)
    rows_b = lax.ppermute(ends_b, AXES, sec_odd)
    rows_a = lax.ppermute(ends_a, AXES, sec_even)
    *planned, flags = call(
        functools.partial(plan, secs, tiles), "plan",
        (
            shape((80, 8 * count), bf16),
            shape((72, LANES), f32),
            shape((rows // 2 * cols, 2 * LANES), bf16),
            shape((LANES, 2 * LANES), bf16),
            shape((2 * LANES, cols), bf16),
            shape((rows * cols, LANES), f32),
        ),
        [pl.BlockSpec(memory_space=pl.ANY), HBM, VMEM],
        (VMEM,) * 6,
        [
            pltpu.SMEM(tile_map.shape, jnp.int32),
            pltpu.SemaphoreType.DMA((1,)),
        ],
        flops=1 << 30,
        args=(send_a, hbm(tile_map), cloudy),
    )
    out = shape((8 * (halves + 2), LANES), bf16)
    send_a, send_b = call(
        functools.partial(pack_corners, tiles, rows, feat, sea_rows), "pack_corners", (out, out),
        [VMEM] * 2 + [pl.BlockSpec(memory_space=pl.ANY)], (VMEM, VMEM),
        args=(tile_a, tile_b, planned[1]),
    )
    corner_b = lax.ppermute(send_b, AXES, sec_odd)
    corner_a = lax.ppermute(send_a, AXES, sec_even)

    weights = (weight_in, weight_out, cloud_in, cloud_out)
    field, sums, ends = call(
        functools.partial(main, secs, tiles), "main",
        (shape(atmos.shape, f32), shape((4, 8, LANES), f32), shape((8, feat), f32)),
        [VMEM] * 11,
        (VMEM,) * 3,
        [pltpu.VMEM((rows * cols, feat), bf16), pltpu.VMEM((2, rows * cols, width), bf16)],
        flops=rows * cols * feat * width * 8,
        args=(atmos, flags, *weights, ocean, tile_a, tile_b, rows_b, rows_a),
    )
    field, pay = call(
        functools.partial(finish, secs), "finish",
        (shape(atmos.shape, f32), shape((count, 4, LANES), f32)),
        [VMEM] * 10,
        (VMEM,) * 2,
        [pltpu.VMEM((2, 16, width), bf16)],
        flops=16 * feat * width * 8,
        args=(field, flags, *weights, ends, corner_b, corner_a, sums),
        aliases={0: 0},
    )
    gathered = lax.all_to_all(pay, AXES, 0, 0)
    return call(
        functools.partial(final, secs, tiles), "final",
        (shape(atmos.shape, f32), shape(ocean.shape, f32), shape((rows, cols), f32)),
        [VMEM] * 14,
        (HBM,) * 3,
        [
            pltpu.VMEM(atmos.shape, f32),
            pltpu.VMEM(ocean.shape, f32),
            pltpu.VMEM(ocean.shape, f32),
            pltpu.VMEM((rows, cols), f32),
            pltpu.SemaphoreType.DMA((rows // 4 + 2,)),
        ],
        args=(gathered, *planned, field, ocean, tile_a, tile_b, rows_b, rows_a, corner_b, corner_a),
    )


def solution(mesh):
    placed = (
        P("sec", "tile", None),
        P("sec", "tile"),
        P(),
        P(),
        P(),
        P(),
        P("sec", "tile", None),
        P(),
    )
    return jax.shard_map(
        local,
        mesh=mesh,
        in_specs=placed,
        out_specs=(P("sec", "tile", None), P("sec", "tile", None), P("sec", "tile")),
        check_vma=False,
    )
```

```python
import functools

import jax
import jax.numpy as jnp
from jax import lax
from jax.experimental import pallas as pl
from jax.experimental.pallas import tpu as pltpu
from jax.sharding import PartitionSpec as P

ASTEPS = 2
OSTEPS = 4
LANES = 128

kappa_air = 0.2
kappa_sea = 0.2

f32 = jnp.float32
bf16 = jnp.bfloat16
VMEM = pl.BlockSpec(memory_space=pltpu.VMEM)
HBM = pl.BlockSpec(memory_space=pltpu.HBM)
AXES = ("sec", "tile")


def exchanges(secs, tiles):
    def whole(partner):
        return [
            (s * tiles + t, partner(s, t)[0] * tiles + partner(s, t)[1])
            for s in range(secs)
            for t in range(tiles)
        ]

    def odd_sec(s, t):
        if s in (0, secs - 1):
            return secs - 1 - s, t
        return (s + 1 if s % 2 else s - 1), t

    def odd_tile(s, t):
        if t in (0, tiles - 1):
            return s ^ 1, t
        return s, (t + 1 if t % 2 else t - 1)

    return (
        whole(lambda s, t: (s ^ 1, t)),
        whole(odd_sec),
        whole(lambda s, t: (s, t ^ 1)),
        whole(odd_tile),
    )


def sublane(shape):
    return lax.broadcasted_iota(jnp.int32, shape, len(shape) - 2)


def turn(v, shift):
    return v if shift % 8 == 0 else pltpu.roll(v, shift % 8, 0)


def halves_of(v):
    return [v[:, at : at + LANES] for at in range(0, v.shape[1], LANES)]


def pack_first(atmos, ocean, out_a, out_b, rows_a, rows_b, west, east, ends, sea, sems):
    rows, cols, feat = atmos.shape
    sea_rows, sea_cols, _ = ocean.shape
    copies = (
        pltpu.make_async_copy(atmos.at[:, 0:ASTEPS], west.at[:, 0:ASTEPS], sems.at[0]),
        pltpu.make_async_copy(
            atmos.at[:, cols - ASTEPS : cols], east.at[:, 8 - ASTEPS : 8], sems.at[1]
        ),
        pltpu.make_async_copy(ocean, sea, sems.at[2]),
        pltpu.make_async_copy(atmos.at[0:ASTEPS], ends.at[0], sems.at[3]),
        pltpu.make_async_copy(atmos.at[rows - ASTEPS : rows], ends.at[1], sems.at[4]),
    )
    for copy in copies:
        copy.start()
    for copy in copies[:3]:
        copy.wait()
    to_west, to_east = [], []
    sub = sublane((8, feat))
    for g in range(rows // 4):
        tile_w, tile_e = west[4 * g], turn(east[4 * g], 2)
        for k in range(1, 4):
            tile_w = jnp.where(sub < 2 * k, tile_w, turn(west[4 * g + k], 2 * k))
            tile_e = jnp.where(sub < 2 * k, tile_e, turn(east[4 * g + k], 2 * k + 2))
        to_west += halves_of(tile_w)
        to_east += halves_of(tile_e)
    low = sublane((8, LANES)) < 4
    for r in range(0, sea_rows, 2):
        to_west.append(jnp.where(low, sea[r, 0:8], turn(sea[r + 1, 0:8], 4)))
        to_east.append(
            jnp.where(low, turn(sea[r, sea_cols - 8 :], 4), sea[r + 1, sea_cols - 8 :])
        )
    to_west = jnp.concatenate(to_west, axis=0).astype(bf16)
    to_east = jnp.concatenate(to_east, axis=0).astype(bf16)
    even = lax.axis_index("tile") % 2 == 0
    out_a[...] = jnp.where(even, to_east, to_west)
    out_b[...] = jnp.where(even, to_west, to_east)
    for copy in copies[3:]:
        copy.wait()
    south = 1 - lax.axis_index("sec") % 2
    for out, end in ((rows_a, south), (rows_b, 1 - south)):
        parts = []
        for r in range(ASTEPS):
            parts += halves_of(ends[end, r])
        parts += [sea[end * (sea_rows - OSTEPS) + r] for r in range(OSTEPS)]
        out[...] = jnp.concatenate(parts, axis=0).astype(bf16)


class Sides:
    def __init__(self, tiles, rows, feat, tile_a, tile_b):
        t = lax.axis_index("tile")
        even = t % 2 == 0
        a, b = tile_a[...].astype(f32), tile_b[...].astype(f32)
        self.west = jnp.where(t > 0, jnp.where(even, b, a), 0.0)
        self.east = jnp.where(t < tiles - 1, jnp.where(even, a, b), 0.0)
        self.halves = feat // LANES
        self.sea_at = rows // 4 * self.halves
        self.low = sublane((8, LANES)) < 4

    def merge(self, tile, shift_w, shift_e):
        span = slice(8 * tile, 8 * tile + 8)
        return jnp.where(self.low, turn(self.east[span], shift_e), turn(self.west[span], shift_w))

    def air(self, r):
        g, k = r // 4, r % 4
        return jnp.concatenate(
            [self.merge(g * self.halves + h, -2 * k - 2, -2 * k) for h in range(self.halves)],
            axis=1,
        )

    def sea(self, r):
        return self.merge(self.sea_at + r // 2, 4 if r % 2 == 0 else 0, 4 * (r % 2))


def pack_corners(tiles, rows, feat, sea_rows, tile_a, tile_b, last, out_a, out_b):
    sides = Sides(tiles, rows, feat, tile_a, tile_b)

    sub = sublane((8, LANES))

    def corners(corner, near, inward):
        second, third = sides.sea(near + inward), sides.sea(near + 2 * inward)
        shared = jnp.where(sub == 2, turn(third, 2), jnp.where(sub == 5, turn(third, -2), second))
        parts = halves_of(sides.air(corner)) + [sides.sea(near), shared]
        return jnp.concatenate(parts, axis=0).astype(bf16)

    even = lax.axis_index("sec") % 2 == 0
    north, south = corners(0, 0, 1), corners(rows - 1, sea_rows - 1, -1)
    out_a[...] = jnp.where(even, south, north)
    out_b[...] = jnp.where(even, north, south)


def from_ends(secs, a, b):
    s = lax.axis_index("sec")
    even = s % 2 == 0
    a, b = a[...].astype(f32), b[...].astype(f32)
    north = jnp.where(s > 0, jnp.where(even, b, a), 0.0)
    south = jnp.where(s < secs - 1, jnp.where(even, a, b), 0.0)
    return north, south


def halves_beside(piece, at, count, halves):
    cut = [piece[at + h * count : at + (h + 1) * count] for h in range(halves)]
    return jnp.concatenate(cut, axis=1)


def five(up, mid, down):
    axis = mid.ndim - 2
    return mid + up + down + (pltpu.roll(mid, 1, axis) + pltpu.roll(mid, mid.shape[axis] - 1, axis))


def on_grid(tiles, row, own):
    t = lax.axis_index("tile")
    side = row[own:]
    sub = sublane(side.shape)
    ok = ((sub >= 4) | (t < tiles - 1)) & ((sub < 4) | (t > 0))
    return jnp.concatenate([row[:own], jnp.where(ok, side, 0.0)], axis=0)


def physics(x, layers, hid):
    first, second = layers
    block = 512
    for j in range(0, first.shape[1], block):
        u = jnp.dot(x, first[:, j : j + block], preferred_element_type=f32)
        hid[:, j : j + block] = (u + u * jnp.tanh(u)).astype(bf16)
    return lambda: jnp.dot(hid[...], second[...], preferred_element_type=f32)


def upright(line):
    n = line.shape[1]
    shape = (n, n)
    eye = sublane(shape) == lax.broadcasted_iota(jnp.int32, shape, 1)
    return jnp.sum(jnp.where(eye, jnp.broadcast_to(line, shape), 0.0), axis=1, keepdims=True)


def tile_iotas():
    return lax.broadcasted_iota(jnp.int32, (8, LANES), 1), sublane((8, LANES))


def add_row(means, new, r):
    lane, sub = tile_iotas()
    cols = new.shape[0]
    for k in range(cols // 8):
        hit = lane == (r // 2) * (cols // 2) + 4 * k + sub // 2
        for q in range(2):
            value = new[8 * k : 8 * k + 8, q * LANES : q * LANES + 1]
            means[q] = means[q] + jnp.where(hit, value, 0.0)


def plan(
    secs, tiles, first, tile_map, cloudy, blend, present, spots, cells, spread, flags,
    place, sems,
):
    map_copy = pltpu.make_async_copy(tile_map, place, sems.at[0])
    map_copy.start()
    rows, cols = cloudy.shape
    half_cols = cols // 2
    cell = sublane(spots.shape)
    at = lax.broadcasted_iota(jnp.int32, spots.shape, 1) % LANES
    spots[...] = (at == cell // cols * half_cols + cell % cols // 2).astype(f32).astype(bf16)
    at = lax.broadcasted_iota(jnp.int32, cells.shape, 1) % LANES
    cells[...] = (at == sublane(cells.shape)).astype(f32).astype(bf16)
    at = lax.broadcasted_iota(jnp.int32, spread.shape, 1) // 2
    spread[...] = (at == sublane(spread.shape) % half_cols).astype(f32).astype(bf16)
    count = secs * tiles
    s, t = lax.axis_index("sec"), lax.axis_index("tile")
    map_copy.wait()
    under = jnp.int32(0)
    for k in range(tiles):
        under = jnp.where(place[k] == t, k, under)

    def device(shape):
        row = sublane(shape)
        block, kind = row // 8, row % 8
        at_s = s + block // 3 - 1
        at_t = jnp.where(kind < 2, t, under) + block % 3 - 1
        ok = (at_s >= 0) & (at_s < secs) & (at_t >= 0) & (at_t < tiles)
        return kind, at_s * tiles, at_t, ok

    present[...] = device(present.shape)[3].astype(f32)
    shape = (blend.shape[0], blend.shape[1] // 2)
    kind, base, at_t, ok = device(shape)
    above = jnp.zeros(shape, jnp.int32)
    for k in range(tiles):
        above = jnp.where(at_t == k, place[k], above)
    column = lax.broadcasted_iota(jnp.int32, shape, 1)
    which, column = column // count, column % count
    here = jnp.where(column == base + at_t, 1.0, 0.0)
    there = jnp.where(column == base + above, 1.0, 0.0)
    top = jnp.where((kind == 1) | (kind == 3), 1.0, 7.0)
    parts = (
        jnp.where((kind == 0) | (kind == 2), -2.0, 0.0) * there,
        jnp.where(kind == 1, -2.0, 0.0) * there,
        top * here,
        jnp.where(kind == 1, 5.0, 0.0) * here,
    )
    total = jnp.zeros(shape, f32)
    for q, part in enumerate(parts):
        total = jnp.where(which == q, part, total)
    total = jnp.where(ok & (kind < 4), total, 0.0)
    blend[...] = jnp.concatenate([total, total], axis=1).astype(bf16)
    values = cloudy[...].astype(f32)
    for r in range(rows):
        flag = upright(values[r : r + 1, :])
        flags[r * cols : (r + 1) * cols, :] = jnp.broadcast_to(flag, (cols, LANES))


def main(
    secs, tiles, atmos, flags, w_in, w_out, c_in, c_out, ocean, tile_a, tile_b, rows_b, rows_a,
    field, sums, ends, xs, hid,
):
    rows, cols, feat = atmos.shape
    sea_rows, sea_cols, sea_feat = ocean.shape
    halves = feat // LANES
    s = lax.axis_index("sec")
    sides = Sides(tiles, rows, feat, tile_a, tile_b)
    north, south = from_ends(secs, rows_a, rows_b)

    def line(r):
        if 0 <= r < rows:
            return jnp.concatenate([atmos[r], sides.air(r)], axis=0)
        piece, k = (north, r + ASTEPS) if r < 0 else (south, r - rows)
        core = halves_beside(piece, k * halves * cols, cols, halves)
        return jnp.concatenate([core, jnp.zeros((8, feat), f32)], axis=0)

    lines, ones = [line(-2), line(-1)], []
    for r in range(-1, rows + 1):
        lines.append(line(r + 1))
        one = on_grid(tiles, five(*lines[-3:]), cols)
        if r == -1:
            one = jnp.where(s > 0, one, 0.0)
        if r == rows:
            one = jnp.where(s < secs - 1, one, 0.0)
        ones.append(one)
        if len(ones) >= 3:
            two = kappa_air**ASTEPS * five(*ones[-3:])[:cols]
            field[r - 1] = two
            xs[(r - 1) * cols : r * cols, :] = (0.5 * two).astype(bf16)
    ends[...] = jnp.zeros(ends.shape, f32)
    for k, r in enumerate((0, rows - 1)):
        ends[2 * k : 2 * k + 1, :] = field[r, 0:1, :]
        ends[2 * k + 1 : 2 * k + 2, :] = field[r, cols - 1 : cols, :]
    clear = physics(xs[...], (w_in, w_out), hid.at[0])()
    cloud = physics(xs[...], (c_in, c_out), hid.at[1])()
    means = [jnp.zeros((8, LANES), f32) for _ in range(2)]
    for r in range(rows):
        span = slice(r * cols, (r + 1) * cols)
        flag = jnp.concatenate([flags[span, :]] * halves, axis=1)
        new = field[r] + (clear[span] + flag * cloud[span]).astype(bf16).astype(f32)
        field[r] = new
        if r in (0, rows - 1):
            sub = sublane(new.shape)
            new = jnp.where((sub > 0) & (sub < cols - 1), new, 0.0)
        add_row(means, new, r)
    lane, sub = tile_iotas()
    tops = [jnp.zeros((8, LANES), f32) for _ in range(2)]
    for r in range(sea_rows):
        for k in range(sea_cols // 8):
            hit = lane == r * sea_cols + 8 * k + sub
            for q in range(2):
                at = q * (sea_feat // 2)
                value = ocean[r, 8 * k : 8 * k + 8, at : at + 1]
                tops[q] = tops[q] + jnp.where(hit, value, 0.0)
    for q, part in enumerate(means + tops):
        sums[q] = part


def finish(
    secs, old, all_flags, w_in, w_out, c_in, c_out, ends, corner_b, corner_a, sums,
    field, pay, hid,
):
    rows, cols, feat = field.shape
    halves = feat // LANES
    half_cols = cols // 2
    north, south = from_ends(secs, corner_a, corner_b)
    north = halves_beside(north, 0, 8, halves)
    south = halves_beside(south, 0, 8, halves)
    sub = sublane((8, feat))
    diagonal = jnp.zeros((8, feat), f32)
    for k, cell in enumerate((north[7:8], north[0:1], south[7:8], south[0:1])):
        diagonal = jnp.where(sub == k, cell, diagonal)
    state = ends[...] + 2.0 * kappa_air**ASTEPS * diagonal
    x = (0.5 * jnp.concatenate([state, jnp.zeros((8, feat), f32)], axis=0)).astype(bf16)
    clear = physics(x, (w_in, w_out), hid.at[0])
    cloud = physics(x, (c_in, c_out), hid.at[1])
    clear, cloud = clear(), cloud()
    places = ((0, 0), (0, cols - 1), (rows - 1, 0), (rows - 1, cols - 1))
    flag = jnp.zeros((8, LANES), f32)
    lane, sub_lane = tile_iotas()
    at = jnp.zeros((8, LANES), jnp.int32)
    for k, (r, c) in enumerate(places):
        cell = r * cols + c
        flag = jnp.where(sub_lane == k, all_flags[cell : cell + 1, :], flag)
        at = jnp.where(sub_lane == k, (r // 2) * half_cols + c // 2, at)
    flag = jnp.concatenate([flag] * halves, axis=1)
    new = state + (clear[:8] + flag * cloud[:8]).astype(bf16).astype(f32)
    for k, (r, c) in enumerate(places):
        field[r, c : c + 1, :] = new[k : k + 1]
    hit = (lane == at) & (sub_lane < 4)
    means = [
        sums[q] + jnp.where(hit, new[:, q * LANES : q * LANES + 1], 0.0) for q in range(2)
    ]
    parts = (0.25 * means[0], 0.25 * means[1], sums[2], sums[3])
    total = jnp.concatenate([jnp.sum(part, axis=0, keepdims=True) for part in parts], axis=0)
    pay[...] = jnp.broadcast_to(total[None], pay.shape)


def sea_steps(secs, tiles, rows, cols, feat, ocean, halos, out):
    sea_rows, sea_cols, sea_feat = ocean.shape
    tile_a, tile_b, rows_a, rows_b, corner_a, corner_b = halos
    s = lax.axis_index("sec")
    sides = Sides(tiles, rows, feat, tile_a, tile_b)
    cores = from_ends(secs, rows_a, rows_b)
    corners = from_ends(secs, corner_a, corner_b)
    halves = feat // LANES
    state = []
    for r in range(-OSTEPS, sea_rows + OSTEPS):
        if 0 <= r < sea_rows:
            core, side = ocean[r], sides.sea(r)
        else:
            end, k = (0, r + OSTEPS) if r < 0 else (1, r - sea_rows)
            at = ASTEPS * halves * cols + k * sea_cols
            core = cores[end][at : at + sea_cols]
            near, shared = (corners[end][8 * (halves + q) : 8 * (halves + q) + 8] for q in range(2))
            low = sublane(near.shape) < 4
            third = jnp.where(low, turn(shared, -2), turn(shared, 2))
            distance = -r if r < 0 else r - sea_rows + 1
            side = (near, shared, third, jnp.zeros(near.shape, f32))[distance - 1]
        state.append(jnp.concatenate([core, side], axis=0))
    for depth in reversed(range(OSTEPS)):
        state = [five(*state[k : k + 3]) for k in range(len(state) - 2)]
        if depth == 0:
            break
        for k, new in enumerate(state):
            new = on_grid(tiles, new, sea_cols)
            if k < depth:
                new = jnp.where(s > 0, new, 0.0)
            elif k >= depth + sea_rows:
                new = jnp.where(s < secs - 1, new, 0.0)
            state[k] = new
    for r in range(sea_rows):
        out[r] = kappa_sea**OSTEPS * state[r][:sea_cols]


def parts_of(v, count):
    parts = []
    for _ in range(count):
        part = v.astype(bf16)
        v = v - part.astype(f32)
        parts.append(part)
    return parts


def final(
    secs, tiles, gathered, blend, inside, spots, cells, spread, field, ocean,
    tile_a, tile_b, rows_b, rows_a, corner_b, corner_a,
    air_out, sea_out, back, stage, sea, sea_stage, back_stage, sems,
):
    rows, cols, feat = air_out.shape
    sea_rows, sea_cols, sea_feat = sea.shape
    halves = feat // LANES
    half_cols = cols // 2

    def upright_at(lines, *lanes):
        first = sublane((16, LANES)) == 0
        groups = [jnp.zeros((16, 2 * LANES), bf16)] * (LANES // 16)
        for line, at in zip(lines, lanes):
            whole = jnp.where(first, jnp.broadcast_to(line, first.shape), 0.0)
            groups[at // 16] = jnp.concatenate(parts_of(whole, 2), axis=1)
        return jnp.concatenate(groups, axis=0)

    def against(one_hot, values):
        return lax.dot_general(
            one_hot, values, (((1,), (1,)), ((), ())), preferred_element_type=f32
        )

    everything = jnp.concatenate([gathered[:, q, :] for q in range(4)], axis=0)
    everything = jnp.concatenate(parts_of(everything, 2), axis=0)
    blocks = jnp.dot(blend[...], everything, preferred_element_type=f32)
    keep = inside[...]
    blocks = {
        (k // 3, k % 3): (blocks[8 * k : 8 * k + 8], keep[8 * k : 8 * k + 8] > 0.0)
        for k in range(9)
    }
    landing = blocks[1, 1][0][3:4]
    patch = against(spots[...], upright_at([0.4 * landing], 0))
    rest = jnp.where(lax.broadcasted_iota(jnp.int32, (cols, LANES), 1) == 0, 0.6, 1.0)

    step_rows = 4
    copies = []
    for first in range(0, rows, step_rows):
        for r in range(first, first + step_rows):
            if r % 2 == 0:
                value = patch[(r // 2) * cols : (r // 2 + 1) * cols]
                added = (value, 0.5 * value)
            for h in range(halves):
                lanes = slice(h * LANES, (h + 1) * LANES)
                stage[r, :, lanes] = field[r, :, lanes] * rest + added[h]
        copies.append(
            pltpu.make_async_copy(
                stage.at[first : first + step_rows],
                air_out.at[first : first + step_rows],
                sems.at[first // step_rows],
            )
        )
        copies[-1].start()

    halos = tile_a, tile_b, rows_a, rows_b, corner_a, corner_b
    sea_steps(secs, tiles, rows, cols, feat, ocean, halos, sea)
    lane = tile_iotas()[0]
    first_c, last_c = lane % sea_cols == 0, lane % sea_cols == sea_cols - 1
    first_r, last_r = lane < sea_cols, lane >= LANES - sea_cols

    def roll(v, shift):
        return pltpu.roll(v, shift % LANES, 1)

    def step(old, wanted):
        def side(at, edge, shift, cross):
            near = roll(old[at][0], shift)
            return lambda other: (
                jnp.where(edge, roll(old[other][0], cross), near) if other in old else near
            )

        new = {}
        for i, j in wanted:
            v, ok = old[i, j]
            up = side((i, j), first_r, sea_cols, sea_cols)((i - 1, j))
            down = side((i, j), last_r, -sea_cols, -sea_cols)((i + 1, j))
            west = side((i, j), first_c, 1, 1 - sea_cols)((i, j - 1))
            east = side((i, j), last_c, -1, sea_cols - 1)((i, j + 1))
            v = v + (up + down) + (west + east)
            new[i, j] = (v if (i, j) == (1, 1) else jnp.where(ok, v, 0.0)), ok
        return new

    plus = [(0, 1), (1, 0), (1, 1), (1, 2), (2, 1)]
    for wanted in [list(blocks)] * (OSTEPS - 2) + [plus, [(1, 1)]]:
        blocks = step(blocks, wanted)
    mine = kappa_sea ** (OSTEPS + 1) * blocks[1, 1][0]
    own = upright_at([mine[0:1], mine[1:2]], 0, sea_feat // 2)
    own = against(cells[...], own)
    lane_s = lax.broadcasted_iota(jnp.int32, (sea_cols, sea_feat), 1)
    surface = jnp.logical_or(lane_s == 0, lane_s == sea_feat // 2)
    for r in range(sea_rows):
        new = own[r * sea_cols : (r + 1) * sea_cols]
        sea_stage[r] = jnp.where(surface, new, sea[r])
    copies.append(pltpu.make_async_copy(sea_stage, sea_out, sems.at[rows // step_rows]))
    copies[-1].start()

    returned = jnp.broadcast_to(mine[2:3], (rows, LANES))
    lane_b = lax.broadcasted_iota(jnp.int32, (rows, LANES), 1)
    lines = jnp.where(lane_b // half_cols == sublane((rows, LANES)) // 2, returned, 0.0)
    lines = jnp.concatenate(parts_of(lines, 2), axis=1)
    back_stage[...] = jnp.dot(lines, spread[...], preferred_element_type=f32)
    copies.append(pltpu.make_async_copy(back_stage, back, sems.at[rows // step_rows + 1]))
    copies[-1].start()
    for copy in copies:
        copy.wait()


def local(atmos, cloudy, weight_in, weight_out, cloud_in, cloud_out, ocean, tile_map):
    rows, cols, feat = atmos.shape
    sea_rows, sea_cols, sea_feat = ocean.shape
    secs, tiles = lax.axis_size("sec"), lax.axis_size("tile")
    count = secs * tiles
    halves = feat // LANES
    width = weight_in.shape[1]
    sec_even, sec_odd, tile_even, tile_odd = exchanges(secs, tiles)
    shape = jax.ShapeDtypeStruct

    def call(
        body, name, out_shape, in_specs, out_specs, scratch=(), flops=0, args=(), aliases={}
    ):
        return pl.pallas_call(
            body,
            out_shape=out_shape,
            in_specs=in_specs,
            out_specs=out_specs,
            scratch_shapes=scratch,
            input_output_aliases=aliases,
            compiler_params=pltpu.CompilerParams(vmem_limit_bytes=8 * 1024 * 1024),
            cost_estimate=pl.CostEstimate(flops=flops, bytes_accessed=0, transcendentals=0),
            name=name,
        )(*args)

    def hbm(a):
        return pltpu.with_memory_space_constraint(a, pltpu.HBM)

    lines = ASTEPS * halves * cols + OSTEPS * sea_cols
    out = shape((8 * (rows // 4 * halves + sea_rows // 2), LANES), bf16)
    ends = shape((lines, LANES), bf16)
    send_a, send_b, ends_a, ends_b = call(
        pack_first, "pack_first", (out, out, ends, ends),
        [HBM] * 2, (VMEM,) * 4,
        [
            pltpu.VMEM((rows, 8, feat), f32),
            pltpu.VMEM((rows, 8, feat), f32),
            pltpu.VMEM((2, ASTEPS, cols, feat), f32),
            pltpu.VMEM(ocean.shape, f32),
            pltpu.SemaphoreType.DMA((5,)),
        ],
        args=(hbm(atmos), hbm(ocean)),
    )
    tile_a = lax.ppermute(send_a, AXES, tile_even)
    tile_b = lax.ppermute(send_b, AXES, tile_odd)
    rows_b = lax.ppermute(ends_b, AXES, sec_odd)
    rows_a = lax.ppermute(ends_a, AXES, sec_even)
    *planned, flags = call(
        functools.partial(plan, secs, tiles), "plan",
        (
            shape((80, 8 * count), bf16),
            shape((72, LANES), f32),
            shape((rows // 2 * cols, 2 * LANES), bf16),
            shape((LANES, 2 * LANES), bf16),
            shape((2 * LANES, cols), bf16),
            shape((rows * cols, LANES), f32),
        ),
        [pl.BlockSpec(memory_space=pl.ANY), HBM, VMEM],
        (VMEM,) * 6,
        [
            pltpu.SMEM(tile_map.shape, jnp.int32),
            pltpu.SemaphoreType.DMA((1,)),
        ],
        flops=1 << 30,
        args=(send_a, hbm(tile_map), cloudy),
    )
    out = shape((8 * (halves + 2), LANES), bf16)
    send_a, send_b = call(
        functools.partial(pack_corners, tiles, rows, feat, sea_rows), "pack_corners", (out, out),
        [VMEM] * 2 + [pl.BlockSpec(memory_space=pl.ANY)], (VMEM, VMEM),
        args=(tile_a, tile_b, planned[1]),
    )
    corner_b = lax.ppermute(send_b, AXES, sec_odd)
    corner_a = lax.ppermute(send_a, AXES, sec_even)

    weights = (weight_in, weight_out, cloud_in, cloud_out)
    field, sums, ends = call(
        functools.partial(main, secs, tiles), "main",
        (shape(atmos.shape, f32), shape((4, 8, LANES), f32), shape((8, feat), f32)),
        [VMEM] * 11,
        (VMEM,) * 3,
        [pltpu.VMEM((rows * cols, feat), bf16), pltpu.VMEM((2, rows * cols, width), bf16)],
        flops=rows * cols * feat * width * 8,
        args=(atmos, flags, *weights, ocean, tile_a, tile_b, rows_b, rows_a),
    )
    field, pay = call(
        functools.partial(finish, secs), "finish",
        (shape(atmos.shape, f32), shape((count, 4, LANES), f32)),
        [VMEM] * 10,
        (VMEM,) * 2,
        [pltpu.VMEM((2, 16, width), bf16)],
        flops=16 * feat * width * 8,
        args=(field, flags, *weights, ends, corner_b, corner_a, sums),
        aliases={0: 0},
    )
    gathered = lax.all_to_all(pay, AXES, 0, 0)
    return call(
        functools.partial(final, secs, tiles), "final",
        (shape(atmos.shape, f32), shape(ocean.shape, f32), shape((rows, cols), f32)),
        [VMEM] * 14,
        (HBM,) * 3,
        [
            pltpu.VMEM(atmos.shape, f32),
            pltpu.VMEM(ocean.shape, f32),
            pltpu.VMEM(ocean.shape, f32),
            pltpu.VMEM((rows, cols), f32),
            pltpu.SemaphoreType.DMA((rows // 4 + 2,)),
        ],
        args=(gathered, *planned, field, ocean, tile_a, tile_b, rows_b, rows_a, corner_b, corner_a),
    )


def solution(mesh):
    placed = (
        P("sec", "tile", None),
        P("sec", "tile"),
        P(),
        P(),
        P(),
        P(),
        P("sec", "tile", None),
        P(),
    )
    return jax.shard_map(
        local,
        mesh=mesh,
        in_specs=placed,
        out_specs=(P("sec", "tile", None), P("sec", "tile", None), P("sec", "tile")),
        check_vma=False,
    )
```
